512 devices in a mesh: dp: 32 (over y, z_hi), spatial: 16 (over z_lo, x, core).
Axes of the slice: x: 4, y: 8, z: 8 (z_hi: 4, z_lo: 2; z = z_hi * 2 + z_lo), core: 2. Of those that a mesh axis runs over, the one named last changes fastest.
Arguments:
- features: bfloat16 [32, 128, 128, 256], P('dp', 'spatial')
- coarse: bfloat16 [32, 32, 32, 512], P('dp', 'spatial'), may hold values from -6 to 6
- timestep: int32 [32], P('dp'), may hold values from 0 to 999
- text_ids: int32 [32, 128], replicated, may hold values from 0 to 32255
- text_table: bfloat16 [32256, 1024], P(('dp', 'spatial')), may hold values from -6 to 6
- w_mod: bfloat16 [1024, 512], replicated, may hold values from -0.1875 to 0.1875
- w_skip: bfloat16 [512, 256], replicated, may hold values from -0.25 to 0.25
- w_conv: bfloat16 [256, 2304], replicated, may hold values from -0.125 to 0.125
- cotangent: bfloat16 [32, 128, 128, 256], P('dp', 'spatial')
Outputs:
- output: bfloat16 [32, 128, 128, 256], P('dp', 'spatial')
- grad_features: bfloat16 [32, 128, 128, 256], P('dp', 'spatial')
- grad_conv: bfloat16 [256, 2304], P('dp')
- grad_mod: bfloat16 [1024, 512], P('dp')
The draws below stay inside these ranges and needn't reach their ends.
All inputs are finite; a program needn't handle non-finite values.
Results may differ from the reference program's by a relative error of at most 0.011.
Values may be sent and summed in bfloat16 or wider, within the bound.
A program may use at most 64 MiB of HBM per device.

```python
import math
import jax
import jax.numpy as jnp
import numpy as np
from jax import lax

C = 256
CC = 512
CE = 1024
GROUPS = 32
L = 128
W = 128
BATCH = 32
H = 128
HC = 32
WC = 32
V = 32256


def draw_features(key, part):
    key = jax.random.fold_in(key, 11)
    first_key, second_key = jax.random.split(key)
    position = jnp.arange(H, dtype=jnp.float32) / (H - 1)
    lifted = (0.6 + 1.2 * position)[None, :, None, None]
    base = jax.random.normal(first_key, (BATCH, H, W, C), jnp.float32)
    offset_term = 0.3 * jax.random.normal(second_key, (BATCH, 1, 1, C), jnp.float32)
    return ((base + offset_term) * lifted).astype(jnp.bfloat16)


def draw_cotangent(key, part):
    key = jax.random.fold_in(key, 23)
    first_key, second_key = jax.random.split(key, 2)
    base = jnp.clip(jax.random.normal(first_key, (BATCH, H, W, C), jnp.float32), -6.0, 6.0)
    offset_term = 0.6 * jax.random.normal(second_key, (BATCH, 1, 1, C), jnp.float32)
    return (base + offset_term).astype(jnp.bfloat16)


def with_ends(drawn, own_key, low, largest):
    extent = drawn.shape
    place = [jax.random.randint(jax.random.fold_in(own_key, axis), (), 0, extent[axis]) for axis in range(len(extent))]
    drawn = drawn.at[tuple(place)].set(low)
    longest = extent.index(max(extent))
    place[longest] = (place[longest] + 1) % extent[longest]
    return drawn.at[tuple(place)].set(largest)


def level_of(own_key, shape, cuts, smallest, largest):
    def one(dim, blocks):
        draws = jax.random.uniform(jax.random.fold_in(jax.random.fold_in(own_key, 6), dim), (blocks,), jnp.float32, smallest / len(cuts), largest / len(cuts))
        return jnp.repeat(jnp.exp(draws), shape[dim] // blocks).reshape((-1,) + (1,) * (len(shape) - dim - 1))

    loudness = one(*cuts[0])
    for cut in cuts[1:]:
        loudness = loudness * one(*cut)
    return loudness


def rank_bounds(number_of, skew):
    loads = [(1 << 20) // math.isqrt(rank ** skew) + 1 for rank in range(1, number_of + 1)]
    deviation = 1 + sum(loads) // (1 << 30)
    return np.cumsum(np.array([max(1, weight // deviation) for weight in loads]))


def ranked_ids(key, dims, amount, slope):
    grid = rank_bounds(amount, slope)
    pick = jax.random.randint(jax.random.fold_in(key, 1), dims, 0, int(grid[amount - 1]))
    grade = jnp.searchsorted(jnp.asarray(grid, jnp.int32), pick, side="right")
    return jax.random.permutation(jax.random.fold_in(key, 2), amount)[grade].astype(jnp.int32)


def centred(stream_key, extent, scale, reach, pieces=(), kind=jnp.bfloat16):
    array = jax.random.normal(stream_key, extent, jnp.float32) * scale
    if len(pieces) > 0:
        array = level_of(stream_key, extent, pieces, -0.22, 0.18) * array
    return jnp.clip(array, min=-reach, max=reach).astype(kind)


def setup_inputs(seed: int = 0) -> dict:
    key_of = jax.random.split(jax.random.key(seed), 10)
    features = draw_features(jax.random.fold_in(key_of[9], 71), 0)
    coarse = centred(key_of[1], (BATCH, HC, WC, CC), 1.0, 6.0, ((0, 32), (1, 16)))
    timestep = with_ends(jax.random.randint(key_of[2], (BATCH,), 0, 1000), jax.random.fold_in(key_of[2], 1), 0, 999).astype(jnp.int32)
    text_ids = with_ends(ranked_ids(key_of[3], (BATCH, L), V, 2), jax.random.fold_in(key_of[3], 3), 0, V - 1).astype(jnp.int32)
    text_table = centred(key_of[4], (V, CE), 1.0, 6.0, ((0, 512),))
    w_mod = centred(key_of[5], (CE, 2 * C), CE ** -0.5, 0.1875)
    w_skip = centred(key_of[6], (CC, C), CC ** -0.5, 0.25)
    w_conv = centred(key_of[7], (C, 9 * C), (9 * C) ** -0.5, 0.125)
    cotangent = draw_cotangent(jax.random.fold_in(key_of[9], 71), 0)
    return {"features": features, "coarse": coarse, "timestep": timestep, "text_ids": text_ids, "text_table": text_table, "w_mod": w_mod, "w_skip": w_skip, "w_conv": w_conv, "cotangent": cotangent}


EPS = 1e-05
OFFSETS = ((-1, -1), (-1, 0), (-1, 1), (0, -1), (0, 0), (0, 1), (1, -1), (1, 0), (1, 1))

def group_average(channel_sums, total_count, groups):
    group_width = channel_sums.shape[-1] // groups
    grouped = channel_sums.reshape(channel_sums.shape[:-1] + (groups, group_width)).sum(-1) / (total_count * group_width)
    return jnp.repeat(grouped, group_width, axis=-1)

def group_moments(first_sums, square_sums, total_count, groups):
    center = group_average(first_sums, total_count, groups)
    spread = group_average(square_sums, total_count, groups) - center * center
    return (center, lax.rsqrt(spread + EPS))

def time_embed(steps, embed_width):
    half_width = embed_width // 2
    freqs = jnp.exp(-math.log(10000.0) * jnp.arange(half_width, dtype=jnp.float32) / half_width)
    angles = steps.astype(jnp.float32)[:, None] * freqs[None, :]
    return jnp.concatenate([jnp.sin(angles), jnp.cos(angles)], axis=1)

def shifted(padded, row_step, col_step, tile_rows, tile_cols):
    return padded[:, 1 + row_step:1 + row_step + tile_rows, 1 + col_step:1 + col_step + tile_cols, :]

def sample_pass(feat, coar, modu, cotan, w_skip, w_conv):
    batch_one, tile_rows, tile_cols, channels = feat.shape
    coarse_width = coar.shape[-1]
    coarse_f = coar.astype(jnp.float32)
    c_center, c_scale = group_moments(lax.optimization_barrier(jnp.sum(coarse_f, axis=(1, 2))), lax.optimization_barrier(jnp.sum(coarse_f * coarse_f, axis=(1, 2))), coar.shape[1] * coar.shape[2], GROUPS)
    coarse_act = jax.nn.silu((coarse_f - c_center[:, None, None, :]) * c_scale[:, None, None, :]).astype(jnp.bfloat16)
    skip_flat = jnp.dot(coarse_act.reshape(-1, coarse_width), w_skip, preferred_element_type=jnp.float32).astype(jnp.bfloat16)
    skip_map = skip_flat.reshape(batch_one, coar.shape[1], coar.shape[2], channels)
    upsampled = jnp.repeat(jnp.repeat(skip_map, 4, axis=1), 4, axis=2)
    merged = (feat.astype(jnp.float32) + upsampled.astype(jnp.float32)).astype(jnp.bfloat16)
    merged_f = merged.astype(jnp.float32)
    fine_count = tile_rows * tile_cols
    f_center, f_scale = group_moments(lax.optimization_barrier(jnp.sum(merged_f, axis=(1, 2))), lax.optimization_barrier(jnp.sum(merged_f * merged_f, axis=(1, 2))), fine_count, GROUPS)
    normed = (merged_f - f_center[:, None, None, :]) * f_scale[:, None, None, :]
    gain = 1.0 + modu[:, :channels]
    offset_term = modu[:, channels:]
    pre_act = normed * gain[:, None, None, :] + offset_term[:, None, None, :]
    hidden = jax.nn.silu(pre_act).astype(jnp.bfloat16)
    padded = jnp.pad(hidden, ((0, 0), (1, 1), (1, 1), (0, 0)))
    hidden_taps = [shifted(padded, row_step, col_step, tile_rows, tile_cols).reshape(-1, channels) for row_step, col_step in OFFSETS]
    conv_out = jnp.zeros((batch_one * tile_rows * tile_cols, channels), jnp.float32)
    for tap_index in range(9):
        conv_out = conv_out + jnp.dot(hidden_taps[tap_index], w_conv[:, tap_index * channels:(tap_index + 1) * channels], preferred_element_type=jnp.float32)
    output = (merged_f + conv_out.reshape(feat.shape)).astype(jnp.bfloat16)
    cot_padded = jnp.pad(cotan, ((0, 0), (1, 1), (1, 1), (0, 0)))
    grad_hidden = jnp.zeros((batch_one * tile_rows * tile_cols, channels), jnp.float32)
    for tap_index in range(9):
        row_step, col_step = OFFSETS[tap_index]
        piece = shifted(cot_padded, -row_step, -col_step, tile_rows, tile_cols).reshape(-1, channels)
        kernel = w_conv[:, tap_index * channels:(tap_index + 1) * channels]
        grad_hidden = grad_hidden + lax.dot_general(piece, kernel, (((1,), (1,)), ((), ())), preferred_element_type=jnp.float32)
    sigma = jax.nn.sigmoid(pre_act)
    grad_pre = grad_hidden.reshape(feat.shape) * sigma * (1.0 + pre_act * (1.0 - sigma))
    grad_gain = lax.optimization_barrier(jnp.sum(grad_pre * normed, axis=(1, 2)))
    grad_offset = lax.optimization_barrier(jnp.sum(grad_pre, axis=(1, 2)))
    mean_one = group_average(gain * grad_offset, fine_count, GROUPS)
    mean_two = group_average(gain * grad_gain, fine_count, GROUPS)
    grad_normed = grad_pre * gain[:, None, None, :]
    grad_merged = f_scale[:, None, None, :] * (grad_normed - mean_one[:, None, None, :] - normed * mean_two[:, None, None, :])
    grad_feat = (cotan.astype(jnp.float32) + grad_merged).astype(jnp.bfloat16)
    cot_flat = cotan.reshape(-1, channels)
    weight_part = jnp.concatenate([lax.dot_general(tap, cot_flat, (((0,), (0,)), ((), ())), preferred_element_type=jnp.float32) for tap in hidden_taps], axis=1)
    mod_grad = jnp.concatenate([grad_gain, grad_offset], axis=1)
    return (output, grad_feat, weight_part, mod_grad)

def reference(features, coarse, timestep, text_ids, text_table, w_mod, w_skip, w_conv, cotangent):
    channels = features.shape[-1]
    pooled = jnp.take(text_table, text_ids, axis=0).astype(jnp.float32).sum(1) / text_ids.shape[1]
    embed = time_embed(timestep, CE) + pooled
    silu_embed = jax.nn.silu(embed).astype(jnp.bfloat16)
    modulation = jnp.dot(silu_embed, w_mod, preferred_element_type=jnp.float32)

    def advance(total, items):
        feat, coar, modu, cotan = items
        output, grad_feat, weight_part, mod_grad = sample_pass(feat[None], coar[None], modu[None], cotan[None], w_skip, w_conv)
        return (total + weight_part, (output[0], grad_feat[0], mod_grad[0]))
    initial = jnp.zeros((channels, 9 * channels), jnp.float32)
    total, (outputs, grad_feats, mod_grads) = lax.scan(advance, initial, (features, coarse, modulation, cotangent))
    grad_conv = total.astype(jnp.bfloat16)
    grad_mod = jnp.dot(silu_embed.astype(jnp.float32).T, mod_grads, precision=lax.Precision.HIGHEST).astype(jnp.bfloat16)
    return (outputs, grad_feats, grad_conv, grad_mod)
```

```python
import functools
import math

import jax
import jax.numpy as jnp
from jax import lax
from jax.experimental import pallas as pl
from jax.experimental.pallas import tpu as pltpu
from jax.sharding import PartitionSpec as P

GROUPS = 32
EPS = 1e-05
MESH = pl.DeviceIdType.MESH
F32 = jnp.float32
BF16 = jnp.bfloat16
LANES = 128
VMEM_LIMIT = 62 * 1024 * 1024


def dot(a, b, dims=((1,), (0,))):
    return lax.dot_general(a, b, (dims, ((), ())), preferred_element_type=F32)


def iota(shape, axis):
    return lax.broadcasted_iota(jnp.int32, shape, axis)


def sigmoid(x):
    return 0.5 * jnp.tanh(0.5 * x) + 0.5


def group_total(tile, width):
    lane = iota(tile.shape, 1)
    step = 1
    while step < width:
        partner = jnp.where(
            (lane & step) != 0, pltpu.roll(tile, step, 1), pltpu.roll(tile, LANES - step, 1)
        )
        tile = tile + partner
        step *= 2
    return tile


def as_row(tile, first, count):
    return jnp.concatenate([tile[first + i : first + i + 1, :] for i in range(count)], axis=1)


def as_rows(row):
    return [row[:, i * LANES : (i + 1) * LANES] for i in range(row.shape[1] // LANES)]


def column_shifts(rows, spread_ref, first_row, reverse):
    width, channels = rows.shape
    column = iota(rows.shape, 0)
    earlier = jnp.where(column == 0, 0.0, pltpu.roll(rows, 1, 0)).astype(BF16)
    later = jnp.where(column == width - 1, 0.0, pltpu.roll(rows, width - 1, 0)).astype(BF16)
    left, right = (later, earlier) if reverse else (earlier, later)
    spread_ref[pl.ds(first_row, width), 0:channels] = left
    spread_ref[pl.ds(first_row, width), channels : 2 * channels] = rows.astype(BF16)
    spread_ref[pl.ds(first_row, width), 2 * channels : 3 * channels] = right


def turned_shifts(rows, turned_ref, first_pixel):
    width, channels = rows.shape
    turned = rows.T
    column = iota(turned.shape, 1)
    later = jnp.where(column == width - 1, 0.0, pltpu.roll(turned, width - 1, 1))
    earlier = jnp.where(column == 0, 0.0, pltpu.roll(turned, 1, 1))
    for i, shifted in enumerate((later, turned, earlier)):
        turned_ref[i * channels : (i + 1) * channels, pl.ds(first_pixel, width)] = shifted.astype(BF16)


def kernel(n_dp, n_sp, tile_rows, width, *refs):
    (
        time_ref, ids_hbm, feat_hbm, coarse_hbm, table_hbm, w_mod_hbm, w_skip_hbm, w_conv_hbm, cot_hbm,
        out_hbm, grad_feat_hbm, grad_conv_hbm, grad_mod_hbm,
        out_ref, grad_feat_ref, grad_conv_ref, grad_mod_ref, ids_ref,
        feat, coarse, table, w_mod, w_skip, w_conv, w_stack, cot,
        cot_edge, far_edge, hid_edge, cot_chip, cot_spread, cot_turned, hid_spread, chosen, up, merged,
        hidden, hidden_pair, grad_hid,
        fine_box, back_box, text_out, text_box, text_sum, text_dp_box, pooled, mod_out, mod_box, mod_rows,
        weight_own, cube_out, cube_box, weight_sum, tail_sum,
        tile_box, tail_box, final_box, final_tail_box,
        load_sem, store_sem, edge_send, edge_recv, send_sem, recv_sem,
    ) = refs
    channels = feat.shape[1]
    pixels = tile_rows * width
    half = channels // 2
    part = channels // n_dp
    dp = lax.axis_index("dp")
    sp = lax.axis_index("spatial")
    chip, core = sp // 2, sp % 2
    other_sp = sp + 1 - 2 * core

    y, z_high = dp // 4, dp % 4
    z_low, x = sp // 8, chip % 4
    z = 2 * z_high + z_low
    odd_x, odd_y, odd_z = x % 2, y % 2, z_low
    high_x, high_y = x // 2, y // 2
    quarter = 2 * odd_z + odd_x
    rank = high_x * 16 + high_y * 4 + z_high

    def block_of(high):
        return 2 * (high % 2) + high // 2

    def neighbour(side, d):
        dx, dy, dz = d % 2, (d // 2) % 2, d // 4
        x_there = (x + dx * (1 - 2 * odd_x) * (1 - 2 * side) + 4) % 4
        y_there = (y + dy * (1 - 2 * odd_y) * (1 - 2 * side) + 8) % 8
        z_there = (z + dz * (1 - 2 * odd_z) * (1 - 2 * side) + 8) % 8
        return (y_there * 4 + z_there // 2, (z_there % 2) * 8 + x_there * 2 + core)

    def of_rank(number):
        x_there, y_there, z_there = number // 16, (number // 4) % 4, number % 4
        return ((2 * y_there + odd_y) * 4 + z_there, z_low * 8 + (2 * x_there + odd_x) * 2 + core)

    owns_tail = jnp.logical_and(high_y == quarter, high_x == 0)
    owner = dp // 2 == sp
    (
        FINE, BACK, TEXT, TEXT_DP, POOLED, MOD, GRAD_MOD, TILE, TAIL, FINAL, FINAL_TAIL,
        PAIR_COT, PAIR_HIDDEN, FAR, CUBE,
    ) = range(15)

    def load(source, target, index):
        return pltpu.make_async_copy(source, target, load_sem.at[index])

    own_lanes = pl.ds(pl.multiple_of(core * half, half), half)
    other_lanes = pl.ds(pl.multiple_of((1 - core) * half, half), half)
    own_pixels = pl.multiple_of(core * pixels, pixels)
    other_pixels = pl.multiple_of((1 - core) * pixels, pixels)
    own_rows = pl.ds(pl.multiple_of(width + core * pixels, width), pixels)
    loads = [
        load(ids_hbm, ids_ref, 1),
        load(table_hbm, table, 2),
        load(coarse_hbm, coarse, 0),
        load(cot_hbm, cot, 3),
        load(cot_hbm.at[:, own_lanes], cot_chip.at[own_rows], 4),
    ]
    later = [
        load(feat_hbm, feat, 5),
        load(w_skip_hbm, w_skip, 6),
        load(w_mod_hbm, w_mod, 7),
        load(w_conv_hbm, w_conv, 8),
    ]
    stacks = [
        load(
            w_conv_hbm.at[:, pl.ds(tap * channels, channels)],
            w_stack.at[pl.ds(tap * channels, channels), :],
            9 + tap,
        )
        for tap in range(9)
    ]
    for copy in loads:
        copy.start()

    barrier = pltpu.get_barrier_semaphore()

    def greet(place):
        pl.semaphore_signal(barrier, inc=1, device_id=place, device_id_type=MESH)

    @pl.loop(1, n_sp, unroll=True)
    def _(i):
        greet((dp, lax.rem(sp + i, n_sp)))

    @pl.when(owner)
    def _():
        @pl.loop(1, n_dp)
        def _(i):
            greet((lax.rem(dp + i, n_dp), sp))

    for copy in later:
        copy.start()

    def remote(source, target, send, recv, place):
        return pltpu.make_async_remote_copy(
            src_ref=source, dst_ref=target, send_sem=send, recv_sem=recv, device_id=place, device_id_type=MESH
        )

    def wait_bytes(sem, ref):
        pltpu.make_async_copy(ref, ref, sem).wait()

    def to_spatial(box, index):
        @pl.loop(1, n_sp, unroll=True)
        def _(i):
            there = lax.rem(sp + i, n_sp)
            remote(box.at[sp], box.at[sp], send_sem.at[index], recv_sem.at[index], (dp, there)).start()

    def to_owners(source_of, box, index):
        for j in range(2):
            there = 2 * sp + j

            @pl.when(there != dp)
            def _():
                remote(source_of(j), box.at[dp], send_sem.at[index], recv_sem.at[index], (there, sp)).start()

    def sent_to_owners(box, index):
        @pl.when(owner)
        def _():
            wait_bytes(send_sem.at[index], box.at[pl.ds(0, 1)])

        @pl.when(jnp.logical_not(owner))
        def _():
            wait_bytes(send_sem.at[index], box.at[pl.ds(0, 2)])

    def from_owner(ref, index):
        @pl.loop(1, n_sp, unroll=True)
        def _(i):
            there = lax.rem(sp + i, n_sp)
            remote(ref, ref, send_sem.at[index], recv_sem.at[index], (dp, there)).start()

    def others(box):
        return box.at[pl.ds(0, box.shape[0] - 1)]

    def receive(box, index):
        wait_bytes(recv_sem.at[index], others(box))

    def total(box):
        return jnp.sum(box[...], axis=0)

    vocab = table.shape[0]
    batch, tokens = ids_ref.shape
    loads[0].wait()
    local_ids = ids_ref[...] - (dp * n_sp + sp) * vocab
    rows_of_vocab = iota((vocab, tokens), 0)
    matches = jnp.concatenate(
        [(local_ids[b : b + 1, :] == rows_of_vocab).astype(F32).astype(BF16) for b in range(batch)], axis=1
    )
    every = (batch, batch * tokens)
    sample = 2 * (iota(every, 0) & (n_sp - 1)) + lax.shift_right_logical(iota(every, 0), n_sp.bit_length() - 1)
    member = (lax.shift_right_logical(iota(every, 1), tokens.bit_length() - 1) == sample).astype(F32).astype(BF16)
    counts = dot(member, matches, ((1,), (1,))).astype(BF16)
    loads[1].wait()
    partial = dot(counts, table[...])
    for i in range(8):
        for j in range(2):
            text_out[:, j, i, :] = partial[j * n_sp : (j + 1) * n_sp, i * LANES : (i + 1) * LANES]

    loads[2].wait()
    coarse_f = coarse[...].astype(F32)
    coarse_sums = jnp.concatenate(
        as_rows(jnp.sum(coarse_f, axis=0, keepdims=True))
        + as_rows(jnp.sum(coarse_f * coarse_f, axis=0, keepdims=True)),
        axis=0,
    )
    for i in range(n_sp):
        text_out[i, 2] = coarse_sums

    pl.semaphore_wait(barrier, jnp.where(owner, n_sp, n_sp + 1))

    @pl.loop(1, n_sp, unroll=True)
    def _(i):
        there = lax.rem(sp + i, n_sp)
        remote(text_out.at[there], text_box.at[sp], send_sem.at[TEXT], recv_sem.at[TEXT], (dp, there)).start()

    text_box[sp] = text_out[sp]

    last = pixels - width

    def edges(source, target, first):
        down = remote(
            source.at[pl.ds(last, width)], target.at[0], edge_send.at[first], edge_recv.at[first], (dp, sp + 1)
        )
        upward = remote(
            source.at[pl.ds(0, width)], target.at[1], edge_send.at[first + 1], edge_recv.at[first + 1], (dp, sp - 1)
        )
        return down, upward

    def start_edges(source, target, first):
        down, upward = edges(source, target, first)

        @pl.when(sp < n_sp - 1)
        def _():
            down.start()

        @pl.when(sp > 0)
        def _():
            upward.start()

    def receive_edges(source, target, first):
        down, upward = edges(source, target, first)

        @pl.when(sp > 0)
        def _():
            down.wait_recv()

        @pl.when(sp < n_sp - 1)
        def _():
            upward.wait_recv()

        @pl.when(sp == 0)
        def _():
            target[0] = jnp.zeros((width, channels), BF16)

        @pl.when(sp == n_sp - 1)
        def _():
            target[1] = jnp.zeros((width, channels), BF16)

    def finish_edges(source, target, first):
        down, upward = edges(source, target, first)

        @pl.when(sp < n_sp - 1)
        def _():
            down.wait_send()

        @pl.when(sp > 0)
        def _():
            upward.wait_send()

    loads[3].wait()
    start_edges(cot, cot_edge, 0)
    pair_cot = remote(
        cot.at[:, other_lanes], cot_chip.at[own_rows], send_sem.at[PAIR_COT], recv_sem.at[PAIR_COT], (dp, other_sp)
    )
    pair_cot.start()
    far = remote(
        cot.at[pl.ds(pl.multiple_of(core * last, width), width), own_lanes],
        far_edge,
        send_sem.at[FAR],
        recv_sem.at[FAR],
        (dp, sp - 2 + 4 * core),
    )
    chips = n_sp // 2
    sends_far = jnp.logical_or(jnp.logical_and(core == 0, chip > 0), jnp.logical_and(core == 1, chip < chips - 1))
    takes_far = jnp.logical_or(jnp.logical_and(core == 0, chip < chips - 1), jnp.logical_and(core == 1, chip > 0))

    @pl.when(sends_far)
    def _():
        far.start()

    for copy in stacks:
        copy.start()

    shape = chosen.shape
    coarse_cols = width // 4
    place = iota(shape, 0)
    wanted = lax.shift_right_logical(place, width.bit_length() - 1) * coarse_cols + (
        lax.shift_right_logical(place & (width - 1), 2)
    )
    chosen[...] = (wanted == iota(shape, 1)).astype(F32).astype(BF16)

    def turn_rows(first_row):
        @pl.loop(0, tile_rows, unroll=True)
        def _(r):
            start = pl.multiple_of(first_row + r * width, width)
            turned_shifts(cot_chip[pl.ds(start, width), :].astype(F32), cot_turned, start)

    loads[4].wait()
    turn_rows(width + own_pixels)

    receive(text_box, TEXT)
    first_sums = total(text_box)
    text_sum[...] = first_sums[0:2]
    to_owners(lambda j: text_sum.at[j], text_dp_box, TEXT_DP)

    later[1].wait()
    coarse_total = group_total(first_sums[2], coarse.shape[1] // GROUPS)
    coarse_count = coarse.shape[0] * n_sp * (coarse.shape[1] // GROUPS)
    tiles = coarse.shape[1] // LANES
    c_mean = coarse_total[0:tiles, :] / coarse_count
    c_scale = lax.rsqrt(coarse_total[tiles : 2 * tiles, :] / coarse_count - c_mean * c_mean + EPS)
    c_normed = (coarse[...].astype(F32) - as_row(c_mean, 0, tiles)) * as_row(c_scale, 0, tiles)
    coarse_act = (c_normed * sigmoid(c_normed)).astype(BF16)
    skip = dot(coarse_act, w_skip[...]).astype(BF16)
    up[...] = dot(chosen[...], skip)

    later[0].wait()

    def merge(r, sums):
        start = pl.multiple_of(r * width, width)
        up_start = pl.multiple_of((r // 4) * width, width)
        rows = (feat[pl.ds(start, width), :].astype(F32) + up[pl.ds(up_start, width), :]).astype(BF16)
        merged[pl.ds(start, width), :] = rows
        rows = rows.astype(F32)
        first, second = sums
        first = first + jnp.sum(rows.reshape(width // 8, 8, channels), axis=0)
        second = second + jnp.sum((rows * rows).reshape(width // 8, 8, channels), axis=0)
        return first, second

    zero = jnp.zeros((8, channels), F32)
    first, second = lax.fori_loop(0, tile_rows, merge, (zero, zero), unroll=True)

    def sums_tile(one, two):
        one = jnp.sum(one, axis=0, keepdims=True)
        two = jnp.sum(two, axis=0, keepdims=True)
        return jnp.concatenate(as_rows(one) + as_rows(two) + [jnp.zeros((4, LANES), F32)], axis=0)

    fine_box[sp] = sums_tile(first, second)
    to_spatial(fine_box, FINE)

    @pl.when(owner)
    def _():
        text_dp_box[dp] = text_sum[dp % 2]
        receive(text_dp_box, TEXT_DP)
        pooled[...] = total(text_dp_box)
        from_owner(pooled, POOLED)

    wait_bytes(recv_sem.at[PAIR_COT], cot_chip.at[own_rows])
    turn_rows(width + other_pixels)
    receive_edges(cot, cot_edge, 0)

    @pl.when(takes_far)
    def _():
        far.wait_recv()

    @pl.when(jnp.logical_not(takes_far))
    def _():
        far_edge[...] = jnp.zeros((width, half), BF16)

    near = cot_edge[core, :, own_lanes].astype(F32)
    farther = far_edge[...].astype(F32)
    turned_shifts(jnp.where(core == 0, near, farther), cot_turned, 0)
    turned_shifts(jnp.where(core == 0, farther, near), cot_turned, width + 2 * pixels)

    @pl.when(jnp.logical_not(owner))
    def _():
        wait_bytes(recv_sem.at[POOLED], pooled)

    row, lane = iota((8, LANES), 0), iota((8, LANES), 1)
    half_width = 4 * LANES
    index = ((row & 3) * LANES + lane).astype(F32)
    angle = time_ref[0].astype(F32) * jnp.exp(-math.log(10000.0) * index / half_width)
    embed = jnp.where(row < 4, jnp.sin(angle), jnp.cos(angle)) + pooled[...] / tokens
    embed = (embed * sigmoid(embed)).astype(BF16).astype(F32)
    mod_out[8:16, :] = embed
    later[2].wait()
    embed_row = jnp.broadcast_to(as_row(embed, 0, 8), (8, 8 * LANES)).astype(BF16)
    modulation = dot(embed_row, w_mod[...])[0:1, :]
    gain = 1.0 + modulation[:, :channels]
    shift = modulation[:, channels:]

    receive(fine_box, FINE)
    fine_total = group_total(total(fine_box), channels // GROUPS)
    fine_count = pixels * n_sp * (channels // GROUPS)
    f_mean = fine_total[0:2, :] / fine_count
    f_scale = lax.rsqrt(fine_total[2:4, :] / fine_count - f_mean * f_mean + EPS)
    center, scale = as_row(f_mean, 0, 2), as_row(f_scale, 0, 2)

    @pl.loop(0, tile_rows, unroll=True)
    def _(r):
        start = pl.multiple_of(r * width, width)
        pre = (merged[pl.ds(start, width), :].astype(F32) - center) * scale * gain + shift
        act = pre * sigmoid(pre)
        hidden[pl.ds(start, width), :] = act.astype(BF16)
        low, high = act[:, :half], act[:, half:]
        block = lax.shift_right_logical(iota(low.shape, 1), 5)
        even = jnp.where((block & 1) == 0, low, pltpu.roll(high, 32, 1))
        odd = jnp.where((block & 1) == 0, pltpu.roll(low, LANES - 32, 1), high)
        rows = pl.ds(pl.multiple_of(own_pixels + start, width), width)
        hidden_pair[rows, :] = jnp.concatenate([even, odd], axis=1).astype(BF16)

        @pl.when(r % 2 == 1)
        def _():
            two = pl.ds(pl.multiple_of(own_pixels + start - width, width), 2 * width)
            remote(
                hidden_pair.at[two], hidden_pair.at[two], send_sem.at[PAIR_HIDDEN], recv_sem.at[PAIR_HIDDEN], (dp, other_sp)
            ).start()

    def weight_term(dr, first_pixel):
        lanes = pl.ds(pl.multiple_of((2 - dr) * width + first_pixel, width), pixels)
        return dot(cot_turned[:, lanes], hidden_pair[pl.ds(first_pixel, pixels), :])

    for dr in range(3):
        weight_own[dr] = weight_term(dr, own_pixels)
    wait_bytes(recv_sem.at[PAIR_HIDDEN], hidden_pair.at[pl.ds(0, pixels)])
    for dr in range(3):
        grads = weight_own[dr] + weight_term(dr, other_pixels)
        for dc in range(3):
            tap = 3 * dr + dc
            grad = grads[dc * half : (dc + 1) * half, :]
            if tap < 8:
                cube_out[tap % 2, tap // 2, 0, 0:half] = grad[:, :half].astype(BF16)
                cube_out[tap % 2, tap // 2, 1, 0:half] = grad[:, half:].astype(BF16)
            else:
                turned = grad.T.astype(BF16)
                for side in range(2):
                    for number in range(8):
                        first = (number % 2) * half + block_of(number // 2) * 32 + side * 16
                        cube_out[side, number // 2, number % 2, half : half + 16] = turned[first : first + 16, :]

    for side in range(2):
        for d in range(1, 8):
            dx, dy, dz = d % 2, (d // 2) % 2, d // 4
            their_quarter = 2 * (odd_z + dz - 2 * odd_z * dz) + (odd_x + dx - 2 * odd_x * dx)
            their_y = odd_y + dy - 2 * odd_y * dy
            remote(
                cube_out.at[side, their_quarter, their_y],
                cube_box.at[side, d],
                send_sem.at[CUBE + side],
                recv_sem.at[CUBE + side],
                neighbour(side, d),
            ).start()
    for side in range(2):
        cube_box[side, 0] = cube_out[side, quarter, odd_y]

    start_edges(hidden, hid_edge, 2)

    @pl.loop(0, tile_rows, unroll=True)
    def _(r):
        start = pl.multiple_of(r * width, width)
        column_shifts(cot[pl.ds(start, width), :].astype(F32), cot_spread, pl.multiple_of(start + width, width), True)

    column_shifts(cot_edge[0].astype(F32), cot_spread, 0, True)
    column_shifts(cot_edge[1].astype(F32), cot_spread, pixels + width, True)
    later[3].wait()
    chunk = pixels // 2

    @pl.loop(0, 2)
    def _(c):
        start = pl.multiple_of(c * chunk, chunk)
        grad = None
        for dr in range(3):
            term = dot(
                cot_spread[pl.ds(pl.multiple_of(start + (2 - dr) * width, width), chunk), :],
                w_conv[:, 3 * dr * channels : 3 * (dr + 1) * channels],
                ((1,), (1,)),
            )
            grad = term if grad is None else grad + term
        grad_hid[pl.ds(start, chunk), :] = grad

    def backward(r, sums):
        start = pl.multiple_of(r * width, width)
        normed = (merged[pl.ds(start, width), :].astype(F32) - center) * scale
        pre = normed * gain + shift
        sigma = sigmoid(pre)
        grad = grad_hid[pl.ds(start, width), :] * sigma * (1.0 + pre * (1.0 - sigma))
        grad_hid[pl.ds(start, width), :] = grad
        first, second = sums
        first = first + jnp.sum((grad * normed).reshape(width // 8, 8, channels), axis=0)
        second = second + jnp.sum(grad.reshape(width // 8, 8, channels), axis=0)
        return first, second

    first, second = lax.fori_loop(0, tile_rows, backward, (zero, zero), unroll=True)
    back_box[sp] = sums_tile(first, second)
    to_spatial(back_box, BACK)

    for side in range(2):
        wait_bytes(recv_sem.at[CUBE + side], cube_box.at[side, pl.ds(1, 7)])
        summed = cube_box[side, 0].astype(F32)
        for d in range(1, 8):
            summed = summed + cube_box[side, d].astype(F32)
        weight_sum[side] = summed[0:half, :].T
        tail_sum[side * 16 : (side + 1) * 16, :] = summed[half : half + 16, :]

    def part_of(number):
        rows = block_of((number // 4) % 4) * 32 + (number % 4) * part
        return weight_sum.at[number // 16, pl.ds(pl.multiple_of(rows, part), part)]

    @pl.loop(1, n_dp, unroll=True)
    def _(i):
        number = lax.rem(rank + i, n_dp)
        remote(part_of(number), tile_box.at[rank], send_sem.at[TILE], recv_sem.at[TILE], of_rank(number)).start()

    for m in range(4):
        number = quarter * 4 + m

        @pl.when(number != rank)
        def _():
            remote(
                tail_sum.at[pl.ds(m * part, part)],
                tail_box.at[rank],
                send_sem.at[TAIL],
                recv_sem.at[TAIL],
                of_rank(number),
            ).start()

        @pl.when(number == rank)
        def _():
            tail_box[rank] = tail_sum[m * part : (m + 1) * part, :]

    tile_box[rank] = part_of(rank)[...]

    @pl.loop(0, tile_rows, unroll=True)
    def _(r):
        start = pl.multiple_of(r * width, width)
        column_shifts(hidden[pl.ds(start, width), :].astype(F32), hid_spread, pl.multiple_of(start + width, width), False)

    receive_edges(hidden, hid_edge, 2)
    column_shifts(hid_edge[0].astype(F32), hid_spread, 0, False)
    column_shifts(hid_edge[1].astype(F32), hid_spread, pixels + width, False)
    for copy in stacks:
        copy.wait()

    @pl.loop(0, 2)
    def _(c):
        start = pl.multiple_of(c * chunk, chunk)
        conv = merged[pl.ds(start, chunk), :].astype(F32)
        for dr in range(3):
            conv = conv + dot(
                hid_spread[pl.ds(pl.multiple_of(start + dr * width, width), chunk), :],
                w_stack[3 * dr * channels : 3 * (dr + 1) * channels, :],
            )
        out_ref[pl.ds(start, chunk), :] = conv.astype(BF16)

    stores = [
        pltpu.make_async_copy(source, target, store_sem.at[i])
        for i, (source, target) in enumerate(
            (
                (out_ref, out_hbm), (grad_feat_ref, grad_feat_hbm),
                (grad_mod_ref, grad_mod_hbm), (grad_conv_ref, grad_conv_hbm),
            )
        )
    ]
    stores[0].start()

    receive(back_box, BACK)
    back = total(back_box)
    mod_out[0:8, :] = back
    to_owners(lambda j: mod_out, mod_box, MOD)
    gain_tile = jnp.concatenate(as_rows(gain) + as_rows(gain), axis=0)
    means = group_total(back[0:4, :] * gain_tile, channels // GROUPS) / fine_count
    mean_two, mean_one = as_row(means, 0, 2), as_row(means, 2, 2)

    @pl.loop(0, tile_rows, unroll=True)
    def _(r):
        start = pl.multiple_of(r * width, width)
        normed = (merged[pl.ds(start, width), :].astype(F32) - center) * scale
        inner = grad_hid[pl.ds(start, width), :] * gain - mean_one - normed * mean_two
        grad_feat_ref[pl.ds(start, width), :] = (cot[pl.ds(start, width), :].astype(F32) + scale * inner).astype(BF16)

    stores[1].start()

    receive(tile_box, TILE)
    final_box[sp] = total(tile_box)
    to_spatial(final_box, FINAL)

    @pl.when(owns_tail)
    def _():
        receive(tail_box, TAIL)
        final_tail_box[core] = total(tail_box)

        @pl.loop(1, n_sp)
        def _(i):
            there = lax.rem(sp + i, n_sp)
            remote(
                final_tail_box.at[core], final_tail_box.at[core], send_sem.at[FINAL_TAIL], recv_sem.at[FINAL_TAIL], (dp, there)
            ).start()

    @pl.when(owner)
    def _():
        mod_box[dp] = mod_out[...]
        receive(mod_box, MOD)
        share = 8 * LANES // n_dp
        in_lanes = LANES // share
        row_of_share = dp // in_lanes
        embeds = jnp.sum(
            jnp.where(iota((n_dp, 8, LANES), 1) == row_of_share, mod_box[:, 8:16, :], 0.0), axis=1
        ).astype(BF16)
        rest = jnp.concatenate([mod_box[:, i, :] for i in range(4)], axis=1)
        grads = None
        for _ in range(3):
            piece = rest.astype(BF16)
            rest = rest - piece.astype(F32)
            term = dot(embeds, piece, ((0,), (0,)))
            grads = term if grads is None else grads + term
        mod_rows[...] = grads
        mod_start = pl.multiple_of((dp % in_lanes) * share, share)
        grad_mod_ref[...] = mod_rows[pl.ds(mod_start, share), :].astype(BF16)
        from_owner(grad_mod_ref, GRAD_MOD)

    @pl.when(jnp.logical_not(owner))
    def _():
        wait_bytes(recv_sem.at[GRAD_MOD], grad_mod_ref)

    stores[2].start()

    receive(final_box, FINAL)

    @pl.when(owns_tail)
    def _():
        wait_bytes(recv_sem.at[FINAL_TAIL], final_tail_box.at[0])

    @pl.when(jnp.logical_not(owns_tail))
    def _():
        wait_bytes(recv_sem.at[FINAL_TAIL], final_tail_box)

    holders = [
        8 * (tap // 4) + 2 * (2 * (tap % 2) + (tap // 2) % 2) + side for tap in range(8) for side in range(2)
    ]
    grad_conv_ref[...] = jnp.concatenate(
        [final_box[j] for j in holders] + [final_tail_box[0], final_tail_box[1]], axis=1
    ).astype(BF16)

    stores[3].start()

    for box, index in (
        (fine_box, FINE), (back_box, BACK), (text_box, TEXT), (tile_box, TILE),
        (final_box, FINAL),
    ):
        wait_bytes(send_sem.at[index], others(box))

    for side in range(2):
        wait_bytes(send_sem.at[CUBE + side], cube_box.at[side, pl.ds(1, 7)])
    sent_to_owners(text_dp_box, TEXT_DP)
    sent_to_owners(mod_box, MOD)

    @pl.when(owner)
    def _():
        wait_bytes(send_sem.at[POOLED], final_box.at[pl.ds(0, n_sp - 1)])
        rows = (n_sp - 1) * grad_mod_ref.shape[0] * 2
        wait_bytes(send_sem.at[GRAD_MOD], hidden.at[pl.ds(0, rows)])

    pair_cot.wait_send()
    wait_bytes(send_sem.at[PAIR_HIDDEN], hidden_pair.at[pl.ds(0, pixels)])

    @pl.when(sends_far)
    def _():
        far.wait_send()

    finish_edges(cot, cot_edge, 0)
    finish_edges(hidden, hid_edge, 2)

    @pl.when(owns_tail)
    def _():
        wait_bytes(send_sem.at[TAIL], tail_box.at[pl.ds(0, 3)])
        wait_bytes(send_sem.at[FINAL_TAIL], final_box.at[pl.ds(0, n_sp - 1)])

    @pl.when(jnp.logical_not(owns_tail))
    def _():
        wait_bytes(send_sem.at[TAIL], tail_box.at[pl.ds(0, 4)])

    for store in stores:
        store.wait()


def write(*refs):
    sources, targets, rooms, load_sem, store_sem = refs[:4], refs[4:8], refs[8:12], refs[12], refs[13]
    moves = []
    for source, room, target in zip(sources, rooms, targets):
        rows = source.shape[0]
        pieces = 4 if rows >= 1024 else 1
        for i in range(pieces):
            piece = pl.ds(i * rows // pieces, rows // pieces)
            number = len(moves)
            moves.append(
                (
                    pltpu.make_async_copy(source.at[piece], room.at[piece], load_sem.at[number]),
                    pltpu.make_async_copy(room.at[piece], target.at[piece], store_sem.at[number]),
                )
            )
    for fetch, _ in moves:
        fetch.start()
    for fetch, store in moves:
        fetch.wait()
        store.start()
    for _, store in moves:
        store.wait()


def body(n_dp, n_sp, features, coarse, timestep, text_ids, text_table, w_mod, w_skip, w_conv, cotangent):
    _, tile_rows, width, channels = features.shape
    pixels = tile_rows * width
    cells = coarse.shape[1] * coarse.shape[2]
    coarse_width = coarse.shape[3]
    part, half = channels // n_dp, channels // 2
    taps = w_conv.shape[1] // channels
    vm = pltpu.VMEM
    tile = (8, LANES)
    anywhere = pl.BlockSpec(memory_space=pl.ANY)
    mod_rows = w_mod.shape[0] // n_dp
    scratch = [
        vm((pixels, channels), BF16),
        vm((pixels, channels), BF16),
        vm((part, taps * channels), BF16),
        vm((mod_rows, 2 * channels), BF16),
        vm(text_ids.shape, jnp.int32),
        vm((pixels, channels), BF16),
        vm((cells, coarse_width), BF16),
        vm(text_table.shape, BF16),
        vm(w_mod.shape, BF16),
        vm(w_skip.shape, BF16),
        vm(w_conv.shape, BF16),
        vm((taps * channels, channels), BF16),
        vm((pixels, channels), BF16),
        vm((2, width, channels), BF16),
        vm((width, half), BF16),
        vm((2, width, channels), BF16),
        vm((2 * pixels + 2 * width, half), BF16),
        vm((pixels + 2 * width, 3 * channels), BF16),
        vm((3 * half, 2 * pixels + 2 * width), BF16),
        vm((pixels + 2 * width, 3 * channels), BF16),
        vm((4 * cells, cells), BF16),
        vm((4 * cells, channels), F32),
        vm((pixels, channels), BF16),
        vm((pixels, channels), BF16),
        vm((2 * pixels, channels), BF16),
        vm((pixels, channels), F32),
        vm((n_sp,) + tile, F32),
        vm((n_sp,) + tile, F32),
        vm((n_sp, 3) + tile, F32),
        vm((n_sp, 3) + tile, F32),
        vm((2,) + tile, F32),
        vm((n_dp,) + tile, F32),
        vm(tile, F32),
        vm((16, LANES), F32),
        vm((n_dp, 16, LANES), F32),
        vm((LANES, 2 * channels), F32),
        vm((3, 3 * half, channels), F32),
        vm((2, 4, 2, half + 16, half), BF16),
        vm((2, 8, half + 16, half), BF16),
        vm((2, half, half), F32),
        vm((32, half), F32),
        vm((n_dp, part, half), F32),
        vm((n_dp, part, half), F32),
        vm((n_sp, part, half), F32),
        vm((2, part, half), F32),
        pltpu.SemaphoreType.DMA((9 + taps,)),
        pltpu.SemaphoreType.DMA((4,)),
        pltpu.SemaphoreType.DMA((4,)),
        pltpu.SemaphoreType.DMA((4,)),
        pltpu.SemaphoreType.DMA((16,)),
        pltpu.SemaphoreType.DMA((16,)),
    ]
    shapes = (
        jax.ShapeDtypeStruct((pixels, channels), BF16),
        jax.ShapeDtypeStruct((pixels, channels), BF16),
        jax.ShapeDtypeStruct((part, taps * channels), BF16),
        jax.ShapeDtypeStruct((mod_rows, 2 * channels), BF16),
    )
    results = pl.pallas_call(
        functools.partial(kernel, n_dp, n_sp, tile_rows, width),
        out_shape=shapes,
        in_specs=[pl.BlockSpec(memory_space=pltpu.SMEM)] + [anywhere] * 8,
        out_specs=(anywhere,) * 4,
        scratch_shapes=scratch,
        compiler_params=pltpu.CompilerParams(
            collective_id=0, has_side_effects=True, vmem_limit_bytes=VMEM_LIMIT
        ),
    )(
        timestep,
        text_ids,
        features.reshape(pixels, channels),
        coarse.reshape(cells, coarse_width),
        text_table,
        w_mod,
        w_skip,
        w_conv,
        cotangent.reshape(pixels, channels),
    )
    output, grad_features, grad_conv, grad_mod = pl.pallas_call(
        write,
        out_shape=shapes,
        in_specs=[anywhere] * 4,
        out_specs=(anywhere,) * 4,
        scratch_shapes=[vm(shape.shape, shape.dtype) for shape in shapes]
        + [pltpu.SemaphoreType.DMA((10,)), pltpu.SemaphoreType.DMA((10,))],
        compiler_params=pltpu.CompilerParams(vmem_limit_bytes=VMEM_LIMIT),
    )(*results)
    return output.reshape(features.shape), grad_features.reshape(features.shape), grad_conv, grad_mod


def solution(mesh):
    in_specs = (
        P("dp", "spatial", None, None),
        P("dp", "spatial", None, None),
        P("dp"),
        P(),
        P(("dp", "spatial"), None),
        P(),
        P(),
        P(),
        P("dp", "spatial", None, None),
    )
    out_specs = (
        P("dp", "spatial", None, None),
        P("dp", "spatial", None, None),
        P("dp", None),
        P("dp", None),
    )
    step = functools.partial(body, mesh.shape["dp"], mesh.shape["spatial"])
    return jax.shard_map(step, mesh=mesh, in_specs=in_specs, out_specs=out_specs, check_vma=False)
```

```python
import functools
import math

import jax
import jax.numpy as jnp
from jax import lax
from jax.experimental import pallas as pl
from jax.experimental.pallas import tpu as pltpu
from jax.sharding import PartitionSpec as P

GROUPS = 32
EPS = 1e-05
MESH = pl.DeviceIdType.MESH
F32 = jnp.float32
BF16 = jnp.bfloat16
LANES = 128
VMEM_LIMIT = 62 * 1024 * 1024


def dot(a, b, dims=((1,), (0,))):
    return lax.dot_general(a, b, (dims, ((), ())), preferred_element_type=F32)


def iota(shape, axis):
    return lax.broadcasted_iota(jnp.int32, shape, axis)


def sigmoid(x):
    return 0.5 * jnp.tanh(0.5 * x) + 0.5


def group_total(tile, width):
    lane = iota(tile.shape, 1)
    step = 1
    while step < width:
        partner = jnp.where(
            (lane & step) != 0, pltpu.roll(tile, step, 1), pltpu.roll(tile, LANES - step, 1)
        )
        tile = tile + partner
        step *= 2
    return tile


def as_row(tile, first, count):
    return jnp.concatenate([tile[first + i : first + i + 1, :] for i in range(count)], axis=1)


def as_rows(row):
    return [row[:, i * LANES : (i + 1) * LANES] for i in range(row.shape[1] // LANES)]


def column_shifts(rows, spread_ref, first_row, reverse):
    width, channels = rows.shape
    column = iota(rows.shape, 0)
    earlier = jnp.where(column == 0, 0.0, pltpu.roll(rows, 1, 0)).astype(BF16)
    later = jnp.where(column == width - 1, 0.0, pltpu.roll(rows, width - 1, 0)).astype(BF16)
    left, right = (later, earlier) if reverse else (earlier, later)
    spread_ref[pl.ds(first_row, width), 0:channels] = left
    spread_ref[pl.ds(first_row, width), channels : 2 * channels] = rows.astype(BF16)
    spread_ref[pl.ds(first_row, width), 2 * channels : 3 * channels] = right


def turned_shifts(rows, turned_ref, first_pixel):
    width, channels = rows.shape
    turned = rows.T
    column = iota(turned.shape, 1)
    later = jnp.where(column == width - 1, 0.0, pltpu.roll(turned, width - 1, 1))
    earlier = jnp.where(column == 0, 0.0, pltpu.roll(turned, 1, 1))
    for i, shifted in enumerate((later, turned, earlier)):
        turned_ref[i * channels : (i + 1) * channels, pl.ds(first_pixel, width)] = shifted.astype(BF16)


def kernel(n_dp, n_sp, tile_rows, width, *refs):
    (
        time_ref, ids_hbm, feat_hbm, coarse_hbm, table_hbm, w_mod_hbm, w_skip_hbm, w_conv_hbm, cot_hbm,
        out_hbm, grad_feat_hbm, grad_conv_hbm, grad_mod_hbm,
        out_ref, grad_feat_ref, grad_conv_ref, grad_mod_ref, ids_ref,
        feat, coarse, table, w_mod, w_skip, w_conv, w_stack, cot,
        cot_edge, far_edge, hid_edge, cot_half, cot_chip, cot_spread, cot_turned, hid_spread, chosen, up, merged,
        hidden, hidden_pair, grad_hid,
        fine_box, back_box, text_out, text_box, text_sum, text_dp_box, pooled, mod_out, mod_box, mod_rows, grad_mod_parts,
        weight_own, cube_out, cube_box, weight_sum, tail_sum,
        tile_box, tail_box, final_box,
        load_sem, store_sem, edge_send, edge_recv, send_sem, recv_sem,
    ) = refs
    channels = feat.shape[1]
    pixels = tile_rows * width
    half = channels // 2
    part = channels // n_dp
    dp = lax.axis_index("dp")
    sp = lax.axis_index("spatial")
    chip, core = sp // 2, sp % 2
    other_sp = sp + 1 - 2 * core

    y, z_high = dp // 4, dp % 4
    z_low, x = sp // 8, chip % 4
    z = 2 * z_high + z_low
    odd_x, odd_y, odd_z = x % 2, y % 2, z_low
    high_x, high_y = x // 2, y // 2
    quarter = 2 * odd_z + odd_x
    rank = high_x * 16 + high_y * 4 + z_high

    def block_of(high):
        return 2 * (high % 2) + high // 2

    def neighbour(side, d):
        dx, dy, dz = d % 2, (d // 2) % 2, d // 4
        x_there = (x + dx * (1 - 2 * odd_x) * (1 - 2 * side) + 4) % 4
        y_there = (y + dy * (1 - 2 * odd_y) * (1 - 2 * side) + 8) % 8
        z_there = (z + dz * (1 - 2 * odd_z) * (1 - 2 * side) + 8) % 8
        return (y_there * 4 + z_there // 2, (z_there % 2) * 8 + x_there * 2 + core)

    def of_rank(number):
        x_there, y_there, z_there = number // 16, (number // 4) % 4, number % 4
        return ((2 * y_there + odd_y) * 4 + z_there, z_low * 8 + (2 * x_there + odd_x) * 2 + core)

    owns_tail = jnp.logical_and(high_y == quarter, high_x == 0)
    owner = dp // 2 == sp
    from_first = lax.rem(sp - dp // 2 + n_sp, n_sp)
    quarter_owner = from_first % 4 == 0
    (
        FINE, BACK, TEXT, TEXT_DP, POOLED, MOD, GRAD_MOD, TILE, TAIL, FINAL,
        PAIR_COT, PAIR_HIDDEN, FAR, CUBE,
    ) = range(14)

    def load(source, target, index):
        return pltpu.make_async_copy(source, target, load_sem.at[index])

    own_lanes = pl.ds(pl.multiple_of(core * half, half), half)
    other_lanes = pl.ds(pl.multiple_of((1 - core) * half, half), half)
    own_pixels = pl.multiple_of(core * pixels, pixels)
    other_pixels = pl.multiple_of((1 - core) * pixels, pixels)
    own_rows = pl.ds(pl.multiple_of(width + core * pixels, width), pixels)
    loads = [
        load(ids_hbm, ids_ref, 1),
        load(table_hbm, table, 2),
        load(coarse_hbm, coarse, 0),
        load(cot_hbm, cot, 3),
    ]
    later = [
        load(feat_hbm, feat, 4),
        load(w_skip_hbm, w_skip, 5),
        load(w_mod_hbm, w_mod, 6),
        load(w_conv_hbm, w_conv, 7),
    ]
    for copy in loads:
        copy.start()

    barrier = pltpu.get_barrier_semaphore()

    def greet(place):
        pl.semaphore_signal(barrier, inc=1, device_id=place, device_id_type=MESH)

    @pl.loop(1, n_sp, unroll=True)
    def _(i):
        greet((dp, lax.rem(sp + i, n_sp)))

    @pl.when(owner)
    def _():
        @pl.loop(1, n_dp)
        def _(i):
            greet((lax.rem(dp + i, n_dp), sp))

    for copy in later:
        copy.start()

    def remote(source, target, send, recv, place):
        return pltpu.make_async_remote_copy(
            src_ref=source, dst_ref=target, send_sem=send, recv_sem=recv, device_id=place, device_id_type=MESH
        )

    def wait_bytes(sem, ref):
        pltpu.make_async_copy(ref, ref, sem).wait()

    def to_spatial(box, index):
        @pl.loop(1, n_sp, unroll=True)
        def _(i):
            there = lax.rem(sp + i, n_sp)
            remote(box.at[sp], box.at[sp], send_sem.at[index], recv_sem.at[index], (dp, there)).start()

    def to_owners(source_of, box, index):
        for j in range(2):
            there = 2 * sp + j

            @pl.when(there != dp)
            def _():
                remote(source_of(j), box.at[dp], send_sem.at[index], recv_sem.at[index], (there, sp)).start()

    def sent_to_owners(box, index):
        @pl.when(owner)
        def _():
            wait_bytes(send_sem.at[index], box.at[pl.ds(0, 1)])

        @pl.when(jnp.logical_not(owner))
        def _():
            wait_bytes(send_sem.at[index], box.at[pl.ds(0, 2)])

    def from_owner(ref, index):
        @pl.loop(1, n_sp, unroll=True)
        def _(i):
            there = lax.rem(sp + i, n_sp)
            remote(ref, ref, send_sem.at[index], recv_sem.at[index], (dp, there)).start()

    def others(box):
        return box.at[pl.ds(0, box.shape[0] - 1)]

    def receive(box, index):
        wait_bytes(recv_sem.at[index], others(box))

    def total(box):
        return jnp.sum(box[...], axis=0)

    vocab = table.shape[0]
    batch, tokens = ids_ref.shape
    loads[0].wait()
    local_ids = ids_ref[...] - (dp * n_sp + sp) * vocab
    rows_of_vocab = iota((vocab, tokens), 0)
    matches = jnp.concatenate(
        [(local_ids[b : b + 1, :] == rows_of_vocab).astype(F32).astype(BF16) for b in range(batch)], axis=1
    )
    every = (batch, batch * tokens)
    sample = 2 * (iota(every, 0) & (n_sp - 1)) + lax.shift_right_logical(iota(every, 0), n_sp.bit_length() - 1)
    member = (lax.shift_right_logical(iota(every, 1), tokens.bit_length() - 1) == sample).astype(F32).astype(BF16)
    counts = dot(member, matches, ((1,), (1,))).astype(BF16)
    loads[1].wait()
    partial = dot(counts, table[...])
    for i in range(8):
        for j in range(2):
            text_out[:, j, i, :] = partial[j * n_sp : (j + 1) * n_sp, i * LANES : (i + 1) * LANES]

    loads[2].wait()
    coarse_f = coarse[...].astype(F32)
    coarse_sums = jnp.concatenate(
        as_rows(jnp.sum(coarse_f, axis=0, keepdims=True))
        + as_rows(jnp.sum(coarse_f * coarse_f, axis=0, keepdims=True)),
        axis=0,
    )
    for i in range(n_sp):
        text_out[i, 2] = coarse_sums

    pl.semaphore_wait(barrier, jnp.where(owner, n_sp, n_sp + 1))

    @pl.loop(1, n_sp, unroll=True)
    def _(i):
        there = lax.rem(sp + i, n_sp)
        remote(text_out.at[there], text_box.at[sp], send_sem.at[TEXT], recv_sem.at[TEXT], (dp, there)).start()

    text_box[sp] = text_out[sp]

    last = pixels - width

    def edges(source, target, first):
        down = remote(
            source.at[pl.ds(last, width)], target.at[0], edge_send.at[first], edge_recv.at[first], (dp, sp + 1)
        )
        upward = remote(
            source.at[pl.ds(0, width)], target.at[1], edge_send.at[first + 1], edge_recv.at[first + 1], (dp, sp - 1)
        )
        return down, upward

    def start_edges(source, target, first):
        down, upward = edges(source, target, first)

        @pl.when(sp < n_sp - 1)
        def _():
            down.start()

        @pl.when(sp > 0)
        def _():
            upward.start()

    def receive_edges(source, target, first):
        down, upward = edges(source, target, first)

        @pl.when(sp > 0)
        def _():
            down.wait_recv()

        @pl.when(sp < n_sp - 1)
        def _():
            upward.wait_recv()

        @pl.when(sp == 0)
        def _():
            target[0] = jnp.zeros((width, channels), BF16)

        @pl.when(sp == n_sp - 1)
        def _():
            target[1] = jnp.zeros((width, channels), BF16)

    def finish_edges(source, target, first):
        down, upward = edges(source, target, first)

        @pl.when(sp < n_sp - 1)
        def _():
            down.wait_send()

        @pl.when(sp > 0)
        def _():
            upward.wait_send()

    loads[3].wait()
    start_edges(cot, cot_edge, 0)
    cot_half[...] = cot[:, other_lanes]
    cot_chip[own_rows, :] = cot[:, own_lanes]
    pair_cot = remote(
        cot_half, cot_chip.at[own_rows], send_sem.at[PAIR_COT], recv_sem.at[PAIR_COT], (dp, other_sp)
    )
    pair_cot.start()
    far = remote(
        cot_chip.at[pl.ds(pl.multiple_of(width + core * (pixels + last), width), width)],
        far_edge,
        send_sem.at[FAR],
        recv_sem.at[FAR],
        (dp, sp - 2 + 4 * core),
    )
    chips = n_sp // 2
    sends_far = jnp.logical_or(jnp.logical_and(core == 0, chip > 0), jnp.logical_and(core == 1, chip < chips - 1))
    takes_far = jnp.logical_or(jnp.logical_and(core == 0, chip < chips - 1), jnp.logical_and(core == 1, chip > 0))

    @pl.when(sends_far)
    def _():
        far.start()

    shape = chosen.shape
    coarse_cols = width // 4
    place = iota(shape, 0)
    wanted = lax.shift_right_logical(place, width.bit_length() - 1) * coarse_cols + (
        lax.shift_right_logical(place & (width - 1), 2)
    )
    chosen[...] = (wanted == iota(shape, 1)).astype(F32).astype(BF16)

    def turn_rows(first_row):
        @pl.loop(0, tile_rows, unroll=True)
        def _(r):
            start = pl.multiple_of(first_row + r * width, width)
            turned_shifts(cot_chip[pl.ds(start, width), :].astype(F32), cot_turned, start)

    turn_rows(width + own_pixels)

    receive(text_box, TEXT)
    first_sums = total(text_box)
    text_sum[...] = first_sums[0:2]
    to_owners(lambda j: text_sum.at[j], text_dp_box, TEXT_DP)

    later[1].wait()
    coarse_total = group_total(first_sums[2], coarse.shape[1] // GROUPS)
    coarse_count = coarse.shape[0] * n_sp * (coarse.shape[1] // GROUPS)
    tiles = coarse.shape[1] // LANES
    c_mean = coarse_total[0:tiles, :] / coarse_count
    c_scale = lax.rsqrt(coarse_total[tiles : 2 * tiles, :] / coarse_count - c_mean * c_mean + EPS)
    c_normed = (coarse[...].astype(F32) - as_row(c_mean, 0, tiles)) * as_row(c_scale, 0, tiles)
    coarse_act = (c_normed * sigmoid(c_normed)).astype(BF16)
    skip = dot(coarse_act, w_skip[...]).astype(BF16)
    up[...] = dot(chosen[...], skip)

    later[0].wait()

    def merge(r, sums):
        start = pl.multiple_of(r * width, width)
        up_start = pl.multiple_of((r // 4) * width, width)
        rows = (feat[pl.ds(start, width), :].astype(F32) + up[pl.ds(up_start, width), :]).astype(BF16)
        merged[pl.ds(start, width), :] = rows
        rows = rows.astype(F32)
        first, second = sums
        first = first + jnp.sum(rows.reshape(width // 8, 8, channels), axis=0)
        second = second + jnp.sum((rows * rows).reshape(width // 8, 8, channels), axis=0)
        return first, second

    zero = jnp.zeros((8, channels), F32)
    first, second = lax.fori_loop(0, tile_rows, merge, (zero, zero), unroll=True)

    def sums_tile(one, two):
        one = jnp.sum(one, axis=0, keepdims=True)
        two = jnp.sum(two, axis=0, keepdims=True)
        return jnp.concatenate(as_rows(one) + as_rows(two) + [jnp.zeros((4, LANES), F32)], axis=0)

    fine_box[sp] = sums_tile(first, second)
    to_spatial(fine_box, FINE)

    @pl.when(owner)
    def _():
        text_dp_box[dp] = text_sum[dp % 2]
        receive(text_dp_box, TEXT_DP)
        pooled[...] = total(text_dp_box)
        from_owner(pooled, POOLED)

    wait_bytes(recv_sem.at[PAIR_COT], cot_chip.at[own_rows])
    turn_rows(width + other_pixels)
    receive_edges(cot, cot_edge, 0)

    @pl.when(takes_far)
    def _():
        far.wait_recv()

    @pl.when(jnp.logical_not(takes_far))
    def _():
        far_edge[...] = jnp.zeros((width, half), BF16)

    near = cot_edge[core, :, own_lanes].astype(F32)
    farther = far_edge[...].astype(F32)
    turned_shifts(jnp.where(core == 0, near, farther), cot_turned, 0)
    turned_shifts(jnp.where(core == 0, farther, near), cot_turned, width + 2 * pixels)

    @pl.when(jnp.logical_not(owner))
    def _():
        wait_bytes(recv_sem.at[POOLED], pooled)

    row, lane = iota((8, LANES), 0), iota((8, LANES), 1)
    half_width = 4 * LANES
    index = ((row & 3) * LANES + lane).astype(F32)
    angle = time_ref[0].astype(F32) * jnp.exp(-math.log(10000.0) * index / half_width)
    embed = jnp.where(row < 4, jnp.sin(angle), jnp.cos(angle)) + pooled[...] / tokens
    embed = (embed * sigmoid(embed)).astype(BF16).astype(F32)
    later[2].wait()
    embed_row = jnp.broadcast_to(as_row(embed, 0, 8), (8, 8 * LANES)).astype(BF16)
    modulation = dot(embed_row, w_mod[...])[0:1, :]
    gain = 1.0 + modulation[:, :channels]
    shift = modulation[:, channels:]

    receive(fine_box, FINE)
    fine_total = group_total(total(fine_box), channels // GROUPS)
    fine_count = pixels * n_sp * (channels // GROUPS)
    f_mean = fine_total[0:2, :] / fine_count
    f_scale = lax.rsqrt(fine_total[2:4, :] / fine_count - f_mean * f_mean + EPS)
    center, scale = as_row(f_mean, 0, 2), as_row(f_scale, 0, 2)

    @pl.loop(0, tile_rows, unroll=True)
    def _(r):
        start = pl.multiple_of(r * width, width)
        pre = (merged[pl.ds(start, width), :].astype(F32) - center) * scale * gain + shift
        act = pre * sigmoid(pre)
        hidden[pl.ds(start, width), :] = act.astype(BF16)
        low, high = act[:, :half], act[:, half:]
        block = lax.shift_right_logical(iota(low.shape, 1), 5)
        even = jnp.where((block & 1) == 0, low, pltpu.roll(high, 32, 1))
        odd = jnp.where((block & 1) == 0, pltpu.roll(low, LANES - 32, 1), high)
        rows = pl.ds(pl.multiple_of(own_pixels + start, width), width)
        hidden_pair[rows, :] = jnp.concatenate([even, odd], axis=1).astype(BF16)

        @pl.when(r % 2 == 1)
        def _():
            two = pl.ds(pl.multiple_of(own_pixels + start - width, width), 2 * width)
            remote(
                hidden_pair.at[two], hidden_pair.at[two], send_sem.at[PAIR_HIDDEN], recv_sem.at[PAIR_HIDDEN], (dp, other_sp)
            ).start()

    def weight_term(dr, first_pixel):
        lanes = pl.ds(pl.multiple_of((2 - dr) * width + first_pixel, width), pixels)
        return dot(cot_turned[:, lanes], hidden_pair[pl.ds(first_pixel, pixels), :])

    for dr in range(3):
        weight_own[dr] = weight_term(dr, own_pixels)
    wait_bytes(recv_sem.at[PAIR_HIDDEN], hidden_pair.at[pl.ds(0, pixels)])
    for dr in range(3):
        grads = weight_own[dr] + weight_term(dr, other_pixels)
        for dc in range(3):
            tap = 3 * dr + dc
            grad = grads[dc * half : (dc + 1) * half, :]
            if tap < 8:
                cube_out[tap % 2, tap // 2, 0, 0:half] = grad[:, :half].astype(BF16)
                cube_out[tap % 2, tap // 2, 1, 0:half] = grad[:, half:].astype(BF16)
            else:
                turned = grad.T.astype(BF16)
                for side in range(2):
                    for number in range(8):
                        first = (number % 2) * half + block_of(number // 2) * 32 + side * 16
                        cube_out[side, number // 2, number % 2, half : half + 16] = turned[first : first + 16, :]

    for side in range(2):
        for d in range(1, 8):
            dx, dy, dz = d % 2, (d // 2) % 2, d // 4
            their_quarter = 2 * (odd_z + dz - 2 * odd_z * dz) + (odd_x + dx - 2 * odd_x * dx)
            their_y = odd_y + dy - 2 * odd_y * dy
            remote(
                cube_out.at[side, their_quarter, their_y],
                cube_box.at[side, d],
                send_sem.at[CUBE + side],
                recv_sem.at[CUBE + side],
                neighbour(side, d),
            ).start()
    for side in range(2):
        cube_box[side, 0] = cube_out[side, quarter, odd_y]

    start_edges(hidden, hid_edge, 2)

    @pl.loop(0, tile_rows, unroll=True)
    def _(r):
        start = pl.multiple_of(r * width, width)
        column_shifts(cot[pl.ds(start, width), :].astype(F32), cot_spread, pl.multiple_of(start + width, width), True)

    column_shifts(cot_edge[0].astype(F32), cot_spread, 0, True)
    column_shifts(cot_edge[1].astype(F32), cot_spread, pixels + width, True)
    later[3].wait()
    chunk = pixels // 2

    @pl.loop(0, 2)
    def _(c):
        start = pl.multiple_of(c * chunk, chunk)
        grad = None
        for dr in range(3):
            term = dot(
                cot_spread[pl.ds(pl.multiple_of(start + (2 - dr) * width, width), chunk), :],
                w_conv[:, 3 * dr * channels : 3 * (dr + 1) * channels],
                ((1,), (1,)),
            )
            grad = term if grad is None else grad + term
        grad_hid[pl.ds(start, chunk), :] = grad

    def backward(r, sums):
        start = pl.multiple_of(r * width, width)
        normed = (merged[pl.ds(start, width), :].astype(F32) - center) * scale
        pre = normed * gain + shift
        sigma = sigmoid(pre)
        grad = grad_hid[pl.ds(start, width), :] * sigma * (1.0 + pre * (1.0 - sigma))
        grad_hid[pl.ds(start, width), :] = grad
        first, second = sums
        first = first + jnp.sum((grad * normed).reshape(width // 8, 8, channels), axis=0)
        second = second + jnp.sum(grad.reshape(width // 8, 8, channels), axis=0)
        return first, second

    first, second = lax.fori_loop(0, tile_rows, backward, (zero, zero), unroll=True)
    back_box[sp] = sums_tile(first, second)
    to_spatial(back_box, BACK)

    for side in range(2):
        wait_bytes(recv_sem.at[CUBE + side], cube_box.at[side, pl.ds(1, 7)])
        summed = cube_box[side, 0].astype(F32)
        for d in range(1, 8):
            summed = summed + cube_box[side, d].astype(F32)
        weight_sum[side] = summed[0:half, :].T
        tail_sum[side * 16 : (side + 1) * 16, :] = summed[half : half + 16, :]

    def part_of(number):
        rows = block_of((number // 4) % 4) * 32 + (number % 4) * part
        return weight_sum.at[number // 16, pl.ds(pl.multiple_of(rows, part), part)]

    @pl.loop(1, n_dp, unroll=True)
    def _(i):
        number = lax.rem(rank + i, n_dp)
        remote(part_of(number), tile_box.at[rank], send_sem.at[TILE], recv_sem.at[TILE], of_rank(number)).start()

    for m in range(4):
        number = quarter * 4 + m

        @pl.when(number != rank)
        def _():
            remote(
                tail_sum.at[pl.ds(m * part, part)],
                tail_box.at[rank],
                send_sem.at[TAIL],
                recv_sem.at[TAIL],
                of_rank(number),
            ).start()

        @pl.when(number == rank)
        def _():
            tail_box[rank] = tail_sum[m * part : (m + 1) * part, :]

    tile_box[rank] = part_of(rank)[...]

    receive(back_box, BACK)
    back = total(back_box)
    for i in range(4):
        pair_there = lax.rem(sp - 4 * i + n_sp, n_sp)
        wanted_row = jnp.sum(jnp.where(row == pair_there // 2, embed, 0.0), axis=0, keepdims=True)
        mod_out[i] = jnp.concatenate([back[i : i + 1, :], wanted_row, jnp.zeros((6, LANES), F32)], axis=0)
        for j in range(2):
            there = 2 * pair_there + j

            @pl.when(there != dp)
            def _():
                remote(mod_out.at[i], mod_box.at[dp], send_sem.at[MOD], recv_sem.at[MOD], (there, sp)).start()

            @pl.when(there == dp)
            def _():
                mod_box[dp] = mod_out[i]

    @pl.loop(0, tile_rows, unroll=True)
    def _(r):
        start = pl.multiple_of(r * width, width)
        column_shifts(hidden[pl.ds(start, width), :].astype(F32), hid_spread, pl.multiple_of(start + width, width), False)

    for tap in range(9):
        w_stack[tap * channels : (tap + 1) * channels, :] = w_conv[:, tap * channels : (tap + 1) * channels]
    receive_edges(hidden, hid_edge, 2)
    column_shifts(hid_edge[0].astype(F32), hid_spread, 0, False)
    column_shifts(hid_edge[1].astype(F32), hid_spread, pixels + width, False)

    @pl.loop(0, 2)
    def _(c):
        start = pl.multiple_of(c * chunk, chunk)
        conv = merged[pl.ds(start, chunk), :].astype(F32)
        for dr in range(3):
            conv = conv + dot(
                hid_spread[pl.ds(pl.multiple_of(start + dr * width, width), chunk), :],
                w_stack[3 * dr * channels : 3 * (dr + 1) * channels, :],
            )
        out_ref[pl.ds(start, chunk), :] = conv.astype(BF16)

    stores = [
        pltpu.make_async_copy(source, target, store_sem.at[i])
        for i, (source, target) in enumerate(
            (
                (out_ref, out_hbm), (grad_feat_ref, grad_feat_hbm),
                (grad_mod_ref, grad_mod_hbm), (grad_conv_ref, grad_conv_hbm),
            )
        )
    ]
    stores[0].start()

    gain_tile = jnp.concatenate(as_rows(gain) + as_rows(gain), axis=0)
    means = group_total(back[0:4, :] * gain_tile, channels // GROUPS) / fine_count
    mean_two, mean_one = as_row(means, 0, 2), as_row(means, 2, 2)

    @pl.loop(0, tile_rows, unroll=True)
    def _(r):
        start = pl.multiple_of(r * width, width)
        normed = (merged[pl.ds(start, width), :].astype(F32) - center) * scale
        inner = grad_hid[pl.ds(start, width), :] * gain - mean_one - normed * mean_two
        grad_feat_ref[pl.ds(start, width), :] = (cot[pl.ds(start, width), :].astype(F32) + scale * inner).astype(BF16)

    stores[1].start()

    receive(tile_box, TILE)
    final_box[sp, 0] = total(tile_box)

    def to_group(source):
        @pl.loop(1, n_sp, unroll=True)
        def _(i):
            there = lax.rem(sp + i, n_sp)
            remote(source, source, send_sem.at[FINAL], recv_sem.at[FINAL], (dp, there)).start()

    @pl.when(owns_tail)
    def _():
        receive(tail_box, TAIL)
        final_box[sp, 1] = total(tail_box)
        to_group(final_box.at[sp])

    @pl.when(jnp.logical_not(owns_tail))
    def _():
        to_group(final_box.at[sp, 0])

    @pl.when(quarter_owner)
    def _():
        receive(mod_box, MOD)
        share = 8 * LANES // n_dp
        in_lanes = LANES // share
        embeds = mod_box[:, 1, :].astype(BF16)
        rest = mod_box[:, 0, :]
        grads = None
        for _ in range(3):
            piece = rest.astype(BF16)
            rest = rest - piece.astype(F32)
            term = dot(embeds, piece, ((0,), (0,)))
            grads = term if grads is None else grads + term
        mod_rows[...] = grads
        mod_start = pl.multiple_of((dp % in_lanes) * share, share)
        number = from_first // 4
        grad_mod_parts[number] = mod_rows[pl.ds(mod_start, share), :].astype(BF16)
        from_owner(grad_mod_parts.at[number], GRAD_MOD)

    @pl.when(owns_tail)
    def _():
        wait_bytes(recv_sem.at[FINAL], tile_box.at[pl.ds(0, n_sp)])

    @pl.when(jnp.logical_not(owns_tail))
    def _():
        wait_bytes(recv_sem.at[FINAL], tile_box.at[pl.ds(0, n_sp + 1)])

    holders = [
        8 * (tap // 4) + 2 * (2 * (tap % 2) + (tap // 2) % 2) + side for tap in range(8) for side in range(2)
    ]
    tail_place = (high_y // 2) * 8 + (high_y % 2) * 2
    grad_conv_ref[...] = jnp.concatenate(
        [final_box[j, 0] for j in holders] + [final_box[tail_place, 1], final_box[tail_place + 1, 1]], axis=1
    ).astype(BF16)

    stores[3].start()

    @pl.when(quarter_owner)
    def _():
        wait_bytes(recv_sem.at[GRAD_MOD], grad_mod_parts.at[pl.ds(0, 3)])

    @pl.when(jnp.logical_not(quarter_owner))
    def _():
        wait_bytes(recv_sem.at[GRAD_MOD], grad_mod_parts)

    grad_mod_ref[...] = jnp.concatenate([grad_mod_parts[i] for i in range(4)], axis=1)
    stores[2].start()

    for box, index in (
        (fine_box, FINE), (back_box, BACK), (text_box, TEXT), (tile_box, TILE),
    ):
        wait_bytes(send_sem.at[index], others(box))

    for side in range(2):
        wait_bytes(send_sem.at[CUBE + side], cube_box.at[side, pl.ds(1, 7)])
    sent_to_owners(text_dp_box, TEXT_DP)

    @pl.when(quarter_owner)
    def _():
        wait_bytes(send_sem.at[MOD], mod_box.at[pl.ds(0, 7)])
        rows = (n_sp - 1) * grad_mod_parts.shape[1] // 2
        wait_bytes(send_sem.at[GRAD_MOD], hidden.at[pl.ds(0, rows)])

    @pl.when(jnp.logical_not(quarter_owner))
    def _():
        wait_bytes(send_sem.at[MOD], mod_box.at[pl.ds(0, 8)])

    @pl.when(owner)
    def _():
        wait_bytes(send_sem.at[POOLED], fine_box.at[pl.ds(0, n_sp - 1)])

    pair_cot.wait_send()
    wait_bytes(send_sem.at[PAIR_HIDDEN], hidden_pair.at[pl.ds(0, pixels)])

    @pl.when(sends_far)
    def _():
        far.wait_send()

    finish_edges(cot, cot_edge, 0)
    finish_edges(hidden, hid_edge, 2)

    @pl.when(owns_tail)
    def _():
        wait_bytes(send_sem.at[TAIL], tail_box.at[pl.ds(0, 3)])
        wait_bytes(send_sem.at[FINAL], tile_box.at[pl.ds(0, 2 * (n_sp - 1))])

    @pl.when(jnp.logical_not(owns_tail))
    def _():
        wait_bytes(send_sem.at[TAIL], tail_box.at[pl.ds(0, 4)])
        wait_bytes(send_sem.at[FINAL], tile_box.at[pl.ds(0, n_sp - 1)])

    for store in stores:
        store.wait()


def write(*refs):
    sources, targets, rooms, load_sem, store_sem = refs[:4], refs[4:8], refs[8:12], refs[12], refs[13]
    moves = []
    for source, room, target in zip(sources, rooms, targets):
        rows = source.shape[0]
        pieces = 4 if rows >= 1024 else 1
        for i in range(pieces):
            piece = pl.ds(i * rows // pieces, rows // pieces)
            number = len(moves)
            moves.append(
                (
                    pltpu.make_async_copy(source.at[piece], room.at[piece], load_sem.at[number]),
                    pltpu.make_async_copy(room.at[piece], target.at[piece], store_sem.at[number]),
                )
            )
    for fetch, _ in moves:
        fetch.start()
    for fetch, store in moves:
        fetch.wait()
        store.start()
    for _, store in moves:
        store.wait()


def body(n_dp, n_sp, features, coarse, timestep, text_ids, text_table, w_mod, w_skip, w_conv, cotangent):
    _, tile_rows, width, channels = features.shape
    pixels = tile_rows * width
    cells = coarse.shape[1] * coarse.shape[2]
    coarse_width = coarse.shape[3]
    part, half = channels // n_dp, channels // 2
    taps = w_conv.shape[1] // channels
    vm = pltpu.VMEM
    tile = (8, LANES)
    anywhere = pl.BlockSpec(memory_space=pl.ANY)
    mod_rows = w_mod.shape[0] // n_dp
    scratch = [
        vm((pixels, channels), BF16),
        vm((pixels, channels), BF16),
        vm((part, taps * channels), BF16),
        vm((mod_rows, 2 * channels), BF16),
        vm(text_ids.shape, jnp.int32),
        vm((pixels, channels), BF16),
        vm((cells, coarse_width), BF16),
        vm(text_table.shape, BF16),
        vm(w_mod.shape, BF16),
        vm(w_skip.shape, BF16),
        vm(w_conv.shape, BF16),
        vm((taps * channels, channels), BF16),
        vm((pixels, channels), BF16),
        vm((2, width, channels), BF16),
        vm((width, half), BF16),
        vm((2, width, channels), BF16),
        vm((pixels, half), BF16),
        vm((2 * pixels + 2 * width, half), BF16),
        vm((pixels + 2 * width, 3 * channels), BF16),
        vm((3 * half, 2 * pixels + 2 * width), BF16),
        vm((pixels + 2 * width, 3 * channels), BF16),
        vm((4 * cells, cells), BF16),
        vm((4 * cells, channels), F32),
        vm((pixels, channels), BF16),
        vm((pixels, channels), BF16),
        vm((2 * pixels, channels), BF16),
        vm((pixels, channels), F32),
        vm((n_sp,) + tile, F32),
        vm((n_sp,) + tile, F32),
        vm((n_sp, 3) + tile, F32),
        vm((n_sp, 3) + tile, F32),
        vm((2,) + tile, F32),
        vm((n_dp,) + tile, F32),
        vm(tile, F32),
        vm((4,) + tile, F32),
        vm((n_dp,) + tile, F32),
        vm((LANES, LANES), F32),
        vm((4, mod_rows, LANES), BF16),
        vm((3, 3 * half, channels), F32),
        vm((2, 4, 2, half + 16, half), BF16),
        vm((2, 8, half + 16, half), BF16),
        vm((2, half, half), F32),
        vm((32, half), F32),
        vm((n_dp, part, half), F32),
        vm((n_dp, part, half), F32),
        vm((n_sp, 2, part, half), F32),
        pltpu.SemaphoreType.DMA((8,)),
        pltpu.SemaphoreType.DMA((4,)),
        pltpu.SemaphoreType.DMA((4,)),
        pltpu.SemaphoreType.DMA((4,)),
        pltpu.SemaphoreType.DMA((15,)),
        pltpu.SemaphoreType.DMA((15,)),
    ]
    shapes = (
        jax.ShapeDtypeStruct((pixels, channels), BF16),
        jax.ShapeDtypeStruct((pixels, channels), BF16),
        jax.ShapeDtypeStruct((part, taps * channels), BF16),
        jax.ShapeDtypeStruct((mod_rows, 2 * channels), BF16),
    )
    results = pl.pallas_call(
        functools.partial(kernel, n_dp, n_sp, tile_rows, width),
        out_shape=shapes,
        in_specs=[pl.BlockSpec(memory_space=pltpu.SMEM)] + [anywhere] * 8,
        out_specs=(anywhere,) * 4,
        scratch_shapes=scratch,
        compiler_params=pltpu.CompilerParams(
            collective_id=0, has_side_effects=True, vmem_limit_bytes=VMEM_LIMIT
        ),
    )(
        timestep,
        text_ids,
        features.reshape(pixels, channels),
        coarse.reshape(cells, coarse_width),
        text_table,
        w_mod,
        w_skip,
        w_conv,
        cotangent.reshape(pixels, channels),
    )
    output, grad_features, grad_conv, grad_mod = pl.pallas_call(
        write,
        out_shape=shapes,
        in_specs=[anywhere] * 4,
        out_specs=(anywhere,) * 4,
        scratch_shapes=[vm(shape.shape, shape.dtype) for shape in shapes]
        + [pltpu.SemaphoreType.DMA((10,)), pltpu.SemaphoreType.DMA((10,))],
        compiler_params=pltpu.CompilerParams(vmem_limit_bytes=VMEM_LIMIT),
    )(*results)
    return output.reshape(features.shape), grad_features.reshape(features.shape), grad_conv, grad_mod


def solution(mesh):
    in_specs = (
        P("dp", "spatial", None, None),
        P("dp", "spatial", None, None),
        P("dp"),
        P(),
        P(("dp", "spatial"), None),
        P(),
        P(),
        P(),
        P("dp", "spatial", None, None),
    )
    out_specs = (
        P("dp", "spatial", None, None),
        P("dp", "spatial", None, None),
        P("dp", None),
        P("dp", None),
    )
    step = functools.partial(body, mesh.shape["dp"], mesh.shape["spatial"])
    return jax.shard_map(step, mesh=mesh, in_specs=in_specs, out_specs=out_specs, check_vma=False)
```

```python
import functools
import math

import jax
import jax.numpy as jnp
from jax import lax
from jax.experimental import pallas as pl
from jax.experimental.pallas import tpu as pltpu
from jax.sharding import PartitionSpec as P

GROUPS = 32
EPS = 1e-05
MESH = pl.DeviceIdType.MESH
F32 = jnp.float32
BF16 = jnp.bfloat16
LANES = 128
VMEM_LIMIT = 62 * 1024 * 1024


def dot(a, b, dims=((1,), (0,))):
    return lax.dot_general(a, b, (dims, ((), ())), preferred_element_type=F32)


def iota(shape, axis):
    return lax.broadcasted_iota(jnp.int32, shape, axis)


def sigmoid(x):
    return 0.5 * jnp.tanh(0.5 * x) + 0.5


def group_total(tile, width):
    lane = iota(tile.shape, 1)
    step = 1
    while step < width:
        partner = jnp.where(
            (lane & step) != 0, pltpu.roll(tile, step, 1), pltpu.roll(tile, LANES - step, 1)
        )
        tile = tile + partner
        step *= 2
    return tile


def as_row(tile, first, count):
    return jnp.concatenate([tile[first + i : first + i + 1, :] for i in range(count)], axis=1)


def as_rows(row):
    return [row[:, i * LANES : (i + 1) * LANES] for i in range(row.shape[1] // LANES)]


def column_shifts(rows, spread_ref, first_row, reverse):
    width, channels = rows.shape
    column = iota(rows.shape, 0)
    earlier = jnp.where(column == 0, 0.0, pltpu.roll(rows, 1, 0)).astype(BF16)
    later = jnp.where(column == width - 1, 0.0, pltpu.roll(rows, width - 1, 0)).astype(BF16)
    left, right = (later, earlier) if reverse else (earlier, later)
    spread_ref[pl.ds(first_row, width), 0:channels] = left
    spread_ref[pl.ds(first_row, width), channels : 2 * channels] = rows.astype(BF16)
    spread_ref[pl.ds(first_row, width), 2 * channels : 3 * channels] = right


def turned_shifts(rows, turned_ref, first_pixel):
    width, channels = rows.shape
    turned = rows.T
    column = iota(turned.shape, 1)
    later = jnp.where(column == width - 1, 0.0, pltpu.roll(turned, width - 1, 1))
    earlier = jnp.where(column == 0, 0.0, pltpu.roll(turned, 1, 1))
    for i, shifted in enumerate((later, turned, earlier)):
        turned_ref[i * channels : (i + 1) * channels, pl.ds(first_pixel, width)] = shifted.astype(BF16)


def kernel(n_dp, n_sp, tile_rows, width, *refs):
    (
        time_ref, ids_hbm, feat_hbm, coarse_hbm, table_hbm, w_mod_hbm, w_skip_hbm, w_conv_hbm, cot_hbm,
        out_hbm, grad_feat_hbm, final_hbm, mod_hbm,
        out_ref, grad_feat_ref, ids_ref,
        feat, coarse, table, w_mod, w_skip, w_conv, w_stack, cot,
        cot_edge, far_edge, hid_edge, cot_half, cot_chip, cot_spread, cot_turned, hid_spread, chosen, up, merged,
        hidden, hidden_pair, grad_hid,
        coarse_box, fine_box, back_box, text_rows, text_out, text_box, text_sum, text_dp_box, pooled,
        mod_out, mod_box, mod_rows, mod_own, weight_own, cube_out, cube_box, weight_out, tail_sum,
        tile_box, tail_box, final_own,
        load_sem, store_sem, edge_send, edge_recv, send_sem, recv_sem,
    ) = refs
    channels = feat.shape[1]
    pixels = tile_rows * width
    half = channels // 2
    part = channels // n_dp
    dp = lax.axis_index("dp")
    sp = lax.axis_index("spatial")
    chip, core = sp // 2, sp % 2
    other_sp = sp + 1 - 2 * core

    y, z_high = dp // 4, dp % 4
    z_low, x = sp // 8, chip % 4
    z = 2 * z_high + z_low
    odd_x, odd_y, odd_z = x % 2, y % 2, z_low
    high_x, high_y = x // 2, y // 2
    quarter = 2 * odd_z + odd_x
    rank = high_x * 16 + high_y * 4 + z_high

    def block_of(high):
        return 2 * (high % 2) + high // 2

    def neighbour(side, d):
        dx, dy, dz = d % 2, (d // 2) % 2, d // 4
        x_there = (x + dx * (1 - 2 * odd_x) * (1 - 2 * side) + 4) % 4
        y_there = (y + dy * (1 - 2 * odd_y) * (1 - 2 * side) + 8) % 8
        z_there = (z + dz * (1 - 2 * odd_z) * (1 - 2 * side) + 8) % 8
        return (y_there * 4 + z_there // 2, (z_there % 2) * 8 + x_there * 2 + core)

    def gatherer(number):
        y_there, z_there = number // 4, number % 4
        return ((2 * y_there + odd_y) * 4 + z_there, z_low * 8 + (2 * (z_there % 2) + odd_x) * 2 + core)

    gathers = high_x == z_high % 2
    owns_tail = jnp.logical_and(gathers, high_y == quarter)
    owner = dp // 2 == sp
    from_first = lax.rem(sp - dp // 2 + n_sp, n_sp)
    quarter_owner = from_first % 4 == 0
    (
        COARSE, FINE, BACK, TEXT, TEXT_DP, POOLED, MOD, GRAD_MOD, TILE, TAIL, FINAL,
        PAIR_COT, PAIR_HIDDEN, FAR, CUBE,
    ) = range(15)

    def load(source, target, index):
        return pltpu.make_async_copy(source, target, load_sem.at[index])

    own_lanes = pl.ds(pl.multiple_of(core * half, half), half)
    other_lanes = pl.ds(pl.multiple_of((1 - core) * half, half), half)
    own_pixels = pl.multiple_of(core * pixels, pixels)
    other_pixels = pl.multiple_of((1 - core) * pixels, pixels)
    own_rows = pl.ds(pl.multiple_of(width + core * pixels, width), pixels)
    loads = [
        load(ids_hbm, ids_ref, 1),
        load(table_hbm, table, 2),
        load(coarse_hbm, coarse, 0),
        load(cot_hbm, cot, 3),
    ]
    later = [
        load(feat_hbm, feat, 4),
        load(w_skip_hbm, w_skip, 5),
        load(w_mod_hbm, w_mod, 6),
        load(w_conv_hbm, w_conv, 7),
    ]
    for copy in loads:
        copy.start()

    barrier = pltpu.get_barrier_semaphore()

    def greet(place):
        pl.semaphore_signal(barrier, inc=1, device_id=place, device_id_type=MESH)

    @pl.loop(1, n_sp, unroll=True)
    def _(i):
        greet((dp, lax.rem(sp + i, n_sp)))

    @pl.when(owner)
    def _():
        @pl.loop(1, n_dp)
        def _(i):
            greet((lax.rem(dp + i, n_dp), sp))

    for copy in later:
        copy.start()

    def remote(source, target, send, recv, place):
        return pltpu.make_async_remote_copy(
            src_ref=source, dst_ref=target, send_sem=send, recv_sem=recv, device_id=place, device_id_type=MESH
        )

    def wait_bytes(sem, ref):
        pltpu.make_async_copy(ref, ref, sem).wait()

    def to_spatial(box, index):
        @pl.loop(1, n_sp, unroll=True)
        def _(i):
            there = lax.rem(sp + i, n_sp)
            remote(box.at[sp], box.at[sp], send_sem.at[index], recv_sem.at[index], (dp, there)).start()

    def to_owners(source_of, box, index):
        for j in range(2):
            there = 2 * sp + j

            @pl.when(there != dp)
            def _():
                remote(source_of(j), box.at[dp], send_sem.at[index], recv_sem.at[index], (there, sp)).start()

    def sent_to_owners(box, index):
        @pl.when(owner)
        def _():
            wait_bytes(send_sem.at[index], box.at[pl.ds(0, 1)])

        @pl.when(jnp.logical_not(owner))
        def _():
            wait_bytes(send_sem.at[index], box.at[pl.ds(0, 2)])

    def from_owner(ref, index):
        @pl.loop(1, n_sp, unroll=True)
        def _(i):
            there = lax.rem(sp + i, n_sp)
            remote(ref, ref, send_sem.at[index], recv_sem.at[index], (dp, there)).start()

    def others(box):
        return box.at[pl.ds(0, box.shape[0] - 1)]

    def receive(box, index):
        wait_bytes(recv_sem.at[index], others(box))

    def total(box):
        return jnp.sum(box[...], axis=0)

    vocab = table.shape[0]
    batch, tokens = ids_ref.shape
    loads[0].wait()
    local_ids = jnp.concatenate(
        [ids_ref[pl.ds(j, n_sp, stride=2), :] for j in range(2)], axis=0
    ) - (dp * n_sp + sp) * vocab
    turned_ids = local_ids.astype(F32).T
    quarters = jnp.concatenate([turned_ids] * 4, axis=1) - 16.0 * lax.shift_right_logical(
        iota((tokens, LANES), 1), 5
    ).astype(F32)
    found = [
        jnp.sum(jnp.where(quarters == float(k), 1.0, 0.0), axis=0, keepdims=True) for k in range(16)
    ]
    found = jnp.concatenate(found, axis=0)
    counts = jnp.concatenate([found[:, q * batch : (q + 1) * batch] for q in range(4)], axis=0)[:vocab].astype(BF16)
    loads[1].wait()
    partial = dot(counts, table[...], ((0,), (0,)))
    for i in range(8):
        for j in range(2):
            text_rows[:, 8 * j + i, :] = partial[j * n_sp : (j + 1) * n_sp, i * LANES : (i + 1) * LANES]
    text_out[...] = text_rows[...].astype(BF16)

    loads[2].wait()
    coarse_f = coarse[...].astype(F32)
    coarse_box[sp] = jnp.concatenate(
        as_rows(jnp.sum(coarse_f, axis=0, keepdims=True))
        + as_rows(jnp.sum(coarse_f * coarse_f, axis=0, keepdims=True)),
        axis=0,
    )

    pl.semaphore_wait(barrier, jnp.where(owner, n_sp, n_sp + 1))

    @pl.loop(1, n_sp, unroll=True)
    def _(i):
        there = lax.rem(sp + i, n_sp)
        remote(text_out.at[there], text_box.at[sp], send_sem.at[TEXT], recv_sem.at[TEXT], (dp, there)).start()

    text_box[sp] = text_out[sp]
    to_spatial(coarse_box, COARSE)

    last = pixels - width

    def edges(source, target, first):
        down = remote(
            source.at[pl.ds(last, width)], target.at[0], edge_send.at[first], edge_recv.at[first], (dp, sp + 1)
        )
        upward = remote(
            source.at[pl.ds(0, width)], target.at[1], edge_send.at[first + 1], edge_recv.at[first + 1], (dp, sp - 1)
        )
        return down, upward

    def start_edges(source, target, first):
        down, upward = edges(source, target, first)

        @pl.when(sp < n_sp - 1)
        def _():
            down.start()

        @pl.when(sp > 0)
        def _():
            upward.start()

    def receive_edges(source, target, first):
        down, upward = edges(source, target, first)

        @pl.when(sp > 0)
        def _():
            down.wait_recv()

        @pl.when(sp < n_sp - 1)
        def _():
            upward.wait_recv()

        @pl.when(sp == 0)
        def _():
            target[0] = jnp.zeros((width, channels), BF16)

        @pl.when(sp == n_sp - 1)
        def _():
            target[1] = jnp.zeros((width, channels), BF16)

    def finish_edges(source, target, first):
        down, upward = edges(source, target, first)

        @pl.when(sp < n_sp - 1)
        def _():
            down.wait_send()

        @pl.when(sp > 0)
        def _():
            upward.wait_send()

    loads[3].wait()
    start_edges(cot, cot_edge, 0)
    cot_half[...] = cot[:, other_lanes]
    cot_chip[own_rows, :] = cot[:, own_lanes]
    pair_cot = remote(
        cot_half, cot_chip.at[own_rows], send_sem.at[PAIR_COT], recv_sem.at[PAIR_COT], (dp, other_sp)
    )
    pair_cot.start()
    far = remote(
        cot_chip.at[pl.ds(pl.multiple_of(width + core * (pixels + last), width), width)],
        far_edge,
        send_sem.at[FAR],
        recv_sem.at[FAR],
        (dp, sp - 2 + 4 * core),
    )
    chips = n_sp // 2
    sends_far = jnp.logical_or(jnp.logical_and(core == 0, chip > 0), jnp.logical_and(core == 1, chip < chips - 1))
    takes_far = jnp.logical_or(jnp.logical_and(core == 0, chip < chips - 1), jnp.logical_and(core == 1, chip > 0))

    @pl.when(sends_far)
    def _():
        far.start()

    shape = chosen.shape
    coarse_cols = width // 4
    place = iota(shape, 0)
    wanted = lax.shift_right_logical(place, width.bit_length() - 1) * coarse_cols + (
        lax.shift_right_logical(place & (width - 1), 2)
    )
    chosen[...] = (wanted == iota(shape, 1)).astype(F32).astype(BF16)

    def turn_rows(first_row):
        @pl.loop(0, tile_rows, unroll=True)
        def _(r):
            start = pl.multiple_of(first_row + r * width, width)
            turned_shifts(cot_chip[pl.ds(start, width), :].astype(F32), cot_turned, start)

    turn_rows(width + own_pixels)

    receive(text_box, TEXT)
    text_sum[...] = jnp.sum(text_box[...].astype(F32), axis=0)
    to_owners(lambda j: text_sum.at[pl.ds(8 * j, 8)], text_dp_box, TEXT_DP)

    later[1].wait()
    receive(coarse_box, COARSE)
    coarse_total = group_total(total(coarse_box), coarse.shape[1] // GROUPS)
    coarse_count = coarse.shape[0] * n_sp * (coarse.shape[1] // GROUPS)
    tiles = coarse.shape[1] // LANES
    c_mean = coarse_total[0:tiles, :] / coarse_count
    c_scale = lax.rsqrt(coarse_total[tiles : 2 * tiles, :] / coarse_count - c_mean * c_mean + EPS)
    c_normed = (coarse[...].astype(F32) - as_row(c_mean, 0, tiles)) * as_row(c_scale, 0, tiles)
    coarse_act = (c_normed * sigmoid(c_normed)).astype(BF16)
    skip = dot(coarse_act, w_skip[...]).astype(BF16)
    up[...] = dot(chosen[...], skip)

    later[0].wait()

    def merge(r, sums):
        start = pl.multiple_of(r * width, width)
        up_start = pl.multiple_of((r // 4) * width, width)
        rows = (feat[pl.ds(start, width), :].astype(F32) + up[pl.ds(up_start, width), :]).astype(BF16)
        merged[pl.ds(start, width), :] = rows
        rows = rows.astype(F32)
        first, second = sums
        first = first + jnp.sum(rows.reshape(width // 8, 8, channels), axis=0)
        second = second + jnp.sum((rows * rows).reshape(width // 8, 8, channels), axis=0)
        return first, second

    zero = jnp.zeros((8, channels), F32)
    first, second = lax.fori_loop(0, tile_rows, merge, (zero, zero), unroll=True)

    def sums_tile(one, two):
        one = jnp.sum(one, axis=0, keepdims=True)
        two = jnp.sum(two, axis=0, keepdims=True)
        return jnp.concatenate(as_rows(one) + as_rows(two) + [jnp.zeros((4, LANES), F32)], axis=0)

    fine_box[sp] = sums_tile(first, second)
    to_spatial(fine_box, FINE)

    @pl.when(owner)
    def _():
        text_dp_box[dp] = text_sum[pl.ds(pl.multiple_of(8 * (dp % 2), 8), 8), :]
        receive(text_dp_box, TEXT_DP)
        pooled[...] = total(text_dp_box)
        from_owner(pooled, POOLED)

    wait_bytes(recv_sem.at[PAIR_COT], cot_chip.at[own_rows])
    turn_rows(width + other_pixels)
    receive_edges(cot, cot_edge, 0)

    @pl.when(takes_far)
    def _():
        far.wait_recv()

    @pl.when(jnp.logical_not(takes_far))
    def _():
        far_edge[...] = jnp.zeros((width, half), BF16)

    near = cot_edge[core, :, own_lanes].astype(F32)
    farther = far_edge[...].astype(F32)
    turned_shifts(jnp.where(core == 0, near, farther), cot_turned, 0)
    turned_shifts(jnp.where(core == 0, farther, near), cot_turned, width + 2 * pixels)

    @pl.when(jnp.logical_not(owner))
    def _():
        wait_bytes(recv_sem.at[POOLED], pooled)

    row, lane = iota((8, LANES), 0), iota((8, LANES), 1)
    half_width = 4 * LANES
    index = ((row & 3) * LANES + lane).astype(F32)
    angle = time_ref[0].astype(F32) * jnp.exp(-math.log(10000.0) * index / half_width)
    embed = jnp.where(row < 4, jnp.sin(angle), jnp.cos(angle)) + pooled[...] / tokens
    embed = (embed * sigmoid(embed)).astype(BF16).astype(F32)
    later[2].wait()
    embed_row = jnp.broadcast_to(as_row(embed, 0, 8), (8, 8 * LANES)).astype(BF16)
    modulation = dot(embed_row, w_mod[...])[0:1, :]
    gain = 1.0 + modulation[:, :channels]
    shift = modulation[:, channels:]

    receive(fine_box, FINE)
    fine_total = group_total(total(fine_box), channels // GROUPS)
    fine_count = pixels * n_sp * (channels // GROUPS)
    f_mean = fine_total[0:2, :] / fine_count
    f_scale = lax.rsqrt(fine_total[2:4, :] / fine_count - f_mean * f_mean + EPS)
    center, scale = as_row(f_mean, 0, 2), as_row(f_scale, 0, 2)

    @pl.loop(0, tile_rows, unroll=True)
    def _(r):
        start = pl.multiple_of(r * width, width)
        pre = (merged[pl.ds(start, width), :].astype(F32) - center) * scale * gain + shift
        act = pre * sigmoid(pre)
        hidden[pl.ds(start, width), :] = act.astype(BF16)
        low, high = act[:, :half], act[:, half:]
        block = lax.shift_right_logical(iota(low.shape, 1), 5)
        even = jnp.where((block & 1) == 0, low, pltpu.roll(high, 32, 1))
        odd = jnp.where((block & 1) == 0, pltpu.roll(low, LANES - 32, 1), high)
        rows = pl.ds(pl.multiple_of(own_pixels + start, width), width)
        hidden_pair[rows, :] = jnp.concatenate([even, odd], axis=1).astype(BF16)

        @pl.when(r % 2 == 1)
        def _():
            two = pl.ds(pl.multiple_of(own_pixels + start - width, width), 2 * width)
            remote(
                hidden_pair.at[two], hidden_pair.at[two], send_sem.at[PAIR_HIDDEN], recv_sem.at[PAIR_HIDDEN], (dp, other_sp)
            ).start()

    def weight_term(dr, first_pixel):
        lanes = pl.ds(pl.multiple_of((2 - dr) * width + first_pixel, width), pixels)
        return dot(cot_turned[:, lanes], hidden_pair[pl.ds(first_pixel, pixels), :])

    for dr in range(3):
        weight_own[dr] = weight_term(dr, own_pixels)
    wait_bytes(recv_sem.at[PAIR_HIDDEN], hidden_pair.at[pl.ds(0, pixels)])
    for dr in range(3):
        grads = weight_own[dr] + weight_term(dr, other_pixels)
        for dc in range(3):
            tap = 3 * dr + dc
            grad = grads[dc * half : (dc + 1) * half, :]
            if tap < 8:
                cube_out[tap % 2, tap // 2, 0, 0:half] = grad[:, :half].astype(BF16)
                cube_out[tap % 2, tap // 2, 1, 0:half] = grad[:, half:].astype(BF16)
            else:
                turned = grad.T.astype(BF16)
                for side in range(2):
                    for number in range(8):
                        first = (number % 2) * half + block_of(number // 2) * 32 + side * 16
                        cube_out[side, number // 2, number % 2, half : half + 16] = turned[first : first + 16, :]

    for side in range(2):
        for d in range(1, 8):
            dx, dy, dz = d % 2, (d // 2) % 2, d // 4
            their_quarter = 2 * (odd_z + dz - 2 * odd_z * dz) + (odd_x + dx - 2 * odd_x * dx)
            their_y = odd_y + dy - 2 * odd_y * dy
            remote(
                cube_out.at[side, their_quarter, their_y],
                cube_box.at[side, d],
                send_sem.at[CUBE + side],
                recv_sem.at[CUBE + side],
                neighbour(side, d),
            ).start()
    for side in range(2):
        cube_box[side, 0] = cube_out[side, quarter, odd_y]

    start_edges(hidden, hid_edge, 2)

    @pl.loop(0, tile_rows, unroll=True)
    def _(r):
        start = pl.multiple_of(r * width, width)
        column_shifts(cot[pl.ds(start, width), :].astype(F32), cot_spread, pl.multiple_of(start + width, width), True)

    column_shifts(cot_edge[0].astype(F32), cot_spread, 0, True)
    column_shifts(cot_edge[1].astype(F32), cot_spread, pixels + width, True)
    later[3].wait()
    chunk = pixels // 2

    @pl.loop(0, 2)
    def _(c):
        start = pl.multiple_of(c * chunk, chunk)
        grad = None
        for dr in range(3):
            term = dot(
                cot_spread[pl.ds(pl.multiple_of(start + (2 - dr) * width, width), chunk), :],
                w_conv[:, 3 * dr * channels : 3 * (dr + 1) * channels],
                ((1,), (1,)),
            )
            grad = term if grad is None else grad + term
        grad_hid[pl.ds(start, chunk), :] = grad

    def backward(r, sums):
        start = pl.multiple_of(r * width, width)
        normed = (merged[pl.ds(start, width), :].astype(F32) - center) * scale
        pre = normed * gain + shift
        sigma = sigmoid(pre)
        grad = grad_hid[pl.ds(start, width), :] * sigma * (1.0 + pre * (1.0 - sigma))
        grad_hid[pl.ds(start, width), :] = grad
        first, second = sums
        first = first + jnp.sum((grad * normed).reshape(width // 8, 8, channels), axis=0)
        second = second + jnp.sum(grad.reshape(width // 8, 8, channels), axis=0)
        return first, second

    first, second = lax.fori_loop(0, tile_rows, backward, (zero, zero), unroll=True)
    back_box[sp] = sums_tile(first, second)
    to_spatial(back_box, BACK)

    sides = []
    for side in range(2):
        wait_bytes(recv_sem.at[CUBE + side], cube_box.at[side, pl.ds(1, 7)])
        summed = cube_box[side, 0].astype(F32)
        for d in range(1, 8):
            summed = summed + cube_box[side, d].astype(F32)
        sides.append(summed[0:half, :].T.reshape(16, part, half))
        tail_sum[side * 16 : (side + 1) * 16, :] = summed[half : half + 16, :]
    weight_out[...] = jnp.concatenate(sides, axis=1).astype(BF16)

    def part_of(number):
        return weight_out.at[block_of(number // 4) * 4 + number % 4]

    @pl.loop(0, 16, unroll=True)
    def _(i):
        number = lax.rem(high_y * 4 + z_high + i, 16)

        @pl.when(jnp.logical_or(i > 0, jnp.logical_not(gathers)))
        def _():
            remote(part_of(number), tile_box.at[rank], send_sem.at[TILE], recv_sem.at[TILE], gatherer(number)).start()

    for m in range(4):
        itself = jnp.logical_and(owns_tail, z_high == m)

        @pl.when(jnp.logical_not(itself))
        def _():
            remote(
                tail_sum.at[pl.ds(m * part, part)],
                tail_box.at[rank],
                send_sem.at[TAIL],
                recv_sem.at[TAIL],
                gatherer(quarter * 4 + m),
            ).start()

        @pl.when(itself)
        def _():
            tail_box[rank] = tail_sum[m * part : (m + 1) * part, :]

    @pl.when(gathers)
    def _():
        tile_box[rank] = part_of(high_y * 4 + z_high)[...]

    receive(back_box, BACK)
    back = total(back_box)
    for i in range(4):
        pair_there = lax.rem(sp - 4 * i + n_sp, n_sp)
        wanted_row = jnp.sum(jnp.where(row == pair_there // 2, embed, 0.0), axis=0, keepdims=True)
        mod_out[i] = jnp.concatenate([back[i : i + 1, :], wanted_row, jnp.zeros((6, LANES), F32)], axis=0)
        for j in range(2):
            there = 2 * pair_there + j

            @pl.when(there != dp)
            def _():
                remote(mod_out.at[i], mod_box.at[dp], send_sem.at[MOD], recv_sem.at[MOD], (there, sp)).start()

            @pl.when(there == dp)
            def _():
                mod_box[dp] = mod_out[i]

    @pl.loop(0, tile_rows, unroll=True)
    def _(r):
        start = pl.multiple_of(r * width, width)
        column_shifts(hidden[pl.ds(start, width), :].astype(F32), hid_spread, pl.multiple_of(start + width, width), False)

    for tap in range(9):
        w_stack[tap * channels : (tap + 1) * channels, :] = w_conv[:, tap * channels : (tap + 1) * channels]
    receive_edges(hidden, hid_edge, 2)
    column_shifts(hid_edge[0].astype(F32), hid_spread, 0, False)
    column_shifts(hid_edge[1].astype(F32), hid_spread, pixels + width, False)

    @pl.loop(0, 2)
    def _(c):
        start = pl.multiple_of(c * chunk, chunk)
        conv = merged[pl.ds(start, chunk), :].astype(F32)
        for dr in range(3):
            conv = conv + dot(
                hid_spread[pl.ds(pl.multiple_of(start + dr * width, width), chunk), :],
                w_stack[3 * dr * channels : 3 * (dr + 1) * channels, :],
            )
        out_ref[pl.ds(start, chunk), :] = conv.astype(BF16)

    stores = [
        pltpu.make_async_copy(source, target, store_sem.at[i])
        for i, (source, target) in enumerate(
            (
                (out_ref, out_hbm), (grad_feat_ref, grad_feat_hbm),
            )
        )
    ]
    stores[0].start()

    gain_tile = jnp.concatenate(as_rows(gain) + as_rows(gain), axis=0)
    means = group_total(back[0:4, :] * gain_tile, channels // GROUPS) / fine_count
    mean_two, mean_one = as_row(means, 0, 2), as_row(means, 2, 2)

    @pl.loop(0, tile_rows, unroll=True)
    def _(r):
        start = pl.multiple_of(r * width, width)
        normed = (merged[pl.ds(start, width), :].astype(F32) - center) * scale
        inner = grad_hid[pl.ds(start, width), :] * gain - mean_one - normed * mean_two
        grad_feat_ref[pl.ds(start, width), :] = (cot[pl.ds(start, width), :].astype(F32) + scale * inner).astype(BF16)

    stores[1].start()

    final_slot = 2 * quarter + core

    def to_group(rows):
        @pl.loop(1, n_sp, unroll=True)
        def _(i):
            remote(
                final_own.at[rows],
                final_hbm.at[final_slot, rows],
                send_sem.at[FINAL],
                recv_sem.at[FINAL],
                (dp, lax.rem(sp + i, n_sp)),
            ).start()

    def own_final(rows):
        return pltpu.make_async_copy(final_own.at[rows], final_hbm.at[final_slot, rows], store_sem.at[2])

    main, both = pl.ds(0, 16), pl.ds(0, 32)
    no_tail = jnp.logical_and(gathers, jnp.logical_not(owns_tail))

    @pl.when(gathers)
    def _():
        receive(tile_box, TILE)
        final_own[0:16, :] = jnp.sum(tile_box[...].astype(F32), axis=0).astype(BF16)

    @pl.when(no_tail)
    def _():
        to_group(main)
        own_final(main).start()

    @pl.when(owns_tail)
    def _():
        receive(tail_box, TAIL)
        final_own[16:32, :] = jnp.concatenate([total(tail_box), jnp.zeros((part, half), F32)], axis=0).astype(BF16)
        to_group(both)
        own_final(both).start()

    @pl.when(quarter_owner)
    def _():
        receive(mod_box, MOD)
        share = 8 * LANES // n_dp
        in_lanes = LANES // share
        embeds = mod_box[:, 1, :].astype(BF16)
        rest = mod_box[:, 0, :]
        grads = None
        for _ in range(3):
            piece = rest.astype(BF16)
            rest = rest - piece.astype(F32)
            term = dot(embeds, piece, ((0,), (0,)))
            grads = term if grads is None else grads + term
        mod_rows[...] = grads
        mod_start = pl.multiple_of((dp % in_lanes) * share, share)
        number = from_first // 4
        mod_own[...] = mod_rows[pl.ds(mod_start, share), :].astype(BF16)

        @pl.loop(1, n_sp, unroll=True)
        def _(i):
            there = lax.rem(sp + i, n_sp)
            remote(mod_own, mod_hbm.at[number], send_sem.at[GRAD_MOD], recv_sem.at[GRAD_MOD], (dp, there)).start()

        pltpu.make_async_copy(mod_own, mod_hbm.at[number], store_sem.at[3]).start()

    def units(count):
        return tile_box.at[pl.ds(0, count)]

    @pl.when(jnp.logical_not(gathers))
    def _():
        wait_bytes(recv_sem.at[FINAL], units(10))

    @pl.when(no_tail)
    def _():
        wait_bytes(recv_sem.at[FINAL], units(9))
        wait_bytes(send_sem.at[FINAL], units(n_sp - 1))
        wait_bytes(send_sem.at[TILE], units(15))
        own_final(main).wait()

    @pl.when(owns_tail)
    def _():
        wait_bytes(recv_sem.at[FINAL], units(8))
        wait_bytes(send_sem.at[FINAL], units(2 * (n_sp - 1)))
        wait_bytes(send_sem.at[TILE], units(15))
        own_final(both).wait()

    @pl.when(jnp.logical_not(gathers))
    def _():
        wait_bytes(send_sem.at[TILE], units(16))

    @pl.when(quarter_owner)
    def _():
        wait_bytes(recv_sem.at[GRAD_MOD], mod_hbm.at[pl.ds(0, 3)])
        pltpu.make_async_copy(mod_own, mod_hbm.at[from_first // 4], store_sem.at[3]).wait()

    @pl.when(jnp.logical_not(quarter_owner))
    def _():
        wait_bytes(recv_sem.at[GRAD_MOD], mod_hbm)

    for box, index in (
        (fine_box, FINE), (back_box, BACK), (text_box, TEXT), (coarse_box, COARSE),
    ):
        wait_bytes(send_sem.at[index], others(box))

    for side in range(2):
        wait_bytes(send_sem.at[CUBE + side], cube_box.at[side, pl.ds(1, 7)])
    sent_to_owners(text_dp_box, TEXT_DP)

    @pl.when(quarter_owner)
    def _():
        wait_bytes(send_sem.at[MOD], mod_box.at[pl.ds(0, 7)])
        wait_bytes(send_sem.at[GRAD_MOD], units(2 * (n_sp - 1)))

    @pl.when(jnp.logical_not(quarter_owner))
    def _():
        wait_bytes(send_sem.at[MOD], mod_box.at[pl.ds(0, 8)])

    @pl.when(owner)
    def _():
        wait_bytes(send_sem.at[POOLED], fine_box.at[pl.ds(0, n_sp - 1)])

    pair_cot.wait_send()
    wait_bytes(send_sem.at[PAIR_HIDDEN], hidden_pair.at[pl.ds(0, pixels)])

    @pl.when(sends_far)
    def _():
        far.wait_send()

    finish_edges(cot, cot_edge, 0)
    finish_edges(hidden, hid_edge, 2)

    @pl.when(owns_tail)
    def _():
        wait_bytes(send_sem.at[TAIL], tail_box.at[pl.ds(0, 3)])

    @pl.when(jnp.logical_not(owns_tail))
    def _():
        wait_bytes(send_sem.at[TAIL], tail_box.at[pl.ds(0, 4)])

    for store in stores:
        store.wait()


def write(
    out, grad_feat, final, mod, out_hbm, grad_feat_hbm, grad_conv_hbm, grad_mod_hbm,
    out_room, grad_feat_room, final_room, mod_room, grad_conv, grad_mod, load_sem, store_sem,
):
    fetch_final = pltpu.make_async_copy(final, final_room, load_sem.at[4])
    fetch_mod = pltpu.make_async_copy(mod, mod_room, load_sem.at[5])
    fetch_final.start()
    fetch_mod.start()
    moves = []
    for source, room, target in ((out, out_room, out_hbm), (grad_feat, grad_feat_room, grad_feat_hbm)):
        rows = source.shape[0] // 2
        for i in range(2):
            piece = pl.ds(i * rows, rows)
            number = len(moves)
            moves.append(
                (
                    pltpu.make_async_copy(source.at[piece], room.at[piece], load_sem.at[number]),
                    pltpu.make_async_copy(room.at[piece], target.at[piece], store_sem.at[number]),
                )
            )
    for fetch, _ in moves:
        fetch.start()
    fetch_final.wait()
    parts = final_room[...].astype(F32)
    tail_quarter = lax.axis_index("dp") // 8
    columns = [
        parts[2 * (tap // 2) + side, 8 * (tap % 2) : 8 * (tap % 2) + 8, :] for tap in range(8) for side in range(2)
    ] + [final_room[2 * tail_quarter + side].astype(F32)[16:24, :] for side in range(2)]
    grad_conv[...] = jnp.concatenate(columns, axis=1).astype(BF16)
    fetch_mod.wait()
    grad_mod[...] = jnp.concatenate([mod_room[i] for i in range(4)], axis=1)
    last = [
        pltpu.make_async_copy(grad_conv, grad_conv_hbm, store_sem.at[4]),
        pltpu.make_async_copy(grad_mod, grad_mod_hbm, store_sem.at[5]),
    ]
    for store in last:
        store.start()
    for fetch, store in moves:
        fetch.wait()
        store.start()
    for _, store in moves:
        store.wait()
    for store in last:
        store.wait()


def body(n_dp, n_sp, features, coarse, timestep, text_ids, text_table, w_mod, w_skip, w_conv, cotangent):
    _, tile_rows, width, channels = features.shape
    pixels = tile_rows * width
    cells = coarse.shape[1] * coarse.shape[2]
    coarse_width = coarse.shape[3]
    part, half = channels // n_dp, channels // 2
    taps = w_conv.shape[1] // channels
    vm = pltpu.VMEM
    tile = (8, LANES)
    anywhere = pl.BlockSpec(memory_space=pl.ANY)
    mod_rows = w_mod.shape[0] // n_dp
    scratch = [
        vm((pixels, channels), BF16),
        vm((pixels, channels), BF16),
        vm(text_ids.shape, jnp.int32),
        vm((pixels, channels), BF16),
        vm((cells, coarse_width), BF16),
        vm(text_table.shape, BF16),
        vm(w_mod.shape, BF16),
        vm(w_skip.shape, BF16),
        vm(w_conv.shape, BF16),
        vm((taps * channels, channels), BF16),
        vm((pixels, channels), BF16),
        vm((2, width, channels), BF16),
        vm((width, half), BF16),
        vm((2, width, channels), BF16),
        vm((pixels, half), BF16),
        vm((2 * pixels + 2 * width, half), BF16),
        vm((pixels + 2 * width, 3 * channels), BF16),
        vm((3 * half, 2 * pixels + 2 * width), BF16),
        vm((pixels + 2 * width, 3 * channels), BF16),
        vm((4 * cells, cells), BF16),
        vm((4 * cells, channels), F32),
        vm((pixels, channels), BF16),
        vm((pixels, channels), BF16),
        vm((2 * pixels, channels), BF16),
        vm((pixels, channels), F32),
        vm((n_sp,) + tile, F32),
        vm((n_sp,) + tile, F32),
        vm((n_sp,) + tile, F32),
        vm((n_sp, 16, LANES), F32),
        vm((n_sp, 16, LANES), BF16),
        vm((n_sp, 16, LANES), BF16),
        vm((16, LANES), F32),
        vm((n_dp,) + tile, F32),
        vm(tile, F32),
        vm((4,) + tile, F32),
        vm((n_dp,) + tile, F32),
        vm((LANES, LANES), F32),
        vm((mod_rows, LANES), BF16),
        vm((3, 3 * half, channels), F32),
        vm((2, 4, 2, half + 16, half), BF16),
        vm((2, 8, half + 16, half), BF16),
        vm((16, 2 * part, half), BF16),
        vm((32, half), F32),
        vm((n_dp, 2 * part, half), BF16),
        vm((n_dp, part, half), F32),
        vm((32, half), BF16),
        pltpu.SemaphoreType.DMA((8,)),
        pltpu.SemaphoreType.DMA((4,)),
        pltpu.SemaphoreType.DMA((4,)),
        pltpu.SemaphoreType.DMA((4,)),
        pltpu.SemaphoreType.DMA((16,)),
        pltpu.SemaphoreType.DMA((16,)),
    ]
    shapes = (
        jax.ShapeDtypeStruct((pixels, channels), BF16),
        jax.ShapeDtypeStruct((pixels, channels), BF16),
        jax.ShapeDtypeStruct((8, 32, half), BF16),
        jax.ShapeDtypeStruct((4, mod_rows, LANES), BF16),
    )
    written = shapes[:2] + (
        jax.ShapeDtypeStruct((part, taps * channels), BF16),
        jax.ShapeDtypeStruct((mod_rows, 2 * channels), BF16),
    )
    results = pl.pallas_call(
        functools.partial(kernel, n_dp, n_sp, tile_rows, width),
        out_shape=shapes,
        in_specs=[pl.BlockSpec(memory_space=pltpu.SMEM)] + [anywhere] * 8,
        out_specs=(anywhere,) * 4,
        scratch_shapes=scratch,
        compiler_params=pltpu.CompilerParams(
            collective_id=0, has_side_effects=True, vmem_limit_bytes=VMEM_LIMIT
        ),
    )(
        timestep,
        text_ids,
        features.reshape(pixels, channels),
        coarse.reshape(cells, coarse_width),
        text_table,
        w_mod,
        w_skip,
        w_conv,
        cotangent.reshape(pixels, channels),
    )
    output, grad_features, grad_conv, grad_mod = pl.pallas_call(
        write,
        out_shape=written,
        in_specs=[anywhere] * 4,
        out_specs=(anywhere,) * 4,
        scratch_shapes=[vm(shape.shape, shape.dtype) for shape in shapes + written[2:]]
        + [pltpu.SemaphoreType.DMA((6,)), pltpu.SemaphoreType.DMA((6,))],
        compiler_params=pltpu.CompilerParams(vmem_limit_bytes=VMEM_LIMIT),
    )(*results)
    return output.reshape(features.shape), grad_features.reshape(features.shape), grad_conv, grad_mod


def solution(mesh):
    in_specs = (
        P("dp", "spatial", None, None),
        P("dp", "spatial", None, None),
        P("dp"),
        P(),
        P(("dp", "spatial"), None),
        P(),
        P(),
        P(),
        P("dp", "spatial", None, None),
    )
    out_specs = (
        P("dp", "spatial", None, None),
        P("dp", "spatial", None, None),
        P("dp", None),
        P("dp", None),
    )
    step = functools.partial(body, mesh.shape["dp"], mesh.shape["spatial"])
    return jax.shard_map(step, mesh=mesh, in_specs=in_specs, out_specs=out_specs, check_vma=False)
```

```python
import functools
import math

import jax
import jax.numpy as jnp
from jax import lax
from jax.experimental import pallas as pl
from jax.experimental.pallas import tpu as pltpu
from jax.sharding import PartitionSpec as P

GROUPS = 32
EPS = 1e-05
MESH = pl.DeviceIdType.MESH
F32 = jnp.float32
BF16 = jnp.bfloat16
LANES = 128
VMEM_LIMIT = 62 * 1024 * 1024


def dot(a, b, dims=((1,), (0,))):
    return lax.dot_general(a, b, (dims, ((), ())), preferred_element_type=F32)


def iota(shape, axis):
    return lax.broadcasted_iota(jnp.int32, shape, axis)


def sigmoid(x):
    return 0.5 * jnp.tanh(0.5 * x) + 0.5


def group_total(tile, width):
    lane = iota(tile.shape, 1)
    step = 1
    while step < width:
        partner = jnp.where(
            (lane & step) != 0, pltpu.roll(tile, step, 1), pltpu.roll(tile, LANES - step, 1)
        )
        tile = tile + partner
        step *= 2
    return tile


def as_row(tile, first, count):
    return jnp.concatenate([tile[first + i : first + i + 1, :] for i in range(count)], axis=1)


def as_rows(row):
    return [row[:, i * LANES : (i + 1) * LANES] for i in range(row.shape[1] // LANES)]


def column_shifts(rows, spread_ref, first_row, reverse):
    width, channels = rows.shape
    column = iota(rows.shape, 0)
    earlier = jnp.where(column == 0, 0.0, pltpu.roll(rows, 1, 0)).astype(BF16)
    later = jnp.where(column == width - 1, 0.0, pltpu.roll(rows, width - 1, 0)).astype(BF16)
    left, right = (later, earlier) if reverse else (earlier, later)
    spread_ref[pl.ds(first_row, width), 0:channels] = left
    spread_ref[pl.ds(first_row, width), channels : 2 * channels] = rows.astype(BF16)
    spread_ref[pl.ds(first_row, width), 2 * channels : 3 * channels] = right


def turned_shifts(rows, turned_ref, first_pixel):
    width, channels = rows.shape
    turned = rows.T
    column = iota(turned.shape, 1)
    later = jnp.where(column == width - 1, 0.0, pltpu.roll(turned, width - 1, 1))
    earlier = jnp.where(column == 0, 0.0, pltpu.roll(turned, 1, 1))
    for i, shifted in enumerate((later, turned, earlier)):
        turned_ref[i * channels : (i + 1) * channels, pl.ds(first_pixel, width)] = shifted.astype(BF16)


def kernel(n_dp, n_sp, tile_rows, width, *refs):
    (
        time_ref, ids_hbm, feat_hbm, coarse_hbm, table_hbm, w_mod_hbm, w_skip_hbm, w_conv_hbm, cot_hbm,
        out_hbm, grad_feat_hbm, final_hbm, mod_hbm,
        out_ref, grad_feat_ref, ids_ref,
        feat, coarse, table, w_mod, w_skip, w_conv, w_stack, cot,
        cot_edge, far_edge, hid_edge, cot_half, cot_chip, cot_spread, cot_turned, hid_spread, chosen, up, merged,
        hidden, hidden_pair, grad_hid,
        coarse_box, fine_box, back_box, text_rows, text_out, text_box, text_sum, text_dp_box, pooled, time_part,
        mod_out, mod_box, mod_rows, mod_own, weight_own, cube_out, cube_box, weight_out, tail_sum,
        tile_box, tail_box, final_own,
        load_sem, store_sem, edge_send, edge_recv, send_sem, recv_sem,
    ) = refs
    channels = feat.shape[1]
    pixels = tile_rows * width
    half = channels // 2
    part = channels // n_dp
    dp = lax.axis_index("dp")
    sp = lax.axis_index("spatial")
    chip, core = sp // 2, sp % 2
    other_sp = sp + 1 - 2 * core

    y, z_high = dp // 4, dp % 4
    z_low, x = sp // 8, chip % 4
    z = 2 * z_high + z_low
    odd_x, odd_y, odd_z = x % 2, y % 2, z_low
    high_x, high_y = x // 2, y // 2
    quarter = 2 * odd_z + odd_x
    rank = high_x * 16 + high_y * 4 + z_high

    def block_of(high):
        return 2 * (high % 2) + high // 2

    def neighbour(side, d):
        dx, dy, dz = d % 2, (d // 2) % 2, d // 4
        x_there = (x + dx * (1 - 2 * odd_x) * (1 - 2 * side) + 4) % 4
        y_there = (y + dy * (1 - 2 * odd_y) * (1 - 2 * side) + 8) % 8
        z_there = (z + dz * (1 - 2 * odd_z) * (1 - 2 * side) + 8) % 8
        return (y_there * 4 + z_there // 2, (z_there % 2) * 8 + x_there * 2 + core)

    def gatherer(number):
        y_there, z_there = number // 4, number % 4
        return ((2 * y_there + odd_y) * 4 + z_there, z_low * 8 + (2 * (z_there % 2) + odd_x) * 2 + core)

    gathers = high_x == z_high % 2
    owns_tail = jnp.logical_and(gathers, high_y == quarter)
    owner = dp // 2 == sp
    from_first = lax.rem(sp - dp // 2 + n_sp, n_sp)
    quarter_owner = from_first % 4 == 0
    (
        COARSE, FINE, BACK, TEXT, TEXT_DP, POOLED, MOD, GRAD_MOD, TILE, TAIL, FINAL,
        PAIR_COT, PAIR_HIDDEN, FAR, CUBE,
    ) = range(15)

    def load(source, target, index):
        return pltpu.make_async_copy(source, target, load_sem.at[index])

    own_lanes = pl.ds(pl.multiple_of(core * half, half), half)
    other_lanes = pl.ds(pl.multiple_of((1 - core) * half, half), half)
    own_pixels = pl.multiple_of(core * pixels, pixels)
    other_pixels = pl.multiple_of((1 - core) * pixels, pixels)
    own_rows = pl.ds(pl.multiple_of(width + core * pixels, width), pixels)
    loads = [
        load(ids_hbm, ids_ref, 1),
        load(table_hbm, table, 2),
        load(coarse_hbm, coarse, 0),
        load(cot_hbm, cot, 3),
    ]
    later = [
        load(feat_hbm, feat, 4),
        load(w_skip_hbm, w_skip, 5),
        load(w_mod_hbm, w_mod, 6),
        load(w_conv_hbm, w_conv, 7),
    ]
    for copy in loads[:2]:
        copy.start()

    barrier = pltpu.get_barrier_semaphore()

    def greet(place):
        pl.semaphore_signal(barrier, inc=1, device_id=place, device_id_type=MESH)

    @pl.loop(1, n_sp, unroll=True)
    def _(i):
        greet((dp, lax.rem(sp + i, n_sp)))

    @pl.when(owner)
    def _():
        @pl.loop(1, n_dp)
        def _(i):
            greet((lax.rem(dp + i, n_dp), sp))

    for copy in loads[2:] + later:
        copy.start()

    def remote(source, target, send, recv, place):
        return pltpu.make_async_remote_copy(
            src_ref=source, dst_ref=target, send_sem=send, recv_sem=recv, device_id=place, device_id_type=MESH
        )

    def wait_bytes(sem, ref):
        pltpu.make_async_copy(ref, ref, sem).wait()

    def to_spatial(box, index):
        @pl.loop(1, n_sp, unroll=True)
        def _(i):
            there = lax.rem(sp + i, n_sp)
            remote(box.at[sp], box.at[sp], send_sem.at[index], recv_sem.at[index], (dp, there)).start()

    def to_owners(source_of, box, index):
        for j in range(2):
            there = 2 * sp + j

            @pl.when(there != dp)
            def _():
                remote(source_of(j), box.at[dp], send_sem.at[index], recv_sem.at[index], (there, sp)).start()

    def sent_to_owners(box, index):
        @pl.when(owner)
        def _():
            wait_bytes(send_sem.at[index], box.at[pl.ds(0, 1)])

        @pl.when(jnp.logical_not(owner))
        def _():
            wait_bytes(send_sem.at[index], box.at[pl.ds(0, 2)])

    def from_owner(ref, index):
        @pl.loop(1, n_sp, unroll=True)
        def _(i):
            there = lax.rem(sp + i, n_sp)
            remote(ref, ref, send_sem.at[index], recv_sem.at[index], (dp, there)).start()

    def others(box):
        return box.at[pl.ds(0, box.shape[0] - 1)]

    def receive(box, index):
        wait_bytes(recv_sem.at[index], others(box))

    def total(box):
        return jnp.sum(box[...], axis=0)

    vocab = table.shape[0]
    batch, tokens = ids_ref.shape
    loads[0].wait()
    local_ids = jnp.concatenate(
        [ids_ref[pl.ds(j, n_sp, stride=2), :] for j in range(2)], axis=0
    ) - (dp * n_sp + sp) * vocab
    turned_ids = local_ids.astype(F32).T
    quarters = jnp.concatenate([turned_ids] * 4, axis=1) - 16.0 * lax.shift_right_logical(
        iota((tokens, LANES), 1), 5
    ).astype(F32)
    found = [
        jnp.sum(jnp.where(quarters == float(k), 1.0, 0.0), axis=0, keepdims=True) for k in range(16)
    ]
    found = jnp.concatenate(found, axis=0)
    counts = jnp.concatenate([found[:, q * batch : (q + 1) * batch] for q in range(4)], axis=0)[:vocab].astype(BF16)
    loads[1].wait()
    partial = dot(counts, table[...], ((0,), (0,)))
    for i in range(8):
        for j in range(2):
            text_rows[:, 8 * j + i, :] = partial[j * n_sp : (j + 1) * n_sp, i * LANES : (i + 1) * LANES]
    text_out[...] = text_rows[...].astype(BF16)

    loads[2].wait()
    coarse_f = coarse[...].astype(F32)
    coarse_box[sp] = jnp.concatenate(
        as_rows(jnp.sum(coarse_f, axis=0, keepdims=True))
        + as_rows(jnp.sum(coarse_f * coarse_f, axis=0, keepdims=True)),
        axis=0,
    )

    pl.semaphore_wait(barrier, jnp.where(owner, n_sp, n_sp + 1))

    @pl.loop(1, n_sp, unroll=True)
    def _(i):
        there = lax.rem(sp + i, n_sp)
        remote(text_out.at[there], text_box.at[sp], send_sem.at[TEXT], recv_sem.at[TEXT], (dp, there)).start()

    text_box[sp] = text_out[sp]
    to_spatial(coarse_box, COARSE)

    last = pixels - width

    def edges(source, target, first):
        down = remote(
            source.at[pl.ds(last, width)], target.at[0], edge_send.at[first], edge_recv.at[first], (dp, sp + 1)
        )
        upward = remote(
            source.at[pl.ds(0, width)], target.at[1], edge_send.at[first + 1], edge_recv.at[first + 1], (dp, sp - 1)
        )
        return down, upward

    def start_edges(source, target, first):
        down, upward = edges(source, target, first)

        @pl.when(sp < n_sp - 1)
        def _():
            down.start()

        @pl.when(sp > 0)
        def _():
            upward.start()

    def receive_edges(source, target, first):
        down, upward = edges(source, target, first)

        @pl.when(sp > 0)
        def _():
            down.wait_recv()

        @pl.when(sp < n_sp - 1)
        def _():
            upward.wait_recv()

        @pl.when(sp == 0)
        def _():
            target[0] = jnp.zeros((width, channels), BF16)

        @pl.when(sp == n_sp - 1)
        def _():
            target[1] = jnp.zeros((width, channels), BF16)

    def finish_edges(source, target, first):
        down, upward = edges(source, target, first)

        @pl.when(sp < n_sp - 1)
        def _():
            down.wait_send()

        @pl.when(sp > 0)
        def _():
            upward.wait_send()

    loads[3].wait()
    start_edges(cot, cot_edge, 0)
    cot_half[...] = cot[:, other_lanes]
    cot_chip[own_rows, :] = cot[:, own_lanes]
    pair_cot = remote(
        cot_half, cot_chip.at[own_rows], send_sem.at[PAIR_COT], recv_sem.at[PAIR_COT], (dp, other_sp)
    )
    pair_cot.start()
    far = remote(
        cot_chip.at[pl.ds(pl.multiple_of(width + core * (pixels + last), width), width)],
        far_edge,
        send_sem.at[FAR],
        recv_sem.at[FAR],
        (dp, sp - 2 + 4 * core),
    )
    chips = n_sp // 2
    sends_far = jnp.logical_or(jnp.logical_and(core == 0, chip > 0), jnp.logical_and(core == 1, chip < chips - 1))
    takes_far = jnp.logical_or(jnp.logical_and(core == 0, chip < chips - 1), jnp.logical_and(core == 1, chip > 0))

    @pl.when(sends_far)
    def _():
        far.start()

    row, lane = iota((8, LANES), 0), iota((8, LANES), 1)
    half_width = 4 * LANES
    index = ((row & 3) * LANES + lane).astype(F32)
    angle = time_ref[0].astype(F32) * jnp.exp(-math.log(10000.0) * index / half_width)
    time_part[...] = jnp.where(row < 4, jnp.sin(angle), jnp.cos(angle))

    shape = chosen.shape
    coarse_cols = width // 4
    place = iota(shape, 0)
    wanted = lax.shift_right_logical(place, width.bit_length() - 1) * coarse_cols + (
        lax.shift_right_logical(place & (width - 1), 2)
    )
    chosen[...] = (wanted == iota(shape, 1)).astype(F32).astype(BF16)

    def turn_rows(first_row):
        @pl.loop(0, tile_rows, unroll=True)
        def _(r):
            start = pl.multiple_of(first_row + r * width, width)
            turned_shifts(cot_chip[pl.ds(start, width), :].astype(F32), cot_turned, start)

    turn_rows(width + own_pixels)

    receive(text_box, TEXT)
    text_sum[...] = jnp.sum(text_box[...].astype(F32), axis=0)
    to_owners(lambda j: text_sum.at[pl.ds(8 * j, 8)], text_dp_box, TEXT_DP)

    later[1].wait()
    receive(coarse_box, COARSE)
    coarse_total = group_total(total(coarse_box), coarse.shape[1] // GROUPS)
    coarse_count = coarse.shape[0] * n_sp * (coarse.shape[1] // GROUPS)
    tiles = coarse.shape[1] // LANES
    c_mean = coarse_total[0:tiles, :] / coarse_count
    c_scale = lax.rsqrt(coarse_total[tiles : 2 * tiles, :] / coarse_count - c_mean * c_mean + EPS)
    c_normed = (coarse[...].astype(F32) - as_row(c_mean, 0, tiles)) * as_row(c_scale, 0, tiles)
    coarse_act = (c_normed * sigmoid(c_normed)).astype(BF16)
    skip = dot(coarse_act, w_skip[...]).astype(BF16)
    up[...] = dot(chosen[...], skip)

    later[0].wait()

    def merge(r, sums):
        start = pl.multiple_of(r * width, width)
        up_start = pl.multiple_of((r // 4) * width, width)
        rows = (feat[pl.ds(start, width), :].astype(F32) + up[pl.ds(up_start, width), :]).astype(BF16)
        merged[pl.ds(start, width), :] = rows
        rows = rows.astype(F32)
        first, second = sums
        first = first + jnp.sum(rows.reshape(width // 8, 8, channels), axis=0)
        second = second + jnp.sum((rows * rows).reshape(width // 8, 8, channels), axis=0)
        return first, second

    zero = jnp.zeros((8, channels), F32)
    first, second = lax.fori_loop(0, tile_rows, merge, (zero, zero), unroll=True)

    def sums_tile(one, two):
        one = jnp.sum(one, axis=0, keepdims=True)
        two = jnp.sum(two, axis=0, keepdims=True)
        return jnp.concatenate(as_rows(one) + as_rows(two) + [jnp.zeros((4, LANES), F32)], axis=0)

    fine_box[sp] = sums_tile(first, second)
    to_spatial(fine_box, FINE)

    @pl.when(owner)
    def _():
        text_dp_box[dp] = text_sum[pl.ds(pl.multiple_of(8 * (dp % 2), 8), 8), :]
        receive(text_dp_box, TEXT_DP)
        pooled[...] = total(text_dp_box)
        from_owner(pooled, POOLED)

    wait_bytes(recv_sem.at[PAIR_COT], cot_chip.at[own_rows])
    turn_rows(width + other_pixels)
    receive_edges(cot, cot_edge, 0)

    @pl.when(takes_far)
    def _():
        far.wait_recv()

    @pl.when(jnp.logical_not(takes_far))
    def _():
        far_edge[...] = jnp.zeros((width, half), BF16)

    near = cot_edge[core, :, own_lanes].astype(F32)
    farther = far_edge[...].astype(F32)
    turned_shifts(jnp.where(core == 0, near, farther), cot_turned, 0)
    turned_shifts(jnp.where(core == 0, farther, near), cot_turned, width + 2 * pixels)

    receive(fine_box, FINE)
    fine_total = group_total(total(fine_box), channels // GROUPS)
    fine_count = pixels * n_sp * (channels // GROUPS)
    f_mean = fine_total[0:2, :] / fine_count
    f_scale = lax.rsqrt(fine_total[2:4, :] / fine_count - f_mean * f_mean + EPS)
    center, scale = as_row(f_mean, 0, 2), as_row(f_scale, 0, 2)

    @pl.when(jnp.logical_not(owner))
    def _():
        wait_bytes(recv_sem.at[POOLED], pooled)

    embed = time_part[...] + pooled[...] / tokens
    embed = (embed * sigmoid(embed)).astype(BF16).astype(F32)
    later[2].wait()
    embed_row = jnp.broadcast_to(as_row(embed, 0, 8), (8, 8 * LANES)).astype(BF16)
    modulation = dot(embed_row, w_mod[...])[0:1, :]
    gain = 1.0 + modulation[:, :channels]
    shift = modulation[:, channels:]

    factor = scale * gain
    term_of_hidden = shift - center * factor

    @pl.loop(0, tile_rows, unroll=True)
    def _(r):
        start = pl.multiple_of(r * width, width)
        pre = merged[pl.ds(start, width), :].astype(F32) * factor + term_of_hidden
        act = pre * sigmoid(pre)
        hidden[pl.ds(start, width), :] = act.astype(BF16)
        low, high = act[:, :half], act[:, half:]
        block = lax.shift_right_logical(iota(low.shape, 1), 5)
        even = jnp.where((block & 1) == 0, low, pltpu.roll(high, 32, 1))
        odd = jnp.where((block & 1) == 0, pltpu.roll(low, LANES - 32, 1), high)
        rows = pl.ds(pl.multiple_of(own_pixels + start, width), width)
        hidden_pair[rows, :] = jnp.concatenate([even, odd], axis=1).astype(BF16)

        @pl.when(r % 2 == 1)
        def _():
            two = pl.ds(pl.multiple_of(own_pixels + start - width, width), 2 * width)
            remote(
                hidden_pair.at[two], hidden_pair.at[two], send_sem.at[PAIR_HIDDEN], recv_sem.at[PAIR_HIDDEN], (dp, other_sp)
            ).start()

    def weight_term(dr, first_pixel):
        lanes = pl.ds(pl.multiple_of((2 - dr) * width + first_pixel, width), pixels)
        return dot(cot_turned[:, lanes], hidden_pair[pl.ds(first_pixel, pixels), :])

    for dr in range(3):
        weight_own[dr] = weight_term(dr, own_pixels)
    wait_bytes(recv_sem.at[PAIR_HIDDEN], hidden_pair.at[pl.ds(0, pixels)])
    def send_shares(their_quarter):
        dx = odd_x + their_quarter % 2 - 2 * odd_x * (their_quarter % 2)
        dz = odd_z + their_quarter // 2 - 2 * odd_z * (their_quarter // 2)
        for dy in range(2):
            their_y = odd_y + dy - 2 * odd_y * dy
            d = dx + 2 * dy + 4 * dz

            @pl.when(d > 0)
            def _():
                for side in range(2):
                    remote(
                        cube_out.at[side, their_quarter, their_y],
                        cube_box.at[side, d],
                        send_sem.at[CUBE + side],
                        recv_sem.at[CUBE + side],
                        neighbour(side, d),
                    ).start()

    for dr in (2, 1, 0):
        grads = weight_own[dr] + weight_term(dr, other_pixels)
        for dc in (2, 1, 0):
            tap = 3 * dr + dc
            grad = grads[dc * half : (dc + 1) * half, :]
            if tap < 8:
                cube_out[tap % 2, tap // 2, 0, 0:half] = grad[:, :half].astype(BF16)
                cube_out[tap % 2, tap // 2, 1, 0:half] = grad[:, half:].astype(BF16)
            else:
                turned = grad.T.astype(BF16)
                for side in range(2):
                    for number in range(8):
                        first = (number % 2) * half + block_of(number // 2) * 32 + side * 16
                        cube_out[side, number // 2, number % 2, half : half + 16] = turned[first : first + 16, :]
        for their_quarter in ((0, 1), (2,), (3,))[dr]:
            send_shares(their_quarter)

    for side in range(2):
        cube_box[side, 0] = cube_out[side, quarter, odd_y]

    start_edges(hidden, hid_edge, 2)

    @pl.loop(0, tile_rows, unroll=True)
    def _(r):
        start = pl.multiple_of(r * width, width)
        column_shifts(cot[pl.ds(start, width), :].astype(F32), cot_spread, pl.multiple_of(start + width, width), True)

    column_shifts(cot_edge[0].astype(F32), cot_spread, 0, True)
    column_shifts(cot_edge[1].astype(F32), cot_spread, pixels + width, True)
    later[3].wait()
    chunk = pixels // 2

    @pl.loop(0, 2)
    def _(c):
        start = pl.multiple_of(c * chunk, chunk)
        grad = None
        for dr in range(3):
            term = dot(
                cot_spread[pl.ds(pl.multiple_of(start + (2 - dr) * width, width), chunk), :],
                w_conv[:, 3 * dr * channels : 3 * (dr + 1) * channels],
                ((1,), (1,)),
            )
            grad = term if grad is None else grad + term
        grad_hid[pl.ds(start, chunk), :] = grad

    def backward(r, sums):
        start = pl.multiple_of(r * width, width)
        normed = (merged[pl.ds(start, width), :].astype(F32) - center) * scale
        pre = normed * gain + shift
        sigma = sigmoid(pre)
        grad = grad_hid[pl.ds(start, width), :] * sigma * (1.0 + pre * (1.0 - sigma))
        grad_hid[pl.ds(start, width), :] = grad
        first, second = sums
        first = first + jnp.sum((grad * normed).reshape(width // 8, 8, channels), axis=0)
        second = second + jnp.sum(grad.reshape(width // 8, 8, channels), axis=0)
        return first, second

    first, second = lax.fori_loop(0, tile_rows, backward, (zero, zero), unroll=True)
    back_box[sp] = sums_tile(first, second)
    to_spatial(back_box, BACK)

    sides = []
    for side in range(2):
        wait_bytes(recv_sem.at[CUBE + side], cube_box.at[side, pl.ds(1, 7)])
        summed = cube_box[side, 0].astype(F32)
        for d in range(1, 8):
            summed = summed + cube_box[side, d].astype(F32)
        sides.append(summed[0:half, :].T.reshape(16, part, half))
        tail_sum[side * 16 : (side + 1) * 16, :] = summed[half : half + 16, :]
    weight_out[...] = jnp.concatenate(sides, axis=1).astype(BF16)

    def part_of(number):
        return weight_out.at[block_of(number // 4) * 4 + number % 4]

    @pl.loop(0, 16, unroll=True)
    def _(i):
        number = lax.rem(high_y * 4 + z_high + i, 16)

        @pl.when(jnp.logical_or(i > 0, jnp.logical_not(gathers)))
        def _():
            remote(part_of(number), tile_box.at[rank], send_sem.at[TILE], recv_sem.at[TILE], gatherer(number)).start()

    for m in range(4):
        itself = jnp.logical_and(owns_tail, z_high == m)

        @pl.when(jnp.logical_not(itself))
        def _():
            remote(
                tail_sum.at[pl.ds(m * part, part)],
                tail_box.at[rank],
                send_sem.at[TAIL],
                recv_sem.at[TAIL],
                gatherer(quarter * 4 + m),
            ).start()

        @pl.when(itself)
        def _():
            tail_box[rank] = tail_sum[m * part : (m + 1) * part, :]

    @pl.when(gathers)
    def _():
        tile_box[rank] = part_of(high_y * 4 + z_high)[...]

    receive(back_box, BACK)
    back = total(back_box)
    for i in range(4):
        pair_there = lax.rem(sp - 4 * i + n_sp, n_sp)
        wanted_row = jnp.sum(jnp.where(row == pair_there // 2, embed, 0.0), axis=0, keepdims=True)
        mod_out[i] = jnp.concatenate([back[i : i + 1, :], wanted_row, jnp.zeros((6, LANES), F32)], axis=0)
        for j in range(2):
            there = 2 * pair_there + j

            @pl.when(there != dp)
            def _():
                remote(mod_out.at[i], mod_box.at[dp], send_sem.at[MOD], recv_sem.at[MOD], (there, sp)).start()

            @pl.when(there == dp)
            def _():
                mod_box[dp] = mod_out[i]

    @pl.loop(0, tile_rows, unroll=True)
    def _(r):
        start = pl.multiple_of(r * width, width)
        column_shifts(hidden[pl.ds(start, width), :].astype(F32), hid_spread, pl.multiple_of(start + width, width), False)

    for tap in range(9):
        w_stack[tap * channels : (tap + 1) * channels, :] = w_conv[:, tap * channels : (tap + 1) * channels]
    receive_edges(hidden, hid_edge, 2)
    column_shifts(hid_edge[0].astype(F32), hid_spread, 0, False)
    column_shifts(hid_edge[1].astype(F32), hid_spread, pixels + width, False)

    @pl.loop(0, 2)
    def _(c):
        start = pl.multiple_of(c * chunk, chunk)
        conv = merged[pl.ds(start, chunk), :].astype(F32)
        for dr in range(3):
            conv = conv + dot(
                hid_spread[pl.ds(pl.multiple_of(start + dr * width, width), chunk), :],
                w_stack[3 * dr * channels : 3 * (dr + 1) * channels, :],
            )
        out_ref[pl.ds(start, chunk), :] = conv.astype(BF16)

    stores = [
        pltpu.make_async_copy(source, target, store_sem.at[i])
        for i, (source, target) in enumerate(
            (
                (out_ref, out_hbm), (grad_feat_ref, grad_feat_hbm),
            )
        )
    ]
    stores[0].start()

    gain_tile = jnp.concatenate(as_rows(gain) + as_rows(gain), axis=0)
    means = group_total(back[0:4, :] * gain_tile, channels // GROUPS) / fine_count
    mean_two, mean_one = as_row(means, 0, 2), as_row(means, 2, 2)

    final_slot = 2 * quarter + core

    def to_group(rows):
        @pl.loop(1, n_sp, unroll=True)
        def _(i):
            remote(
                final_own.at[rows],
                final_hbm.at[final_slot, rows],
                send_sem.at[FINAL],
                recv_sem.at[FINAL],
                (dp, lax.rem(sp + i, n_sp)),
            ).start()

    def own_final(rows):
        return pltpu.make_async_copy(final_own.at[rows], final_hbm.at[final_slot, rows], store_sem.at[2])

    main, both = pl.ds(0, 16), pl.ds(0, 32)
    no_tail = jnp.logical_and(gathers, jnp.logical_not(owns_tail))

    @pl.when(gathers)
    def _():
        receive(tile_box, TILE)
        final_own[0:16, :] = jnp.sum(tile_box[...].astype(F32), axis=0).astype(BF16)

    @pl.when(no_tail)
    def _():
        to_group(main)
        own_final(main).start()

    @pl.when(owns_tail)
    def _():
        receive(tail_box, TAIL)
        final_own[16:32, :] = jnp.concatenate([total(tail_box), jnp.zeros((part, half), F32)], axis=0).astype(BF16)
        to_group(both)
        own_final(both).start()

    @pl.loop(0, tile_rows, unroll=True)
    def _(r):
        start = pl.multiple_of(r * width, width)
        normed = (merged[pl.ds(start, width), :].astype(F32) - center) * scale
        inner = grad_hid[pl.ds(start, width), :] * gain - mean_one - normed * mean_two
        grad_feat_ref[pl.ds(start, width), :] = (cot[pl.ds(start, width), :].astype(F32) + scale * inner).astype(BF16)

    stores[1].start()

    @pl.when(quarter_owner)
    def _():
        receive(mod_box, MOD)
        share = 8 * LANES // n_dp
        in_lanes = LANES // share
        embeds = mod_box[:, 1, :].astype(BF16)
        rest = mod_box[:, 0, :]
        grads = None
        for _ in range(3):
            piece = rest.astype(BF16)
            rest = rest - piece.astype(F32)
            term = dot(embeds, piece, ((0,), (0,)))
            grads = term if grads is None else grads + term
        mod_rows[...] = grads
        mod_start = pl.multiple_of((dp % in_lanes) * share, share)
        number = from_first // 4
        mod_own[...] = mod_rows[pl.ds(mod_start, share), :].astype(BF16)

        @pl.loop(1, n_sp, unroll=True)
        def _(i):
            there = lax.rem(sp + i, n_sp)
            remote(mod_own, mod_hbm.at[number], send_sem.at[GRAD_MOD], recv_sem.at[GRAD_MOD], (dp, there)).start()

        pltpu.make_async_copy(mod_own, mod_hbm.at[number], store_sem.at[3]).start()

    def units(count):
        return tile_box.at[pl.ds(0, count)]

    @pl.when(jnp.logical_not(gathers))
    def _():
        wait_bytes(recv_sem.at[FINAL], units(10))

    @pl.when(no_tail)
    def _():
        wait_bytes(recv_sem.at[FINAL], units(9))
        wait_bytes(send_sem.at[FINAL], units(n_sp - 1))
        wait_bytes(send_sem.at[TILE], units(15))
        own_final(main).wait()

    @pl.when(owns_tail)
    def _():
        wait_bytes(recv_sem.at[FINAL], units(8))
        wait_bytes(send_sem.at[FINAL], units(2 * (n_sp - 1)))
        wait_bytes(send_sem.at[TILE], units(15))
        own_final(both).wait()

    @pl.when(jnp.logical_not(gathers))
    def _():
        wait_bytes(send_sem.at[TILE], units(16))

    @pl.when(quarter_owner)
    def _():
        wait_bytes(recv_sem.at[GRAD_MOD], mod_hbm.at[pl.ds(0, 3)])
        pltpu.make_async_copy(mod_own, mod_hbm.at[from_first // 4], store_sem.at[3]).wait()

    @pl.when(jnp.logical_not(quarter_owner))
    def _():
        wait_bytes(recv_sem.at[GRAD_MOD], mod_hbm)

    for box, index in (
        (fine_box, FINE), (back_box, BACK), (text_box, TEXT), (coarse_box, COARSE),
    ):
        wait_bytes(send_sem.at[index], others(box))

    for side in range(2):
        wait_bytes(send_sem.at[CUBE + side], cube_box.at[side, pl.ds(1, 7)])
    sent_to_owners(text_dp_box, TEXT_DP)

    @pl.when(quarter_owner)
    def _():
        wait_bytes(send_sem.at[MOD], mod_box.at[pl.ds(0, 7)])
        wait_bytes(send_sem.at[GRAD_MOD], units(2 * (n_sp - 1)))

    @pl.when(jnp.logical_not(quarter_owner))
    def _():
        wait_bytes(send_sem.at[MOD], mod_box.at[pl.ds(0, 8)])

    @pl.when(owner)
    def _():
        wait_bytes(send_sem.at[POOLED], fine_box.at[pl.ds(0, n_sp - 1)])

    pair_cot.wait_send()
    wait_bytes(send_sem.at[PAIR_HIDDEN], hidden_pair.at[pl.ds(0, pixels)])

    @pl.when(sends_far)
    def _():
        far.wait_send()

    finish_edges(cot, cot_edge, 0)
    finish_edges(hidden, hid_edge, 2)

    @pl.when(owns_tail)
    def _():
        wait_bytes(send_sem.at[TAIL], tail_box.at[pl.ds(0, 3)])

    @pl.when(jnp.logical_not(owns_tail))
    def _():
        wait_bytes(send_sem.at[TAIL], tail_box.at[pl.ds(0, 4)])

    for store in stores:
        store.wait()


def write(
    out, grad_feat, final, mod, out_hbm, grad_feat_hbm, grad_conv_hbm, grad_mod_hbm,
    out_room, grad_feat_room, final_room, mod_room, grad_conv, grad_mod, load_sem, store_sem,
):
    fetch_final = pltpu.make_async_copy(final, final_room, load_sem.at[4])
    fetch_mod = pltpu.make_async_copy(mod, mod_room, load_sem.at[5])
    fetch_final.start()
    fetch_mod.start()
    moves = []
    for source, room, target in ((out, out_room, out_hbm), (grad_feat, grad_feat_room, grad_feat_hbm)):
        rows = source.shape[0] // 2
        for i in range(2):
            piece = pl.ds(i * rows, rows)
            number = len(moves)
            moves.append(
                (
                    pltpu.make_async_copy(source.at[piece], room.at[piece], load_sem.at[number]),
                    pltpu.make_async_copy(room.at[piece], target.at[piece], store_sem.at[number]),
                )
            )
    for fetch, _ in moves:
        fetch.start()
    fetch_final.wait()
    parts = final_room[...].astype(F32)
    tail_quarter = lax.axis_index("dp") // 8
    columns = [
        parts[2 * (tap // 2) + side, 8 * (tap % 2) : 8 * (tap % 2) + 8, :] for tap in range(8) for side in range(2)
    ] + [final_room[2 * tail_quarter + side].astype(F32)[16:24, :] for side in range(2)]
    grad_conv[...] = jnp.concatenate(columns, axis=1).astype(BF16)
    fetch_mod.wait()
    grad_mod[...] = jnp.concatenate([mod_room[i] for i in range(4)], axis=1)
    last = [
        pltpu.make_async_copy(grad_conv, grad_conv_hbm, store_sem.at[4]),
        pltpu.make_async_copy(grad_mod, grad_mod_hbm, store_sem.at[5]),
    ]
    for store in last:
        store.start()
    for fetch, store in moves:
        fetch.wait()
        store.start()
    for _, store in moves:
        store.wait()
    for store in last:
        store.wait()


def body(n_dp, n_sp, features, coarse, timestep, text_ids, text_table, w_mod, w_skip, w_conv, cotangent):
    _, tile_rows, width, channels = features.shape
    pixels = tile_rows * width
    cells = coarse.shape[1] * coarse.shape[2]
    coarse_width = coarse.shape[3]
    part, half = channels // n_dp, channels // 2
    taps = w_conv.shape[1] // channels
    vm = pltpu.VMEM
    tile = (8, LANES)
    anywhere = pl.BlockSpec(memory_space=pl.ANY)
    mod_rows = w_mod.shape[0] // n_dp
    scratch = [
        vm((pixels, channels), BF16),
        vm((pixels, channels), BF16),
        vm(text_ids.shape, jnp.int32),
        vm((pixels, channels), BF16),
        vm((cells, coarse_width), BF16),
        vm(text_table.shape, BF16),
        vm(w_mod.shape, BF16),
        vm(w_skip.shape, BF16),
        vm(w_conv.shape, BF16),
        vm((taps * channels, channels), BF16),
        vm((pixels, channels), BF16),
        vm((2, width, channels), BF16),
        vm((width, half), BF16),
        vm((2, width, channels), BF16),
        vm((pixels, half), BF16),
        vm((2 * pixels + 2 * width, half), BF16),
        vm((pixels + 2 * width, 3 * channels), BF16),
        vm((3 * half, 2 * pixels + 2 * width), BF16),
        vm((pixels + 2 * width, 3 * channels), BF16),
        vm((4 * cells, cells), BF16),
        vm((4 * cells, channels), F32),
        vm((pixels, channels), BF16),
        vm((pixels, channels), BF16),
        vm((2 * pixels, channels), BF16),
        vm((pixels, channels), F32),
        vm((n_sp,) + tile, F32),
        vm((n_sp,) + tile, F32),
        vm((n_sp,) + tile, F32),
        vm((n_sp, 16, LANES), F32),
        vm((n_sp, 16, LANES), BF16),
        vm((n_sp, 16, LANES), BF16),
        vm((16, LANES), F32),
        vm((n_dp,) + tile, F32),
        vm(tile, F32),
        vm(tile, F32),
        vm((4,) + tile, F32),
        vm((n_dp,) + tile, F32),
        vm((LANES, LANES), F32),
        vm((mod_rows, LANES), BF16),
        vm((3, 3 * half, channels), F32),
        vm((2, 4, 2, half + 16, half), BF16),
        vm((2, 8, half + 16, half), BF16),
        vm((16, 2 * part, half), BF16),
        vm((32, half), F32),
        vm((n_dp, 2 * part, half), BF16),
        vm((n_dp, part, half), F32),
        vm((32, half), BF16),
        pltpu.SemaphoreType.DMA((8,)),
        pltpu.SemaphoreType.DMA((4,)),
        pltpu.SemaphoreType.DMA((4,)),
        pltpu.SemaphoreType.DMA((4,)),
        pltpu.SemaphoreType.DMA((16,)),
        pltpu.SemaphoreType.DMA((16,)),
    ]
    shapes = (
        jax.ShapeDtypeStruct((pixels, channels), BF16),
        jax.ShapeDtypeStruct((pixels, channels), BF16),
        jax.ShapeDtypeStruct((8, 32, half), BF16),
        jax.ShapeDtypeStruct((4, mod_rows, LANES), BF16),
    )
    written = shapes[:2] + (
        jax.ShapeDtypeStruct((part, taps * channels), BF16),
        jax.ShapeDtypeStruct((mod_rows, 2 * channels), BF16),
    )
    results = pl.pallas_call(
        functools.partial(kernel, n_dp, n_sp, tile_rows, width),
        out_shape=shapes,
        in_specs=[pl.BlockSpec(memory_space=pltpu.SMEM)] + [anywhere] * 8,
        out_specs=(anywhere,) * 4,
        scratch_shapes=scratch,
        compiler_params=pltpu.CompilerParams(
            collective_id=0, has_side_effects=True, vmem_limit_bytes=VMEM_LIMIT
        ),
    )(
        timestep,
        text_ids,
        features.reshape(pixels, channels),
        coarse.reshape(cells, coarse_width),
        text_table,
        w_mod,
        w_skip,
        w_conv,
        cotangent.reshape(pixels, channels),
    )
    output, grad_features, grad_conv, grad_mod = pl.pallas_call(
        write,
        out_shape=written,
        in_specs=[anywhere] * 4,
        out_specs=(anywhere,) * 4,
        scratch_shapes=[vm(shape.shape, shape.dtype) for shape in shapes + written[2:]]
        + [pltpu.SemaphoreType.DMA((6,)), pltpu.SemaphoreType.DMA((6,))],
        compiler_params=pltpu.CompilerParams(vmem_limit_bytes=VMEM_LIMIT),
    )(*results)
    return output.reshape(features.shape), grad_features.reshape(features.shape), grad_conv, grad_mod


def solution(mesh):
    in_specs = (
        P("dp", "spatial", None, None),
        P("dp", "spatial", None, None),
        P("dp"),
        P(),
        P(("dp", "spatial"), None),
        P(),
        P(),
        P(),
        P("dp", "spatial", None, None),
    )
    out_specs = (
        P("dp", "spatial", None, None),
        P("dp", "spatial", None, None),
        P("dp", None),
        P("dp", None),
    )
    step = functools.partial(body, mesh.shape["dp"], mesh.shape["spatial"])
    return jax.shard_map(step, mesh=mesh, in_specs=in_specs, out_specs=out_specs, check_vma=False)
```

```python
import functools
import math

import jax
import jax.numpy as jnp
from jax import lax
from jax.experimental import pallas as pl
from jax.experimental.pallas import tpu as pltpu
from jax.sharding import PartitionSpec as P

GROUPS = 32
EPS = 1e-05
MESH = pl.DeviceIdType.MESH
F32 = jnp.float32
BF16 = jnp.bfloat16
LANES = 128
VMEM_LIMIT = 62 * 1024 * 1024


def dot(a, b, dims=((1,), (0,))):
    return lax.dot_general(a, b, (dims, ((), ())), preferred_element_type=F32)


def iota(shape, axis):
    return lax.broadcasted_iota(jnp.int32, shape, axis)


def sigmoid(x):
    return 0.5 * jnp.tanh(0.5 * x) + 0.5


def group_total(tile, width):
    lane = iota(tile.shape, 1)
    step = 1
    while step < width:
        partner = jnp.where(
            (lane & step) != 0, pltpu.roll(tile, step, 1), pltpu.roll(tile, LANES - step, 1)
        )
        tile = tile + partner
        step *= 2
    return tile


def as_row(tile, first, count):
    return jnp.concatenate([tile[first + i : first + i + 1, :] for i in range(count)], axis=1)


def as_rows(row):
    return [row[:, i * LANES : (i + 1) * LANES] for i in range(row.shape[1] // LANES)]


def column_shifts(rows, spread_ref, first_row, reverse):
    width, channels = rows.shape
    column = iota(rows.shape, 0)
    earlier = jnp.where(column == 0, 0.0, pltpu.roll(rows, 1, 0)).astype(BF16)
    later = jnp.where(column == width - 1, 0.0, pltpu.roll(rows, width - 1, 0)).astype(BF16)
    left, right = (later, earlier) if reverse else (earlier, later)
    spread_ref[pl.ds(first_row, width), 0:channels] = left
    spread_ref[pl.ds(first_row, width), channels : 2 * channels] = rows.astype(BF16)
    spread_ref[pl.ds(first_row, width), 2 * channels : 3 * channels] = right


def turned_shifts(rows, turned_ref, first_pixel):
    width, channels = rows.shape
    turned = rows.T
    column = iota(turned.shape, 1)
    later = jnp.where(column == width - 1, 0.0, pltpu.roll(turned, width - 1, 1))
    earlier = jnp.where(column == 0, 0.0, pltpu.roll(turned, 1, 1))
    for i, shifted in enumerate((later, turned, earlier)):
        turned_ref[i * channels : (i + 1) * channels, pl.ds(first_pixel, width)] = shifted.astype(BF16)


def kernel(n_dp, n_sp, tile_rows, width, *refs):
    (
        time_ref, ids_hbm, feat_hbm, coarse_hbm, table_hbm, w_mod_hbm, w_skip_hbm, w_conv_hbm, cot_hbm,
        out_hbm, grad_feat_hbm, final_hbm, mod_hbm,
        out_ref, grad_feat_ref, ids_ref,
        feat, coarse, table, w_mod, w_skip, w_conv, w_stack, cot,
        cot_edge, far_edge, hid_edge, cot_half, cot_chip, cot_spread, cot_turned, hid_spread, chosen, up, merged,
        hidden, hidden_pair, grad_hid,
        coarse_box, fine_box, back_box, text_rows, text_out, text_box, text_sum, text_dp_box, pooled, time_part,
        mod_out, mod_box, mod_rows, mod_own, weight_own, cube_out, cube_box, weight_out, tail_sum,
        tile_box, tail_box, final_own,
        load_sem, store_sem, edge_send, edge_recv, send_sem, recv_sem,
    ) = refs
    channels = feat.shape[1]
    pixels = tile_rows * width
    half = channels // 2
    part = channels // n_dp
    dp = lax.axis_index("dp")
    sp = lax.axis_index("spatial")
    chip, core = sp // 2, sp % 2
    other_sp = sp + 1 - 2 * core

    y, z_high = dp // 4, dp % 4
    z_low, x = sp // 8, chip % 4
    z = 2 * z_high + z_low
    odd_x, odd_y, odd_z = x % 2, y % 2, z_low
    high_x, high_y = x // 2, y // 2
    quarter = 2 * odd_z + odd_x
    rank = high_x * 16 + high_y * 4 + z_high

    def block_of(high):
        return 2 * (high % 2) + high // 2

    def neighbour(side, d):
        dx, dy, dz = d % 2, (d // 2) % 2, d // 4
        x_there = (x + dx * (1 - 2 * odd_x) * (1 - 2 * side) + 4) % 4
        y_there = (y + dy * (1 - 2 * odd_y) * (1 - 2 * side) + 8) % 8
        z_there = (z + dz * (1 - 2 * odd_z) * (1 - 2 * side) + 8) % 8
        return (y_there * 4 + z_there // 2, (z_there % 2) * 8 + x_there * 2 + core)

    def gatherer(number):
        y_there, z_there = number // 4, number % 4
        return ((2 * y_there + odd_y) * 4 + z_there, z_low * 8 + (2 * (z_there % 2) + odd_x) * 2 + core)

    gathers = high_x == z_high % 2
    owns_tail = jnp.logical_and(gathers, high_y == quarter)
    owner = dp // 2 == sp
    from_first = lax.rem(sp - dp // 2 + n_sp, n_sp)
    quarter_owner = from_first % 4 == 0
    (
        COARSE, FINE, BACK, TEXT, TEXT_DP, POOLED, MOD, GRAD_MOD, TILE, TAIL, FINAL,
        PAIR_COT, PAIR_HIDDEN, FAR, CUBE,
    ) = range(15)

    def load(source, target, index):
        return pltpu.make_async_copy(source, target, load_sem.at[index])

    own_lanes = pl.ds(pl.multiple_of(core * half, half), half)
    other_lanes = pl.ds(pl.multiple_of((1 - core) * half, half), half)
    own_pixels = pl.multiple_of(core * pixels, pixels)
    other_pixels = pl.multiple_of((1 - core) * pixels, pixels)
    own_rows = pl.ds(pl.multiple_of(width + core * pixels, width), pixels)
    loads = [
        load(ids_hbm, ids_ref, 1),
        load(table_hbm, table, 2),
        load(coarse_hbm, coarse, 0),
        load(cot_hbm, cot, 3),
    ]
    later = [
        load(feat_hbm, feat, 4),
        load(w_skip_hbm, w_skip, 5),
        load(w_mod_hbm, w_mod, 6),
        load(w_conv_hbm, w_conv, 7),
    ]
    for copy in loads[:2]:
        copy.start()

    barrier = pltpu.get_barrier_semaphore()

    def greet(place):
        pl.semaphore_signal(barrier, inc=1, device_id=place, device_id_type=MESH)

    @pl.when(owner)
    def _():
        @pl.loop(1, n_dp)
        def _(i):
            greet((lax.rem(dp + i, n_dp), sp))

    @pl.loop(1, n_sp, unroll=True)
    def _(i):
        greet((dp, lax.rem(sp + i, n_sp)))

    for copy in loads[2:] + later:
        copy.start()

    def remote(source, target, send, recv, place):
        return pltpu.make_async_remote_copy(
            src_ref=source, dst_ref=target, send_sem=send, recv_sem=recv, device_id=place, device_id_type=MESH
        )

    def wait_bytes(sem, ref):
        pltpu.make_async_copy(ref, ref, sem).wait()

    def to_spatial(box, index):
        @pl.loop(1, n_sp, unroll=True)
        def _(i):
            there = lax.rem(sp + i, n_sp)
            remote(box.at[sp], box.at[sp], send_sem.at[index], recv_sem.at[index], (dp, there)).start()

    def to_owners(source_of, box, index):
        for j in range(2):
            there = 2 * sp + j

            @pl.when(there != dp)
            def _():
                remote(source_of(j), box.at[dp], send_sem.at[index], recv_sem.at[index], (there, sp)).start()

    def sent_to_owners(box, index):
        @pl.when(owner)
        def _():
            wait_bytes(send_sem.at[index], box.at[pl.ds(0, 1)])

        @pl.when(jnp.logical_not(owner))
        def _():
            wait_bytes(send_sem.at[index], box.at[pl.ds(0, 2)])

    def from_owner(ref, index):
        @pl.loop(1, n_sp, unroll=True)
        def _(i):
            there = lax.rem(sp + i, n_sp)
            remote(ref, ref, send_sem.at[index], recv_sem.at[index], (dp, there)).start()

    def others(box):
        return box.at[pl.ds(0, box.shape[0] - 1)]

    def receive(box, index):
        wait_bytes(recv_sem.at[index], others(box))

    def total(box):
        return jnp.sum(box[...], axis=0)

    vocab = table.shape[0]
    batch, tokens = ids_ref.shape
    loads[0].wait()
    local_ids = jnp.concatenate(
        [ids_ref[pl.ds(j, n_sp, stride=2), :] for j in range(2)], axis=0
    ) - (dp * n_sp + sp) * vocab
    turned_ids = local_ids.astype(F32).T
    quarters = jnp.concatenate([turned_ids] * 4, axis=1) - 16.0 * lax.shift_right_logical(
        iota((tokens, LANES), 1), 5
    ).astype(F32)
    found = [
        jnp.sum(jnp.where(quarters == float(k), 1.0, 0.0), axis=0, keepdims=True) for k in range(16)
    ]
    found = jnp.concatenate(found, axis=0)
    counts = jnp.concatenate([found[:, q * batch : (q + 1) * batch] for q in range(4)], axis=0)[:vocab].astype(BF16)
    loads[1].wait()
    partial = dot(counts, table[...], ((0,), (0,)))
    for i in range(8):
        for j in range(2):
            text_rows[:, 8 * j + i, :] = partial[j * n_sp : (j + 1) * n_sp, i * LANES : (i + 1) * LANES]
    text_out[...] = text_rows[...].astype(BF16)

    loads[2].wait()
    coarse_f = coarse[...].astype(F32)
    coarse_box[sp] = jnp.concatenate(
        as_rows(jnp.sum(coarse_f, axis=0, keepdims=True))
        + as_rows(jnp.sum(coarse_f * coarse_f, axis=0, keepdims=True)),
        axis=0,
    )

    pl.semaphore_wait(barrier, jnp.where(owner, n_sp, n_sp + 1))

    @pl.loop(1, n_sp, unroll=True)
    def _(i):
        there = lax.rem(sp + i, n_sp)
        remote(text_out.at[there], text_box.at[sp], send_sem.at[TEXT], recv_sem.at[TEXT], (dp, there)).start()

    text_box[sp] = text_out[sp]
    to_spatial(coarse_box, COARSE)

    last = pixels - width

    def edges(source, target, first):
        down = remote(
            source.at[pl.ds(last, width)], target.at[0], edge_send.at[first], edge_recv.at[first], (dp, sp + 1)
        )
        upward = remote(
            source.at[pl.ds(0, width)], target.at[1], edge_send.at[first + 1], edge_recv.at[first + 1], (dp, sp - 1)
        )
        return down, upward

    def start_edges(source, target, first):
        down, upward = edges(source, target, first)

        @pl.when(sp < n_sp - 1)
        def _():
            down.start()

        @pl.when(sp > 0)
        def _():
            upward.start()

    def receive_edges(source, target, first):
        down, upward = edges(source, target, first)

        @pl.when(sp > 0)
        def _():
            down.wait_recv()

        @pl.when(sp < n_sp - 1)
        def _():
            upward.wait_recv()

        @pl.when(sp == 0)
        def _():
            target[0] = jnp.zeros((width, channels), BF16)

        @pl.when(sp == n_sp - 1)
        def _():
            target[1] = jnp.zeros((width, channels), BF16)

    def finish_edges(source, target, first):
        down, upward = edges(source, target, first)

        @pl.when(sp < n_sp - 1)
        def _():
            down.wait_send()

        @pl.when(sp > 0)
        def _():
            upward.wait_send()

    loads[3].wait()
    start_edges(cot, cot_edge, 0)
    cot_half[...] = cot[:, other_lanes]
    cot_chip[own_rows, :] = cot[:, own_lanes]
    pair_cot = remote(
        cot_half, cot_chip.at[own_rows], send_sem.at[PAIR_COT], recv_sem.at[PAIR_COT], (dp, other_sp)
    )
    pair_cot.start()
    far = remote(
        cot_chip.at[pl.ds(pl.multiple_of(width + core * (pixels + last), width), width)],
        far_edge,
        send_sem.at[FAR],
        recv_sem.at[FAR],
        (dp, sp - 2 + 4 * core),
    )
    chips = n_sp // 2
    sends_far = jnp.logical_or(jnp.logical_and(core == 0, chip > 0), jnp.logical_and(core == 1, chip < chips - 1))
    takes_far = jnp.logical_or(jnp.logical_and(core == 0, chip < chips - 1), jnp.logical_and(core == 1, chip > 0))

    @pl.when(sends_far)
    def _():
        far.start()

    row, lane = iota((8, LANES), 0), iota((8, LANES), 1)
    half_width = 4 * LANES
    index = ((row & 3) * LANES + lane).astype(F32)
    angle = time_ref[0].astype(F32) * jnp.exp(-math.log(10000.0) * index / half_width)
    time_part[...] = jnp.where(row < 4, jnp.sin(angle), jnp.cos(angle))

    shape = chosen.shape
    coarse_cols = width // 4
    place = iota(shape, 0)
    wanted = lax.shift_right_logical(place, width.bit_length() - 1) * coarse_cols + (
        lax.shift_right_logical(place & (width - 1), 2)
    )
    chosen[...] = (wanted == iota(shape, 1)).astype(F32).astype(BF16)

    def turn_rows(first_row):
        @pl.loop(0, tile_rows, unroll=True)
        def _(r):
            start = pl.multiple_of(first_row + r * width, width)
            turned_shifts(cot_chip[pl.ds(start, width), :].astype(F32), cot_turned, start)

    receive(text_box, TEXT)
    text_sum[...] = jnp.sum(text_box[...].astype(F32), axis=0)
    to_owners(lambda j: text_sum.at[pl.ds(8 * j, 8)], text_dp_box, TEXT_DP)

    later[1].wait()
    receive(coarse_box, COARSE)
    coarse_total = group_total(total(coarse_box), coarse.shape[1] // GROUPS)
    coarse_count = coarse.shape[0] * n_sp * (coarse.shape[1] // GROUPS)
    tiles = coarse.shape[1] // LANES
    c_mean = coarse_total[0:tiles, :] / coarse_count
    c_scale = lax.rsqrt(coarse_total[tiles : 2 * tiles, :] / coarse_count - c_mean * c_mean + EPS)
    c_normed = (coarse[...].astype(F32) - as_row(c_mean, 0, tiles)) * as_row(c_scale, 0, tiles)
    coarse_act = (c_normed * sigmoid(c_normed)).astype(BF16)
    skip = dot(coarse_act, w_skip[...]).astype(BF16)
    up[...] = dot(chosen[...], skip)

    later[0].wait()

    def merge(r, sums):
        start = pl.multiple_of(r * width, width)
        up_start = pl.multiple_of((r // 4) * width, width)
        rows = (feat[pl.ds(start, width), :].astype(F32) + up[pl.ds(up_start, width), :]).astype(BF16)
        merged[pl.ds(start, width), :] = rows
        rows = rows.astype(F32)
        first, second = sums
        first = first + jnp.sum(rows.reshape(width // 8, 8, channels), axis=0)
        second = second + jnp.sum((rows * rows).reshape(width // 8, 8, channels), axis=0)
        return first, second

    zero = jnp.zeros((8, channels), F32)
    first, second = lax.fori_loop(0, tile_rows, merge, (zero, zero), unroll=True)

    def sums_tile(one, two):
        one = jnp.sum(one, axis=0, keepdims=True)
        two = jnp.sum(two, axis=0, keepdims=True)
        return jnp.concatenate(as_rows(one) + as_rows(two) + [jnp.zeros((4, LANES), F32)], axis=0)

    fine_box[sp] = sums_tile(first, second)
    to_spatial(fine_box, FINE)

    @pl.when(owner)
    def _():
        text_dp_box[dp] = text_sum[pl.ds(pl.multiple_of(8 * (dp % 2), 8), 8), :]
        receive(text_dp_box, TEXT_DP)
        pooled[...] = total(text_dp_box)
        from_owner(pooled, POOLED)

    turn_rows(width + own_pixels)
    wait_bytes(recv_sem.at[PAIR_COT], cot_chip.at[own_rows])
    turn_rows(width + other_pixels)
    receive_edges(cot, cot_edge, 0)

    @pl.when(takes_far)
    def _():
        far.wait_recv()

    @pl.when(jnp.logical_not(takes_far))
    def _():
        far_edge[...] = jnp.zeros((width, half), BF16)

    near = cot_edge[core, :, own_lanes].astype(F32)
    farther = far_edge[...].astype(F32)
    turned_shifts(jnp.where(core == 0, near, farther), cot_turned, 0)
    turned_shifts(jnp.where(core == 0, farther, near), cot_turned, width + 2 * pixels)

    receive(fine_box, FINE)
    fine_total = group_total(total(fine_box), channels // GROUPS)
    fine_count = pixels * n_sp * (channels // GROUPS)
    f_mean = fine_total[0:2, :] / fine_count
    f_scale = lax.rsqrt(fine_total[2:4, :] / fine_count - f_mean * f_mean + EPS)
    center, scale = as_row(f_mean, 0, 2), as_row(f_scale, 0, 2)

    @pl.when(jnp.logical_not(owner))
    def _():
        wait_bytes(recv_sem.at[POOLED], pooled)

    embed = time_part[...] + pooled[...] / tokens
    embed = (embed * sigmoid(embed)).astype(BF16).astype(F32)
    later[2].wait()
    embed_row = jnp.broadcast_to(as_row(embed, 0, 8), (8, 8 * LANES)).astype(BF16)
    modulation = dot(embed_row, w_mod[...])[0:1, :]
    gain = 1.0 + modulation[:, :channels]
    shift = modulation[:, channels:]

    factor = scale * gain
    term_of_hidden = shift - center * factor

    @pl.loop(0, tile_rows, unroll=True)
    def _(r):
        start = pl.multiple_of(r * width, width)
        pre = merged[pl.ds(start, width), :].astype(F32) * factor + term_of_hidden
        act = pre * sigmoid(pre)
        hidden[pl.ds(start, width), :] = act.astype(BF16)
        low, high = act[:, :half], act[:, half:]
        block = lax.shift_right_logical(iota(low.shape, 1), 5)
        even = jnp.where((block & 1) == 0, low, pltpu.roll(high, 32, 1))
        odd = jnp.where((block & 1) == 0, pltpu.roll(low, LANES - 32, 1), high)
        rows = pl.ds(pl.multiple_of(own_pixels + start, width), width)
        hidden_pair[rows, :] = jnp.concatenate([even, odd], axis=1).astype(BF16)

        @pl.when(r % 2 == 1)
        def _():
            two = pl.ds(pl.multiple_of(own_pixels + start - width, width), 2 * width)
            remote(
                hidden_pair.at[two], hidden_pair.at[two], send_sem.at[PAIR_HIDDEN], recv_sem.at[PAIR_HIDDEN], (dp, other_sp)
            ).start()

    def weight_term(dr, first_pixel):
        lanes = pl.ds(pl.multiple_of((2 - dr) * width + first_pixel, width), pixels)
        return dot(cot_turned[:, lanes], hidden_pair[pl.ds(first_pixel, pixels), :])

    for dr in range(3):
        weight_own[dr] = weight_term(dr, own_pixels)
    wait_bytes(recv_sem.at[PAIR_HIDDEN], hidden_pair.at[pl.ds(0, pixels)])
    def send_shares(their_quarter):
        dx = odd_x + their_quarter % 2 - 2 * odd_x * (their_quarter % 2)
        dz = odd_z + their_quarter // 2 - 2 * odd_z * (their_quarter // 2)
        for dy in range(2):
            their_y = odd_y + dy - 2 * odd_y * dy
            d = dx + 2 * dy + 4 * dz

            @pl.when(d > 0)
            def _():
                for side in range(2):
                    remote(
                        cube_out.at[side, their_quarter, their_y],
                        cube_box.at[side, d],
                        send_sem.at[CUBE + side],
                        recv_sem.at[CUBE + side],
                        neighbour(side, d),
                    ).start()

    for dr in (2, 1, 0):
        grads = weight_own[dr] + weight_term(dr, other_pixels)
        for dc in (2, 1, 0):
            tap = 3 * dr + dc
            grad = grads[dc * half : (dc + 1) * half, :]
            if tap < 8:
                cube_out[tap % 2, tap // 2, 0, 0:half] = grad[:, :half].astype(BF16)
                cube_out[tap % 2, tap // 2, 1, 0:half] = grad[:, half:].astype(BF16)
            else:
                turned = grad.T.astype(BF16)
                for side in range(2):
                    for number in range(8):
                        first = (number % 2) * half + block_of(number // 2) * 32 + side * 16
                        cube_out[side, number // 2, number % 2, half : half + 16] = turned[first : first + 16, :]
        for their_quarter in ((0, 1), (2,), (3,))[dr]:
            send_shares(their_quarter)

    for side in range(2):
        cube_box[side, 0] = cube_out[side, quarter, odd_y]

    start_edges(hidden, hid_edge, 2)

    @pl.loop(0, tile_rows, unroll=True)
    def _(r):
        start = pl.multiple_of(r * width, width)
        column_shifts(cot[pl.ds(start, width), :].astype(F32), cot_spread, pl.multiple_of(start + width, width), True)

    column_shifts(cot_edge[0].astype(F32), cot_spread, 0, True)
    column_shifts(cot_edge[1].astype(F32), cot_spread, pixels + width, True)
    later[3].wait()
    chunk = pixels // 2

    @pl.loop(0, 2)
    def _(c):
        start = pl.multiple_of(c * chunk, chunk)
        grad = None
        for dr in range(3):
            term = dot(
                cot_spread[pl.ds(pl.multiple_of(start + (2 - dr) * width, width), chunk), :],
                w_conv[:, 3 * dr * channels : 3 * (dr + 1) * channels],
                ((1,), (1,)),
            )
            grad = term if grad is None else grad + term
        grad_hid[pl.ds(start, chunk), :] = grad

    def backward(r, sums):
        start = pl.multiple_of(r * width, width)
        normed = (merged[pl.ds(start, width), :].astype(F32) - center) * scale
        pre = normed * gain + shift
        sigma = sigmoid(pre)
        grad = grad_hid[pl.ds(start, width), :] * sigma * (1.0 + pre * (1.0 - sigma))
        grad_hid[pl.ds(start, width), :] = grad
        first, second = sums
        first = first + jnp.sum((grad * normed).reshape(width // 8, 8, channels), axis=0)
        second = second + jnp.sum(grad.reshape(width // 8, 8, channels), axis=0)
        return first, second

    first, second = lax.fori_loop(0, tile_rows, backward, (zero, zero), unroll=True)
    back_box[sp] = sums_tile(first, second)
    to_spatial(back_box, BACK)

    sides = []
    for side in range(2):
        wait_bytes(recv_sem.at[CUBE + side], cube_box.at[side, pl.ds(1, 7)])
        summed = cube_box[side, 0].astype(F32)
        for d in range(1, 8):
            summed = summed + cube_box[side, d].astype(F32)
        sides.append(summed[0:half, :].T.reshape(16, part, half))
        tail_sum[side * 16 : (side + 1) * 16, :] = summed[half : half + 16, :]
    weight_out[...] = jnp.concatenate(sides, axis=1).astype(BF16)

    def part_of(number):
        return weight_out.at[block_of(number // 4) * 4 + number % 4]

    @pl.loop(0, 16, unroll=True)
    def _(i):
        number = lax.rem(high_y * 4 + z_high + i, 16)

        @pl.when(jnp.logical_or(i > 0, jnp.logical_not(gathers)))
        def _():
            remote(part_of(number), tile_box.at[rank], send_sem.at[TILE], recv_sem.at[TILE], gatherer(number)).start()

    for m in range(4):
        itself = jnp.logical_and(owns_tail, z_high == m)

        @pl.when(jnp.logical_not(itself))
        def _():
            remote(
                tail_sum.at[pl.ds(m * part, part)],
                tail_box.at[rank],
                send_sem.at[TAIL],
                recv_sem.at[TAIL],
                gatherer(quarter * 4 + m),
            ).start()

        @pl.when(itself)
        def _():
            tail_box[rank] = tail_sum[m * part : (m + 1) * part, :]

    @pl.when(gathers)
    def _():
        tile_box[rank] = part_of(high_y * 4 + z_high)[...]

    receive(back_box, BACK)
    back = total(back_box)
    for i in range(4):
        pair_there = lax.rem(sp - 4 * i + n_sp, n_sp)
        wanted_row = jnp.sum(jnp.where(row == pair_there // 2, embed, 0.0), axis=0, keepdims=True)
        mod_out[i] = jnp.concatenate([back[i : i + 1, :], wanted_row, jnp.zeros((6, LANES), F32)], axis=0)
        for j in range(2):
            there = 2 * pair_there + j

            @pl.when(there != dp)
            def _():
                remote(mod_out.at[i], mod_box.at[dp], send_sem.at[MOD], recv_sem.at[MOD], (there, sp)).start()

            @pl.when(there == dp)
            def _():
                mod_box[dp] = mod_out[i]

    @pl.loop(0, tile_rows, unroll=True)
    def _(r):
        start = pl.multiple_of(r * width, width)
        column_shifts(hidden[pl.ds(start, width), :].astype(F32), hid_spread, pl.multiple_of(start + width, width), False)

    for tap in range(9):
        w_stack[tap * channels : (tap + 1) * channels, :] = w_conv[:, tap * channels : (tap + 1) * channels]
    receive_edges(hidden, hid_edge, 2)
    column_shifts(hid_edge[0].astype(F32), hid_spread, 0, False)
    column_shifts(hid_edge[1].astype(F32), hid_spread, pixels + width, False)

    @pl.loop(0, 2)
    def _(c):
        start = pl.multiple_of(c * chunk, chunk)
        conv = merged[pl.ds(start, chunk), :].astype(F32)
        for dr in range(3):
            conv = conv + dot(
                hid_spread[pl.ds(pl.multiple_of(start + dr * width, width), chunk), :],
                w_stack[3 * dr * channels : 3 * (dr + 1) * channels, :],
            )
        out_ref[pl.ds(start, chunk), :] = conv.astype(BF16)

    stores = [
        pltpu.make_async_copy(source, target, store_sem.at[i])
        for i, (source, target) in enumerate(
            (
                (out_ref, out_hbm), (grad_feat_ref, grad_feat_hbm),
            )
        )
    ]
    stores[0].start()

    gain_tile = jnp.concatenate(as_rows(gain) + as_rows(gain), axis=0)
    means = group_total(back[0:4, :] * gain_tile, channels // GROUPS) / fine_count
    mean_two, mean_one = as_row(means, 0, 2), as_row(means, 2, 2)

    final_slot = 2 * quarter + core

    def to_group(rows):
        @pl.loop(1, n_sp, unroll=True)
        def _(i):
            remote(
                final_own.at[rows],
                final_hbm.at[final_slot, rows],
                send_sem.at[FINAL],
                recv_sem.at[FINAL],
                (dp, lax.rem(sp + i, n_sp)),
            ).start()

    def own_final(rows):
        return pltpu.make_async_copy(final_own.at[rows], final_hbm.at[final_slot, rows], store_sem.at[2])

    main, both = pl.ds(0, 16), pl.ds(0, 32)
    no_tail = jnp.logical_and(gathers, jnp.logical_not(owns_tail))

    @pl.when(gathers)
    def _():
        receive(tile_box, TILE)
        final_own[0:16, :] = jnp.sum(tile_box[...].astype(F32), axis=0).astype(BF16)

    @pl.when(no_tail)
    def _():
        to_group(main)
        own_final(main).start()

    @pl.when(owns_tail)
    def _():
        receive(tail_box, TAIL)
        final_own[16:32, :] = jnp.concatenate([total(tail_box), jnp.zeros((part, half), F32)], axis=0).astype(BF16)
        to_group(both)
        own_final(both).start()

    @pl.loop(0, tile_rows, unroll=True)
    def _(r):
        start = pl.multiple_of(r * width, width)
        normed = (merged[pl.ds(start, width), :].astype(F32) - center) * scale
        inner = grad_hid[pl.ds(start, width), :] * gain - mean_one - normed * mean_two
        grad_feat_ref[pl.ds(start, width), :] = (cot[pl.ds(start, width), :].astype(F32) + scale * inner).astype(BF16)

    stores[1].start()

    @pl.when(quarter_owner)
    def _():
        receive(mod_box, MOD)
        share = 8 * LANES // n_dp
        in_lanes = LANES // share
        embeds = mod_box[:, 1, :].astype(BF16)
        rest = mod_box[:, 0, :]
        grads = None
        for _ in range(3):
            piece = rest.astype(BF16)
            rest = rest - piece.astype(F32)
            term = dot(embeds, piece, ((0,), (0,)))
            grads = term if grads is None else grads + term
        mod_rows[...] = grads
        mod_start = pl.multiple_of((dp % in_lanes) * share, share)
        number = from_first // 4
        mod_own[...] = mod_rows[pl.ds(mod_start, share), :].astype(BF16)

        @pl.loop(1, n_sp, unroll=True)
        def _(i):
            there = lax.rem(sp + i, n_sp)
            remote(mod_own, mod_hbm.at[number], send_sem.at[GRAD_MOD], recv_sem.at[GRAD_MOD], (dp, there)).start()

        pltpu.make_async_copy(mod_own, mod_hbm.at[number], store_sem.at[3]).start()

    def units(count):
        return tile_box.at[pl.ds(0, count)]

    @pl.when(jnp.logical_not(gathers))
    def _():
        wait_bytes(recv_sem.at[FINAL], units(10))

    @pl.when(no_tail)
    def _():
        wait_bytes(recv_sem.at[FINAL], units(9))
        wait_bytes(send_sem.at[FINAL], units(n_sp - 1))
        wait_bytes(send_sem.at[TILE], units(15))
        own_final(main).wait()

    @pl.when(owns_tail)
    def _():
        wait_bytes(recv_sem.at[FINAL], units(8))
        wait_bytes(send_sem.at[FINAL], units(2 * (n_sp - 1)))
        wait_bytes(send_sem.at[TILE], units(15))
        own_final(both).wait()

    @pl.when(jnp.logical_not(gathers))
    def _():
        wait_bytes(send_sem.at[TILE], units(16))

    @pl.when(quarter_owner)
    def _():
        wait_bytes(recv_sem.at[GRAD_MOD], mod_hbm.at[pl.ds(0, 3)])
        pltpu.make_async_copy(mod_own, mod_hbm.at[from_first // 4], store_sem.at[3]).wait()

    @pl.when(jnp.logical_not(quarter_owner))
    def _():
        wait_bytes(recv_sem.at[GRAD_MOD], mod_hbm)

    for box, index in (
        (fine_box, FINE), (back_box, BACK), (text_box, TEXT), (coarse_box, COARSE),
    ):
        wait_bytes(send_sem.at[index], others(box))

    for side in range(2):
        wait_bytes(send_sem.at[CUBE + side], cube_box.at[side, pl.ds(1, 7)])
    sent_to_owners(text_dp_box, TEXT_DP)

    @pl.when(quarter_owner)
    def _():
        wait_bytes(send_sem.at[MOD], mod_box.at[pl.ds(0, 7)])
        wait_bytes(send_sem.at[GRAD_MOD], units(2 * (n_sp - 1)))

    @pl.when(jnp.logical_not(quarter_owner))
    def _():
        wait_bytes(send_sem.at[MOD], mod_box.at[pl.ds(0, 8)])

    @pl.when(owner)
    def _():
        wait_bytes(send_sem.at[POOLED], fine_box.at[pl.ds(0, n_sp - 1)])

    pair_cot.wait_send()
    wait_bytes(send_sem.at[PAIR_HIDDEN], hidden_pair.at[pl.ds(0, pixels)])

    @pl.when(sends_far)
    def _():
        far.wait_send()

    finish_edges(cot, cot_edge, 0)
    finish_edges(hidden, hid_edge, 2)

    @pl.when(owns_tail)
    def _():
        wait_bytes(send_sem.at[TAIL], tail_box.at[pl.ds(0, 3)])

    @pl.when(jnp.logical_not(owns_tail))
    def _():
        wait_bytes(send_sem.at[TAIL], tail_box.at[pl.ds(0, 4)])

    for store in stores:
        store.wait()


def write(
    out, grad_feat, final, mod, out_hbm, grad_feat_hbm, grad_conv_hbm, grad_mod_hbm,
    out_room, grad_feat_room, final_room, mod_room, grad_conv, grad_mod, load_sem, store_sem,
):
    fetch_final = pltpu.make_async_copy(final, final_room, load_sem.at[4])
    fetch_mod = pltpu.make_async_copy(mod, mod_room, load_sem.at[5])
    fetch_final.start()
    fetch_mod.start()
    moves = []
    for source, room, target in ((out, out_room, out_hbm), (grad_feat, grad_feat_room, grad_feat_hbm)):
        rows = source.shape[0] // 2
        for i in range(2):
            piece = pl.ds(i * rows, rows)
            number = len(moves)
            moves.append(
                (
                    pltpu.make_async_copy(source.at[piece], room.at[piece], load_sem.at[number]),
                    pltpu.make_async_copy(room.at[piece], target.at[piece], store_sem.at[number]),
                )
            )
    for fetch, _ in moves:
        fetch.start()
    fetch_final.wait()
    parts = final_room[...].astype(F32)
    tail_quarter = lax.axis_index("dp") // 8
    columns = [
        parts[2 * (tap // 2) + side, 8 * (tap % 2) : 8 * (tap % 2) + 8, :] for tap in range(8) for side in range(2)
    ] + [final_room[2 * tail_quarter + side].astype(F32)[16:24, :] for side in range(2)]
    grad_conv[...] = jnp.concatenate(columns, axis=1).astype(BF16)
    fetch_mod.wait()
    grad_mod[...] = jnp.concatenate([mod_room[i] for i in range(4)], axis=1)
    last = [
        pltpu.make_async_copy(grad_conv, grad_conv_hbm, store_sem.at[4]),
        pltpu.make_async_copy(grad_mod, grad_mod_hbm, store_sem.at[5]),
    ]
    for store in last:
        store.start()
    for fetch, store in moves:
        fetch.wait()
        store.start()
    for _, store in moves:
        store.wait()
    for store in last:
        store.wait()


def body(n_dp, n_sp, features, coarse, timestep, text_ids, text_table, w_mod, w_skip, w_conv, cotangent):
    _, tile_rows, width, channels = features.shape
    pixels = tile_rows * width
    cells = coarse.shape[1] * coarse.shape[2]
    coarse_width = coarse.shape[3]
    part, half = channels // n_dp, channels // 2
    taps = w_conv.shape[1] // channels
    vm = pltpu.VMEM
    tile = (8, LANES)
    anywhere = pl.BlockSpec(memory_space=pl.ANY)
    mod_rows = w_mod.shape[0] // n_dp
    scratch = [
        vm((pixels, channels), BF16),
        vm((pixels, channels), BF16),
        vm(text_ids.shape, jnp.int32),
        vm((pixels, channels), BF16),
        vm((cells, coarse_width), BF16),
        vm(text_table.shape, BF16),
        vm(w_mod.shape, BF16),
        vm(w_skip.shape, BF16),
        vm(w_conv.shape, BF16),
        vm((taps * channels, channels), BF16),
        vm((pixels, channels), BF16),
        vm((2, width, channels), BF16),
        vm((width, half), BF16),
        vm((2, width, channels), BF16),
        vm((pixels, half), BF16),
        vm((2 * pixels + 2 * width, half), BF16),
        vm((pixels + 2 * width, 3 * channels), BF16),
        vm((3 * half, 2 * pixels + 2 * width), BF16),
        vm((pixels + 2 * width, 3 * channels), BF16),
        vm((4 * cells, cells), BF16),
        vm((4 * cells, channels), F32),
        vm((pixels, channels), BF16),
        vm((pixels, channels), BF16),
        vm((2 * pixels, channels), BF16),
        vm((pixels, channels), F32),
        vm((n_sp,) + tile, F32),
        vm((n_sp,) + tile, F32),
        vm((n_sp,) + tile, F32),
        vm((n_sp, 16, LANES), F32),
        vm((n_sp, 16, LANES), BF16),
        vm((n_sp, 16, LANES), BF16),
        vm((16, LANES), F32),
        vm((n_dp,) + tile, F32),
        vm(tile, F32),
        vm(tile, F32),
        vm((4,) + tile, F32),
        vm((n_dp,) + tile, F32),
        vm((LANES, LANES), F32),
        vm((mod_rows, LANES), BF16),
        vm((3, 3 * half, channels), F32),
        vm((2, 4, 2, half + 16, half), BF16),
        vm((2, 8, half + 16, half), BF16),
        vm((16, 2 * part, half), BF16),
        vm((32, half), F32),
        vm((n_dp, 2 * part, half), BF16),
        vm((n_dp, part, half), F32),
        vm((32, half), BF16),
        pltpu.SemaphoreType.DMA((8,)),
        pltpu.SemaphoreType.DMA((4,)),
        pltpu.SemaphoreType.DMA((4,)),
        pltpu.SemaphoreType.DMA((4,)),
        pltpu.SemaphoreType.DMA((16,)),
        pltpu.SemaphoreType.DMA((16,)),
    ]
    shapes = (
        jax.ShapeDtypeStruct((pixels, channels), BF16),
        jax.ShapeDtypeStruct((pixels, channels), BF16),
        jax.ShapeDtypeStruct((8, 32, half), BF16),
        jax.ShapeDtypeStruct((4, mod_rows, LANES), BF16),
    )
    written = shapes[:2] + (
        jax.ShapeDtypeStruct((part, taps * channels), BF16),
        jax.ShapeDtypeStruct((mod_rows, 2 * channels), BF16),
    )
    results = pl.pallas_call(
        functools.partial(kernel, n_dp, n_sp, tile_rows, width),
        out_shape=shapes,
        in_specs=[pl.BlockSpec(memory_space=pltpu.SMEM)] + [anywhere] * 8,
        out_specs=(anywhere,) * 4,
        scratch_shapes=scratch,
        compiler_params=pltpu.CompilerParams(
            collective_id=0, has_side_effects=True, vmem_limit_bytes=VMEM_LIMIT
        ),
    )(
        timestep,
        text_ids,
        features.reshape(pixels, channels),
        coarse.reshape(cells, coarse_width),
        text_table,
        w_mod,
        w_skip,
        w_conv,
        cotangent.reshape(pixels, channels),
    )
    output, grad_features, grad_conv, grad_mod = pl.pallas_call(
        write,
        out_shape=written,
        in_specs=[anywhere] * 4,
        out_specs=(anywhere,) * 4,
        scratch_shapes=[vm(shape.shape, shape.dtype) for shape in shapes + written[2:]]
        + [pltpu.SemaphoreType.DMA((6,)), pltpu.SemaphoreType.DMA((6,))],
        compiler_params=pltpu.CompilerParams(vmem_limit_bytes=VMEM_LIMIT),
    )(*results)
    return output.reshape(features.shape), grad_features.reshape(features.shape), grad_conv, grad_mod


def solution(mesh):
    in_specs = (
        P("dp", "spatial", None, None),
        P("dp", "spatial", None, None),
        P("dp"),
        P(),
        P(("dp", "spatial"), None),
        P(),
        P(),
        P(),
        P("dp", "spatial", None, None),
    )
    out_specs = (
        P("dp", "spatial", None, None),
        P("dp", "spatial", None, None),
        P("dp", None),
        P("dp", None),
    )
    step = functools.partial(body, mesh.shape["dp"], mesh.shape["spatial"])
    return jax.shard_map(step, mesh=mesh, in_specs=in_specs, out_specs=out_specs, check_vma=False)
```

```python
import functools
import math

import jax
import jax.numpy as jnp
from jax import lax
from jax.experimental import pallas as pl
from jax.experimental.pallas import tpu as pltpu
from jax.sharding import PartitionSpec as P

GROUPS = 32
EPS = 1e-05
MESH = pl.DeviceIdType.MESH
F32 = jnp.float32
BF16 = jnp.bfloat16
LANES = 128
VMEM_LIMIT = 62 * 1024 * 1024


def dot(a, b, dims=((1,), (0,))):
    return lax.dot_general(a, b, (dims, ((), ())), preferred_element_type=F32)


def iota(shape, axis):
    return lax.broadcasted_iota(jnp.int32, shape, axis)


def sigmoid(x):
    return 0.5 * jnp.tanh(0.5 * x) + 0.5


def group_total(tile, width):
    lane = iota(tile.shape, 1)
    step = 1
    while step < width:
        partner = jnp.where(
            (lane & step) != 0, pltpu.roll(tile, step, 1), pltpu.roll(tile, LANES - step, 1)
        )
        tile = tile + partner
        step *= 2
    return tile


def as_row(tile, first, count):
    return jnp.concatenate([tile[first + i : first + i + 1, :] for i in range(count)], axis=1)


def as_rows(row):
    return [row[:, i * LANES : (i + 1) * LANES] for i in range(row.shape[1] // LANES)]


def from_neighbours(earlier, here, later, width):
    rows = here.shape[0]
    column = iota(here.shape, 0) & (width - 1)
    return (
        here
        + jnp.where(column == 0, 0.0, pltpu.roll(earlier, 1, 0))
        + jnp.where(column == width - 1, 0.0, pltpu.roll(later, rows - 1, 0))
    )


def turned_shifts(rows, turned_ref, first_pixel):
    width, channels = rows.shape
    turned = rows.T
    column = iota(turned.shape, 1)
    later = jnp.where(column == width - 1, 0.0, pltpu.roll(turned, width - 1, 1))
    earlier = jnp.where(column == 0, 0.0, pltpu.roll(turned, 1, 1))
    for i, shifted in enumerate((later, turned, earlier)):
        turned_ref[i * channels : (i + 1) * channels, pl.ds(first_pixel, width)] = shifted.astype(BF16)


def kernel(n_dp, n_sp, tile_rows, width, *refs):
    (
        time_ref, ids_hbm, feat_hbm, coarse_hbm, table_hbm, w_mod_hbm, w_skip_hbm, w_conv_hbm, cot_hbm,
        out_hbm, grad_feat_hbm, final_hbm, mod_hbm,
        out_ref, grad_feat_ref, ids_ref,
        feat, coarse, table, w_mod, w_skip, w_conv, cot_rows,
        far_edge, cot_half, cot_chip, cot_turned, chosen, up, merged, hid_rows, hidden_pair, grad_hid,
        coarse_box, fine_box, back_box, text_rows, text_out, text_box, text_sum, text_dp_box, pooled, time_part,
        mod_out, mod_box, mod_rows, mod_own, weight_own, cube_out, cube_box, weight_out, tail_sum,
        tile_box, tail_box, final_own,
        load_sem, store_sem, edge_send, edge_recv, send_sem, recv_sem,
    ) = refs
    channels = feat.shape[1]
    pixels = tile_rows * width
    half = channels // 2
    part = channels // n_dp
    cot, hidden = (ref.at[pl.ds(width, pixels)] for ref in (cot_rows, hid_rows))
    dp = lax.axis_index("dp")
    sp = lax.axis_index("spatial")
    chip, core = sp // 2, sp % 2
    other_sp = sp + 1 - 2 * core

    y, z_high = dp // 4, dp % 4
    z_low, x = sp // 8, chip % 4
    z = 2 * z_high + z_low
    odd_x, odd_y, odd_z = x % 2, y % 2, z_low
    high_x, high_y = x // 2, y // 2
    quarter = 2 * odd_z + odd_x
    rank = high_x * 16 + high_y * 4 + z_high

    def block_of(high):
        return 2 * (high % 2) + high // 2

    def neighbour(side, d):
        dx, dy, dz = d % 2, (d // 2) % 2, d // 4
        x_there = (x + dx * (1 - 2 * odd_x) * (1 - 2 * side) + 4) % 4
        y_there = (y + dy * (1 - 2 * odd_y) * (1 - 2 * side) + 8) % 8
        z_there = (z + dz * (1 - 2 * odd_z) * (1 - 2 * side) + 8) % 8
        return (y_there * 4 + z_there // 2, (z_there % 2) * 8 + x_there * 2 + core)

    def gatherer(number):
        y_there, z_there = number // 4, number % 4
        return ((2 * y_there + odd_y) * 4 + z_there, z_low * 8 + (2 * (z_there % 2) + odd_x) * 2 + core)

    gathers = high_x == z_high % 2
    group = []
    for dz, dx, dc in (
        (1, 2, 0), (1, 2, 1), (1, 1, 0), (1, 1, 1), (1, 3, 0), (1, 3, 1), (0, 2, 0), (0, 2, 1),
        (1, 0, 0), (1, 0, 1), (0, 1, 0), (0, 1, 1), (0, 3, 0), (0, 3, 1), (0, 0, 1),
    ):
        group.append(lax.rem(z_low + dz, 2) * 8 + lax.rem(x + dx, 4) * 2 + lax.rem(core + dc, 2))
    high_steps = sorted(
        ((dy, dz) for dy in range(4) for dz in range(4)), key=lambda s: -min(s[0], 4 - s[0]) - min(s[1], 4 - s[1])
    )
    dp_steps = sorted(
        ((dy, dz) for dy in range(8) for dz in range(4)), key=lambda s: -min(s[0], 8 - s[0]) - 2 * min(s[1], 4 - s[1])
    )[:-1]

    owns_tail = jnp.logical_and(gathers, high_y == quarter)
    owner = dp // 2 == sp
    from_first = lax.rem(sp - dp // 2 + n_sp, n_sp)
    quarter_owner = from_first % 4 == 0
    (
        COARSE, FINE, BACK, TEXT, TEXT_DP, POOLED, MOD, GRAD_MOD, TILE, TAIL, FINAL,
        PAIR_COT, PAIR_HIDDEN, FAR, CUBE,
    ) = range(15)

    def load(source, target, index):
        return pltpu.make_async_copy(source, target, load_sem.at[index])

    own_lanes = pl.ds(pl.multiple_of(core * half, half), half)
    other_lanes = pl.ds(pl.multiple_of((1 - core) * half, half), half)
    own_pixels = pl.multiple_of(core * pixels, pixels)
    other_pixels = pl.multiple_of((1 - core) * pixels, pixels)
    own_rows = pl.ds(pl.multiple_of(width + core * pixels, width), pixels)
    loads = [
        load(ids_hbm, ids_ref, 1),
        load(table_hbm, table, 2),
        load(coarse_hbm, coarse, 0),
        load(cot_hbm, cot, 3),
    ]
    later = [
        load(feat_hbm, feat, 4),
        load(w_skip_hbm, w_skip, 5),
        load(w_mod_hbm, w_mod, 6),
        load(w_conv_hbm, w_conv, 7),
    ]
    for copy in loads[:2]:
        copy.start()

    barrier = pltpu.get_barrier_semaphore()

    def greet(place):
        pl.semaphore_signal(barrier, inc=1, device_id=place, device_id_type=MESH)

    @pl.when(owner)
    def _():
        for dy, dz in dp_steps:
            greet((lax.rem(y + dy, 8) * 4 + lax.rem(z_high + dz, 4), sp))

    for there in group:
        greet((dp, there))

    for copy in loads[2:] + later:
        copy.start()

    def remote(source, target, send, recv, place):
        return pltpu.make_async_remote_copy(
            src_ref=source, dst_ref=target, send_sem=send, recv_sem=recv, device_id=place, device_id_type=MESH
        )

    def wait_bytes(sem, ref):
        pltpu.make_async_copy(ref, ref, sem).wait()

    def to_spatial(box, index):
        for there in group:
            remote(box.at[sp], box.at[sp], send_sem.at[index], recv_sem.at[index], (dp, there)).start()

    def to_owners(source_of, box, index):
        for j in range(2):
            there = 2 * sp + j

            @pl.when(there != dp)
            def _():
                remote(source_of(j), box.at[dp], send_sem.at[index], recv_sem.at[index], (there, sp)).start()

    def sent_to_owners(box, index):
        @pl.when(owner)
        def _():
            wait_bytes(send_sem.at[index], box.at[pl.ds(0, 1)])

        @pl.when(jnp.logical_not(owner))
        def _():
            wait_bytes(send_sem.at[index], box.at[pl.ds(0, 2)])

    def from_owner(ref, index):
        for there in group:
            remote(ref, ref, send_sem.at[index], recv_sem.at[index], (dp, there)).start()

    def others(box):
        return box.at[pl.ds(0, box.shape[0] - 1)]

    def receive(box, index):
        wait_bytes(recv_sem.at[index], others(box))

    def total(box):
        return jnp.sum(box[...], axis=0)

    vocab = table.shape[0]
    batch, tokens = ids_ref.shape
    loads[0].wait()
    local_ids = jnp.concatenate(
        [ids_ref[pl.ds(j, n_sp, stride=2), :] for j in range(2)], axis=0
    ) - (dp * n_sp + sp) * vocab
    turned_ids = local_ids.astype(F32).T
    quarters = jnp.concatenate([turned_ids] * 4, axis=1) - 16.0 * lax.shift_right_logical(
        iota((tokens, LANES), 1), 5
    ).astype(F32)
    found = [
        jnp.sum(jnp.where(quarters == float(k), 1.0, 0.0), axis=0, keepdims=True) for k in range(16)
    ]
    found = jnp.concatenate(found, axis=0)
    counts = jnp.concatenate([found[:, q * batch : (q + 1) * batch] for q in range(4)], axis=0)[:vocab].astype(BF16)
    loads[1].wait()
    partial = dot(counts, table[...], ((0,), (0,)))
    for i in range(8):
        for j in range(2):
            text_rows[:, 8 * j + i, :] = partial[j * n_sp : (j + 1) * n_sp, i * LANES : (i + 1) * LANES]
    text_out[...] = text_rows[...].astype(BF16)

    loads[2].wait()
    coarse_f = coarse[...].astype(F32)
    coarse_box[sp] = jnp.concatenate(
        as_rows(jnp.sum(coarse_f, axis=0, keepdims=True))
        + as_rows(jnp.sum(coarse_f * coarse_f, axis=0, keepdims=True)),
        axis=0,
    )

    pl.semaphore_wait(barrier, jnp.where(owner, n_sp, n_sp + 1))

    to_spatial(coarse_box, COARSE)
    for there in group:
        remote(text_out.at[there], text_box.at[sp], send_sem.at[TEXT], recv_sem.at[TEXT], (dp, there)).start()

    text_box[sp] = text_out[sp]

    last = pixels - width

    def edges(rows, first):
        down = remote(
            rows.at[pl.ds(pixels, width)],
            rows.at[pl.ds(0, width)],
            edge_send.at[first],
            edge_recv.at[first],
            (dp, sp + 1),
        )
        upward = remote(
            rows.at[pl.ds(width, width)],
            rows.at[pl.ds(width + pixels, width)],
            edge_send.at[first + 1],
            edge_recv.at[first + 1],
            (dp, sp - 1),
        )
        return down, upward

    def start_edges(rows, first):
        down, upward = edges(rows, first)

        @pl.when(sp < n_sp - 1)
        def _():
            down.start()

        @pl.when(sp > 0)
        def _():
            upward.start()

    def receive_edges(rows, first):
        down, upward = edges(rows, first)

        @pl.when(sp > 0)
        def _():
            down.wait_recv()

        @pl.when(sp < n_sp - 1)
        def _():
            upward.wait_recv()

        @pl.when(sp == 0)
        def _():
            rows[0:width, :] = jnp.zeros((width, channels), BF16)

        @pl.when(sp == n_sp - 1)
        def _():
            rows[width + pixels :, :] = jnp.zeros((width, channels), BF16)

    def finish_edges(rows, first):
        down, upward = edges(rows, first)

        @pl.when(sp < n_sp - 1)
        def _():
            down.wait_send()

        @pl.when(sp > 0)
        def _():
            upward.wait_send()

    loads[3].wait()
    start_edges(cot_rows, 0)
    cot_half[...] = cot[:, other_lanes]
    cot_chip[own_rows, :] = cot[:, own_lanes]
    pair_cot = remote(
        cot_half, cot_chip.at[own_rows], send_sem.at[PAIR_COT], recv_sem.at[PAIR_COT], (dp, other_sp)
    )
    pair_cot.start()
    far = remote(
        cot_chip.at[pl.ds(pl.multiple_of(width + core * (pixels + last), width), width)],
        far_edge,
        send_sem.at[FAR],
        recv_sem.at[FAR],
        (dp, sp - 2 + 4 * core),
    )
    chips = n_sp // 2
    sends_far = jnp.logical_or(jnp.logical_and(core == 0, chip > 0), jnp.logical_and(core == 1, chip < chips - 1))
    takes_far = jnp.logical_or(jnp.logical_and(core == 0, chip < chips - 1), jnp.logical_and(core == 1, chip > 0))

    @pl.when(sends_far)
    def _():
        far.start()

    row, lane = iota((8, LANES), 0), iota((8, LANES), 1)
    half_width = 4 * LANES
    index = ((row & 3) * LANES + lane).astype(F32)
    angle = time_ref[0].astype(F32) * jnp.exp(-math.log(10000.0) * index / half_width)
    time_part[...] = jnp.where(row < 4, jnp.sin(angle), jnp.cos(angle))

    shape = chosen.shape
    coarse_cols = width // 4
    place = iota(shape, 0)
    wanted = lax.shift_right_logical(place, width.bit_length() - 1) * coarse_cols + (
        lax.shift_right_logical(place & (width - 1), 2)
    )
    chosen[...] = (wanted == iota(shape, 1)).astype(F32).astype(BF16)

    def turn_rows(first_row):
        @pl.loop(0, tile_rows, unroll=True)
        def _(r):
            start = pl.multiple_of(first_row + r * width, width)
            turned_shifts(cot_chip[pl.ds(start, width), :].astype(F32), cot_turned, start)

    receive(text_box, TEXT)
    text_sum[...] = jnp.sum(text_box[...].astype(F32), axis=0)
    to_owners(lambda j: text_sum.at[pl.ds(8 * j, 8)], text_dp_box, TEXT_DP)

    later[1].wait()
    receive(coarse_box, COARSE)
    coarse_total = group_total(total(coarse_box), coarse.shape[1] // GROUPS)
    coarse_count = coarse.shape[0] * n_sp * (coarse.shape[1] // GROUPS)
    tiles = coarse.shape[1] // LANES
    c_mean = coarse_total[0:tiles, :] / coarse_count
    c_scale = lax.rsqrt(coarse_total[tiles : 2 * tiles, :] / coarse_count - c_mean * c_mean + EPS)
    c_normed = (coarse[...].astype(F32) - as_row(c_mean, 0, tiles)) * as_row(c_scale, 0, tiles)
    coarse_act = (c_normed * sigmoid(c_normed)).astype(BF16)
    skip = dot(coarse_act, w_skip[...]).astype(BF16)
    up[...] = dot(chosen[...], skip)

    later[0].wait()

    def merge(r, sums):
        start = pl.multiple_of(r * width, width)
        up_start = pl.multiple_of((r // 4) * width, width)
        rows = (feat[pl.ds(start, width), :].astype(F32) + up[pl.ds(up_start, width), :]).astype(BF16)
        merged[pl.ds(start, width), :] = rows
        rows = rows.astype(F32)
        first, second = sums
        first = first + jnp.sum(rows.reshape(width // 8, 8, channels), axis=0)
        second = second + jnp.sum((rows * rows).reshape(width // 8, 8, channels), axis=0)
        return first, second

    zero = jnp.zeros((8, channels), F32)
    first, second = lax.fori_loop(0, tile_rows, merge, (zero, zero), unroll=True)

    def sums_tile(one, two):
        one = jnp.sum(one, axis=0, keepdims=True)
        two = jnp.sum(two, axis=0, keepdims=True)
        return jnp.concatenate(as_rows(one) + as_rows(two) + [jnp.zeros((4, LANES), F32)], axis=0)

    fine_box[sp] = sums_tile(first, second)
    to_spatial(fine_box, FINE)

    @pl.when(owner)
    def _():
        text_dp_box[dp] = text_sum[pl.ds(pl.multiple_of(8 * (dp % 2), 8), 8), :]
        receive(text_dp_box, TEXT_DP)
        pooled[...] = total(text_dp_box)
        from_owner(pooled, POOLED)

    turn_rows(width + own_pixels)
    wait_bytes(recv_sem.at[PAIR_COT], cot_chip.at[own_rows])
    turn_rows(width + other_pixels)
    receive_edges(cot_rows, 0)

    @pl.when(takes_far)
    def _():
        far.wait_recv()

    @pl.when(jnp.logical_not(takes_far))
    def _():
        far_edge[...] = jnp.zeros((width, half), BF16)

    near = cot_rows[pl.ds(pl.multiple_of(core * (width + pixels), width), width), own_lanes].astype(F32)
    farther = far_edge[...].astype(F32)
    turned_shifts(jnp.where(core == 0, near, farther), cot_turned, 0)
    turned_shifts(jnp.where(core == 0, farther, near), cot_turned, width + 2 * pixels)

    receive(fine_box, FINE)
    fine_total = group_total(total(fine_box), channels // GROUPS)
    fine_count = pixels * n_sp * (channels // GROUPS)
    f_mean = fine_total[0:2, :] / fine_count
    f_scale = lax.rsqrt(fine_total[2:4, :] / fine_count - f_mean * f_mean + EPS)
    center, scale = as_row(f_mean, 0, 2), as_row(f_scale, 0, 2)

    @pl.when(jnp.logical_not(owner))
    def _():
        wait_bytes(recv_sem.at[POOLED], pooled)

    embed = time_part[...] + pooled[...] / tokens
    embed = (embed * sigmoid(embed)).astype(BF16).astype(F32)
    later[2].wait()
    embed_row = jnp.broadcast_to(as_row(embed, 0, 8), (8, 8 * LANES)).astype(BF16)
    modulation = dot(embed_row, w_mod[...])[0:1, :]
    gain = 1.0 + modulation[:, :channels]
    shift = modulation[:, channels:]

    factor = scale * gain
    term_of_hidden = shift - center * factor

    @pl.loop(0, tile_rows, unroll=True)
    def _(r):
        start = pl.multiple_of(r * width, width)
        pre = merged[pl.ds(start, width), :].astype(F32) * factor + term_of_hidden
        act = pre * sigmoid(pre)
        hidden[pl.ds(start, width), :] = act.astype(BF16)
        low, high = act[:, :half], act[:, half:]
        block = lax.shift_right_logical(iota(low.shape, 1), 5)
        even = jnp.where((block & 1) == 0, low, pltpu.roll(high, 32, 1))
        odd = jnp.where((block & 1) == 0, pltpu.roll(low, LANES - 32, 1), high)
        rows = pl.ds(pl.multiple_of(own_pixels + start, width), width)
        hidden_pair[rows, :] = jnp.concatenate([even, odd], axis=1).astype(BF16)

        @pl.when(r % 2 == 1)
        def _():
            two = pl.ds(pl.multiple_of(own_pixels + start - width, width), 2 * width)
            remote(
                hidden_pair.at[two], hidden_pair.at[two], send_sem.at[PAIR_HIDDEN], recv_sem.at[PAIR_HIDDEN], (dp, other_sp)
            ).start()

    def weight_term(dr, first_pixel):
        lanes = pl.ds(pl.multiple_of((2 - dr) * width + first_pixel, width), pixels)
        return dot(cot_turned[:, lanes], hidden_pair[pl.ds(first_pixel, pixels), :])

    for dr in range(3):
        weight_own[dr] = weight_term(dr, own_pixels)
    wait_bytes(recv_sem.at[PAIR_HIDDEN], hidden_pair.at[pl.ds(0, pixels)])
    def send_shares(their_quarter):
        dx = odd_x + their_quarter % 2 - 2 * odd_x * (their_quarter % 2)
        dz = odd_z + their_quarter // 2 - 2 * odd_z * (their_quarter // 2)
        for dy in range(2):
            their_y = odd_y + dy - 2 * odd_y * dy
            d = dx + 2 * dy + 4 * dz

            @pl.when(d > 0)
            def _():
                for side in range(2):
                    remote(
                        cube_out.at[side, their_quarter, their_y],
                        cube_box.at[side, d],
                        send_sem.at[CUBE + side],
                        recv_sem.at[CUBE + side],
                        neighbour(side, d),
                    ).start()

    for dr in (2, 1, 0):
        grads = weight_own[dr] + weight_term(dr, other_pixels)
        for dc in (2, 1, 0):
            tap = 3 * dr + dc
            grad = grads[dc * half : (dc + 1) * half, :]
            if tap < 8:
                cube_out[tap % 2, tap // 2, 0, 0:half] = grad[:, :half].astype(BF16)
                cube_out[tap % 2, tap // 2, 1, 0:half] = grad[:, half:].astype(BF16)
            else:
                turned = grad.T.astype(BF16)
                for side in range(2):
                    for number in range(8):
                        first = (number % 2) * half + block_of(number // 2) * 32 + side * 16
                        cube_out[side, number // 2, number % 2, half : half + 16] = turned[first : first + 16, :]
        for their_quarter in ((0, 1), (2,), (3,))[dr]:
            send_shares(their_quarter)

    for side in range(2):
        cube_box[side, 0] = cube_out[side, quarter, odd_y]

    start_edges(hid_rows, 2)

    later[3].wait()
    chunk = pixels // 2

    @pl.loop(0, 2)
    def _(c):
        start = pl.multiple_of(c * chunk, chunk)
        terms = []
        for dc in range(3):
            term = None
            for dr in range(3):
                tap = 3 * dr + dc
                more = dot(
                    cot_rows[pl.ds(pl.multiple_of(start + (2 - dr) * width, width), chunk), :],
                    w_conv[:, tap * channels : (tap + 1) * channels],
                    ((1,), (1,)),
                )
                term = more if term is None else term + more
            terms.append(term)
        grad_hid[pl.ds(start, chunk), :] = from_neighbours(terms[2], terms[1], terms[0], width)

    def backward(r, sums):
        start = pl.multiple_of(r * width, width)
        normed = (merged[pl.ds(start, width), :].astype(F32) - center) * scale
        pre = normed * gain + shift
        sigma = sigmoid(pre)
        grad = grad_hid[pl.ds(start, width), :] * sigma * (1.0 + pre * (1.0 - sigma))
        grad_hid[pl.ds(start, width), :] = grad
        first, second = sums
        first = first + jnp.sum((grad * normed).reshape(width // 8, 8, channels), axis=0)
        second = second + jnp.sum(grad.reshape(width // 8, 8, channels), axis=0)
        return first, second

    first, second = lax.fori_loop(0, tile_rows, backward, (zero, zero), unroll=True)
    back_box[sp] = sums_tile(first, second)
    to_spatial(back_box, BACK)

    sides = []
    for side in range(2):
        wait_bytes(recv_sem.at[CUBE + side], cube_box.at[side, pl.ds(1, 7)])
        summed = cube_box[side, 0].astype(F32)
        for d in range(1, 8):
            summed = summed + cube_box[side, d].astype(F32)
        sides.append(summed[0:half, :].T.reshape(16, part, half))
        tail_sum[side * 16 : (side + 1) * 16, :] = summed[half : half + 16, :]
    weight_out[...] = jnp.concatenate(sides, axis=1).astype(BF16)

    def part_of(number):
        return weight_out.at[block_of(number // 4) * 4 + number % 4]

    for dy, dz in high_steps:
        number = lax.rem(high_y + dy, 4) * 4 + lax.rem(z_high + dz, 4)
        copy = remote(
            part_of(number), tile_box.at[rank], send_sem.at[TILE], recv_sem.at[TILE], gatherer(number)
        )
        if dy + dz > 0:
            copy.start()
        else:
            pl.when(jnp.logical_not(gathers))(copy.start)

    for m in range(4):
        itself = jnp.logical_and(owns_tail, z_high == m)

        @pl.when(jnp.logical_not(itself))
        def _():
            remote(
                tail_sum.at[pl.ds(m * part, part)],
                tail_box.at[rank],
                send_sem.at[TAIL],
                recv_sem.at[TAIL],
                gatherer(quarter * 4 + m),
            ).start()

        @pl.when(itself)
        def _():
            tail_box[rank] = tail_sum[m * part : (m + 1) * part, :]

    @pl.when(gathers)
    def _():
        tile_box[rank] = part_of(high_y * 4 + z_high)[...]

    receive(back_box, BACK)
    back = total(back_box)
    for i in range(4):
        pair_there = lax.rem(sp - 4 * i + n_sp, n_sp)
        wanted_row = jnp.sum(jnp.where(row == pair_there // 2, embed, 0.0), axis=0, keepdims=True)
        mod_out[i] = jnp.concatenate([back[i : i + 1, :], wanted_row, jnp.zeros((6, LANES), F32)], axis=0)
        for j in range(2):
            there = 2 * pair_there + j

            @pl.when(there != dp)
            def _():
                remote(mod_out.at[i], mod_box.at[dp], send_sem.at[MOD], recv_sem.at[MOD], (there, sp)).start()

            @pl.when(there == dp)
            def _():
                mod_box[dp] = mod_out[i]

    receive_edges(hid_rows, 2)

    @pl.loop(0, 2)
    def _(c):
        start = pl.multiple_of(c * chunk, chunk)
        terms = []
        for dc in range(3):
            term = merged[pl.ds(start, chunk), :].astype(F32) if dc == 1 else None
            for dr in range(3):
                tap = 3 * dr + dc
                more = dot(
                    hid_rows[pl.ds(pl.multiple_of(start + dr * width, width), chunk), :],
                    w_conv[:, tap * channels : (tap + 1) * channels],
                )
                term = more if term is None else term + more
            terms.append(term)
        out_ref[pl.ds(start, chunk), :] = from_neighbours(terms[0], terms[1], terms[2], width).astype(BF16)

    stores = [
        pltpu.make_async_copy(source, target, store_sem.at[i])
        for i, (source, target) in enumerate(
            (
                (out_ref, out_hbm), (grad_feat_ref, grad_feat_hbm),
            )
        )
    ]
    stores[0].start()

    gain_tile = jnp.concatenate(as_rows(gain) + as_rows(gain), axis=0)
    means = group_total(back[0:4, :] * gain_tile, channels // GROUPS) / fine_count
    mean_two, mean_one = as_row(means, 0, 2), as_row(means, 2, 2)

    final_slot = 2 * quarter + core

    def to_group(rows):
        for there in group:
            remote(
                final_own.at[rows],
                final_hbm.at[final_slot, rows],
                send_sem.at[FINAL],
                recv_sem.at[FINAL],
                (dp, there),
            ).start()

    def own_final(rows):
        return pltpu.make_async_copy(final_own.at[rows], final_hbm.at[final_slot, rows], store_sem.at[2])

    main, both = pl.ds(0, 16), pl.ds(0, 32)
    no_tail = jnp.logical_and(gathers, jnp.logical_not(owns_tail))

    @pl.when(gathers)
    def _():
        receive(tile_box, TILE)
        final_own[0:16, :] = jnp.sum(tile_box[...].astype(F32), axis=0).astype(BF16)

    @pl.when(no_tail)
    def _():
        to_group(main)
        own_final(main).start()

    @pl.when(owns_tail)
    def _():
        receive(tail_box, TAIL)
        final_own[16:32, :] = jnp.concatenate([total(tail_box), jnp.zeros((part, half), F32)], axis=0).astype(BF16)
        to_group(both)
        own_final(both).start()

    @pl.loop(0, tile_rows, unroll=True)
    def _(r):
        start = pl.multiple_of(r * width, width)
        normed = (merged[pl.ds(start, width), :].astype(F32) - center) * scale
        inner = grad_hid[pl.ds(start, width), :] * gain - mean_one - normed * mean_two
        grad_feat_ref[pl.ds(start, width), :] = (cot[pl.ds(start, width), :].astype(F32) + scale * inner).astype(BF16)

    stores[1].start()

    @pl.when(quarter_owner)
    def _():
        receive(mod_box, MOD)
        share = 8 * LANES // n_dp
        in_lanes = LANES // share
        embeds = mod_box[:, 1, :].astype(BF16)
        rest = mod_box[:, 0, :]
        grads = None
        for _ in range(3):
            piece = rest.astype(BF16)
            rest = rest - piece.astype(F32)
            term = dot(embeds, piece, ((0,), (0,)))
            grads = term if grads is None else grads + term
        mod_rows[...] = grads
        mod_start = pl.multiple_of((dp % in_lanes) * share, share)
        number = from_first // 4
        mod_own[...] = mod_rows[pl.ds(mod_start, share), :].astype(BF16)

        for there in group:
            remote(mod_own, mod_hbm.at[number], send_sem.at[GRAD_MOD], recv_sem.at[GRAD_MOD], (dp, there)).start()

        pltpu.make_async_copy(mod_own, mod_hbm.at[number], store_sem.at[3]).start()

    def units(count):
        return tile_box.at[pl.ds(0, count)]

    @pl.when(jnp.logical_not(gathers))
    def _():
        wait_bytes(recv_sem.at[FINAL], units(10))

    @pl.when(no_tail)
    def _():
        wait_bytes(recv_sem.at[FINAL], units(9))
        wait_bytes(send_sem.at[FINAL], units(n_sp - 1))
        wait_bytes(send_sem.at[TILE], units(15))
        own_final(main).wait()

    @pl.when(owns_tail)
    def _():
        wait_bytes(recv_sem.at[FINAL], units(8))
        wait_bytes(send_sem.at[FINAL], units(2 * (n_sp - 1)))
        wait_bytes(send_sem.at[TILE], units(15))
        own_final(both).wait()

    @pl.when(jnp.logical_not(gathers))
    def _():
        wait_bytes(send_sem.at[TILE], units(16))

    @pl.when(quarter_owner)
    def _():
        wait_bytes(recv_sem.at[GRAD_MOD], mod_hbm.at[pl.ds(0, 3)])
        pltpu.make_async_copy(mod_own, mod_hbm.at[from_first // 4], store_sem.at[3]).wait()

    @pl.when(jnp.logical_not(quarter_owner))
    def _():
        wait_bytes(recv_sem.at[GRAD_MOD], mod_hbm)

    for box, index in (
        (fine_box, FINE), (back_box, BACK), (text_box, TEXT), (coarse_box, COARSE),
    ):
        wait_bytes(send_sem.at[index], others(box))

    for side in range(2):
        wait_bytes(send_sem.at[CUBE + side], cube_box.at[side, pl.ds(1, 7)])
    sent_to_owners(text_dp_box, TEXT_DP)

    @pl.when(quarter_owner)
    def _():
        wait_bytes(send_sem.at[MOD], mod_box.at[pl.ds(0, 7)])
        wait_bytes(send_sem.at[GRAD_MOD], units(2 * (n_sp - 1)))

    @pl.when(jnp.logical_not(quarter_owner))
    def _():
        wait_bytes(send_sem.at[MOD], mod_box.at[pl.ds(0, 8)])

    @pl.when(owner)
    def _():
        wait_bytes(send_sem.at[POOLED], fine_box.at[pl.ds(0, n_sp - 1)])

    pair_cot.wait_send()
    wait_bytes(send_sem.at[PAIR_HIDDEN], hidden_pair.at[pl.ds(0, pixels)])

    @pl.when(sends_far)
    def _():
        far.wait_send()

    finish_edges(cot_rows, 0)
    finish_edges(hid_rows, 2)

    @pl.when(owns_tail)
    def _():
        wait_bytes(send_sem.at[TAIL], tail_box.at[pl.ds(0, 3)])

    @pl.when(jnp.logical_not(owns_tail))
    def _():
        wait_bytes(send_sem.at[TAIL], tail_box.at[pl.ds(0, 4)])

    for store in stores:
        store.wait()


def write(
    out, grad_feat, final, mod, out_hbm, grad_feat_hbm, grad_conv_hbm, grad_mod_hbm,
    out_room, grad_feat_room, final_room, mod_room, grad_conv, grad_mod, load_sem, store_sem,
):
    fetch_final = pltpu.make_async_copy(final, final_room, load_sem.at[4])
    fetch_mod = pltpu.make_async_copy(mod, mod_room, load_sem.at[5])
    fetch_final.start()
    fetch_mod.start()
    moves = []
    for source, room, target in ((out, out_room, out_hbm), (grad_feat, grad_feat_room, grad_feat_hbm)):
        rows = source.shape[0] // 2
        for i in range(2):
            piece = pl.ds(i * rows, rows)
            number = len(moves)
            moves.append(
                (
                    pltpu.make_async_copy(source.at[piece], room.at[piece], load_sem.at[number]),
                    pltpu.make_async_copy(room.at[piece], target.at[piece], store_sem.at[number]),
                )
            )
    for fetch, _ in moves:
        fetch.start()
    fetch_final.wait()
    parts = final_room[...].astype(F32)
    tail_quarter = lax.axis_index("dp") // 8
    columns = [
        parts[2 * (tap // 2) + side, 8 * (tap % 2) : 8 * (tap % 2) + 8, :] for tap in range(8) for side in range(2)
    ] + [final_room[2 * tail_quarter + side].astype(F32)[16:24, :] for side in range(2)]
    grad_conv[...] = jnp.concatenate(columns, axis=1).astype(BF16)
    fetch_mod.wait()
    grad_mod[...] = jnp.concatenate([mod_room[i] for i in range(4)], axis=1)
    last = [
        pltpu.make_async_copy(grad_conv, grad_conv_hbm, store_sem.at[4]),
        pltpu.make_async_copy(grad_mod, grad_mod_hbm, store_sem.at[5]),
    ]
    for store in last:
        store.start()
    for fetch, store in moves:
        fetch.wait()
        store.start()
    for _, store in moves:
        store.wait()
    for store in last:
        store.wait()


def body(n_dp, n_sp, features, coarse, timestep, text_ids, text_table, w_mod, w_skip, w_conv, cotangent):
    _, tile_rows, width, channels = features.shape
    pixels = tile_rows * width
    cells = coarse.shape[1] * coarse.shape[2]
    coarse_width = coarse.shape[3]
    part, half = channels // n_dp, channels // 2
    taps = w_conv.shape[1] // channels
    vm = pltpu.VMEM
    tile = (8, LANES)
    anywhere = pl.BlockSpec(memory_space=pl.ANY)
    mod_rows = w_mod.shape[0] // n_dp
    scratch = [
        vm((pixels, channels), BF16),
        vm((pixels, channels), BF16),
        vm(text_ids.shape, jnp.int32),
        vm((pixels, channels), BF16),
        vm((cells, coarse_width), BF16),
        vm(text_table.shape, BF16),
        vm(w_mod.shape, BF16),
        vm(w_skip.shape, BF16),
        vm(w_conv.shape, BF16),
        vm((pixels + 2 * width, channels), BF16),
        vm((width, half), BF16),
        vm((pixels, half), BF16),
        vm((2 * pixels + 2 * width, half), BF16),
        vm((3 * half, 2 * pixels + 2 * width), BF16),
        vm((4 * cells, cells), BF16),
        vm((4 * cells, channels), F32),
        vm((pixels, channels), BF16),
        vm((pixels + 2 * width, channels), BF16),
        vm((2 * pixels, channels), BF16),
        vm((pixels, channels), F32),
        vm((n_sp,) + tile, F32),
        vm((n_sp,) + tile, F32),
        vm((n_sp,) + tile, F32),
        vm((n_sp, 16, LANES), F32),
        vm((n_sp, 16, LANES), BF16),
        vm((n_sp, 16, LANES), BF16),
        vm((16, LANES), F32),
        vm((n_dp,) + tile, F32),
        vm(tile, F32),
        vm(tile, F32),
        vm((4,) + tile, F32),
        vm((n_dp,) + tile, F32),
        vm((LANES, LANES), F32),
        vm((mod_rows, LANES), BF16),
        vm((3, 3 * half, channels), F32),
        vm((2, 4, 2, half + 16, half), BF16),
        vm((2, 8, half + 16, half), BF16),
        vm((16, 2 * part, half), BF16),
        vm((32, half), F32),
        vm((n_dp, 2 * part, half), BF16),
        vm((n_dp, part, half), F32),
        vm((32, half), BF16),
        pltpu.SemaphoreType.DMA((8,)),
        pltpu.SemaphoreType.DMA((4,)),
        pltpu.SemaphoreType.DMA((4,)),
        pltpu.SemaphoreType.DMA((4,)),
        pltpu.SemaphoreType.DMA((16,)),
        pltpu.SemaphoreType.DMA((16,)),
    ]
    shapes = (
        jax.ShapeDtypeStruct((pixels, channels), BF16),
        jax.ShapeDtypeStruct((pixels, channels), BF16),
        jax.ShapeDtypeStruct((8, 32, half), BF16),
        jax.ShapeDtypeStruct((4, mod_rows, LANES), BF16),
    )
    written = shapes[:2] + (
        jax.ShapeDtypeStruct((part, taps * channels), BF16),
        jax.ShapeDtypeStruct((mod_rows, 2 * channels), BF16),
    )
    results = pl.pallas_call(
        functools.partial(kernel, n_dp, n_sp, tile_rows, width),
        out_shape=shapes,
        in_specs=[pl.BlockSpec(memory_space=pltpu.SMEM)] + [anywhere] * 8,
        out_specs=(anywhere,) * 4,
        scratch_shapes=scratch,
        compiler_params=pltpu.CompilerParams(
            collective_id=0, has_side_effects=True, vmem_limit_bytes=VMEM_LIMIT
        ),
    )(
        timestep,
        text_ids,
        features.reshape(pixels, channels),
        coarse.reshape(cells, coarse_width),
        text_table,
        w_mod,
        w_skip,
        w_conv,
        cotangent.reshape(pixels, channels),
    )
    output, grad_features, grad_conv, grad_mod = pl.pallas_call(
        write,
        out_shape=written,
        in_specs=[anywhere] * 4,
        out_specs=(anywhere,) * 4,
        scratch_shapes=[vm(shape.shape, shape.dtype) for shape in shapes + written[2:]]
        + [pltpu.SemaphoreType.DMA((6,)), pltpu.SemaphoreType.DMA((6,))],
        compiler_params=pltpu.CompilerParams(vmem_limit_bytes=VMEM_LIMIT),
    )(*results)
    return output.reshape(features.shape), grad_features.reshape(features.shape), grad_conv, grad_mod


def solution(mesh):
    in_specs = (
        P("dp", "spatial", None, None),
        P("dp", "spatial", None, None),
        P("dp"),
        P(),
        P(("dp", "spatial"), None),
        P(),
        P(),
        P(),
        P("dp", "spatial", None, None),
    )
    out_specs = (
        P("dp", "spatial", None, None),
        P("dp", "spatial", None, None),
        P("dp", None),
        P("dp", None),
    )
    step = functools.partial(body, mesh.shape["dp"], mesh.shape["spatial"])
    return jax.shard_map(step, mesh=mesh, in_specs=in_specs, out_specs=out_specs, check_vma=False)
```

```python
import functools
import math

import jax
import jax.numpy as jnp
from jax import lax
from jax.experimental import pallas as pl
from jax.experimental.pallas import tpu as pltpu
from jax.sharding import PartitionSpec as P

GROUPS = 32
EPS = 1e-05
MESH = pl.DeviceIdType.MESH
F32 = jnp.float32
BF16 = jnp.bfloat16
LANES = 128
VMEM_LIMIT = 62 * 1024 * 1024


def dot(a, b, dims=((1,), (0,))):
    return lax.dot_general(a, b, (dims, ((), ())), preferred_element_type=F32)


def iota(shape, axis):
    return lax.broadcasted_iota(jnp.int32, shape, axis)


def sigmoid(x):
    return 0.5 * jnp.tanh(0.5 * x) + 0.5


def group_total(tile, width):
    lane = iota(tile.shape, 1)
    step = 1
    while step < width:
        partner = jnp.where(
            (lane & step) != 0, pltpu.roll(tile, step, 1), pltpu.roll(tile, LANES - step, 1)
        )
        tile = tile + partner
        step *= 2
    return tile


def as_row(tile, first, count):
    return jnp.concatenate([tile[first + i : first + i + 1, :] for i in range(count)], axis=1)


def as_rows(row):
    return [row[:, i * LANES : (i + 1) * LANES] for i in range(row.shape[1] // LANES)]


def from_neighbours(earlier, here, later, width):
    rows = here.shape[0]
    column = iota(here.shape, 0) & (width - 1)
    return (
        here
        + jnp.where(column == 0, 0.0, pltpu.roll(earlier, 1, 0))
        + jnp.where(column == width - 1, 0.0, pltpu.roll(later, rows - 1, 0))
    )


def turned_shifts(rows, turned_ref, first_pixel):
    width, channels = rows.shape
    turned = rows.T
    column = iota(turned.shape, 1)
    later = jnp.where(column == width - 1, 0.0, pltpu.roll(turned, width - 1, 1))
    earlier = jnp.where(column == 0, 0.0, pltpu.roll(turned, 1, 1))
    for i, shifted in enumerate((later, turned, earlier)):
        turned_ref[i * channels : (i + 1) * channels, pl.ds(first_pixel, width)] = shifted.astype(BF16)


def kernel(n_dp, n_sp, tile_rows, width, *refs):
    (
        time_ref, ids_hbm, feat_hbm, coarse_hbm, table_hbm, w_mod_hbm, w_skip_hbm, w_conv_hbm, cot_hbm,
        out_hbm, grad_feat_hbm, final_hbm, mod_hbm,
        out_ref, grad_feat_ref, ids_ref,
        feat, coarse, table, w_mod, w_skip, w_conv, cot_rows,
        far_edge, cot_half, cot_chip, cot_turned, chosen, up, merged, hid_rows, hidden_pair, grad_hid,
        coarse_box, fine_box, back_box, text_rows, text_out, text_box, text_sum, text_dp_box, pooled, time_part,
        mod_out, mod_box, mod_rows, mod_own, weight_own, cube_out, cube_box, weight_out, tail_sum,
        tile_box, tail_box, final_own,
        load_sem, store_sem, edge_send, edge_recv, send_sem, recv_sem,
    ) = refs
    channels = feat.shape[1]
    pixels = tile_rows * width
    half = channels // 2
    part = channels // n_dp
    cot, hidden = (ref.at[pl.ds(width, pixels)] for ref in (cot_rows, hid_rows))
    dp = lax.axis_index("dp")
    sp = lax.axis_index("spatial")
    chip, core = sp // 2, sp % 2
    other_sp = sp + 1 - 2 * core

    y, z_high = dp // 4, dp % 4
    z_low, x = sp // 8, chip % 4
    z = 2 * z_high + z_low
    odd_x, odd_y, odd_z = x % 2, y % 2, z_low
    high_x, high_y = x // 2, y // 2
    quarter = 2 * odd_z + odd_x
    rank = high_x * 16 + high_y * 4 + z_high

    def block_of(high):
        return 2 * (high % 2) + high // 2

    def neighbour(side, d):
        dx, dy, dz = d % 2, (d // 2) % 2, d // 4
        x_there = (x + dx * (1 - 2 * odd_x) * (1 - 2 * side) + 4) % 4
        y_there = (y + dy * (1 - 2 * odd_y) * (1 - 2 * side) + 8) % 8
        z_there = (z + dz * (1 - 2 * odd_z) * (1 - 2 * side) + 8) % 8
        return (y_there * 4 + z_there // 2, (z_there % 2) * 8 + x_there * 2 + core)

    def gatherer(number):
        y_there, z_there = number // 4, number % 4
        return ((2 * y_there + odd_y) * 4 + z_there, z_low * 8 + (2 * (z_there % 2) + odd_x) * 2 + core)

    gathers = high_x == z_high % 2
    group = []
    for dz, dx, dc in (
        (1, 2, 0), (1, 2, 1), (1, 1, 0), (1, 1, 1), (1, 3, 0), (1, 3, 1), (0, 2, 0), (0, 2, 1),
        (1, 0, 0), (1, 0, 1), (0, 1, 0), (0, 1, 1), (0, 3, 0), (0, 3, 1), (0, 0, 1),
    ):
        group.append(lax.rem(z_low + dz, 2) * 8 + lax.rem(x + dx, 4) * 2 + lax.rem(core + dc, 2))
    high_steps = sorted(
        ((dy, dz) for dy in range(4) for dz in range(4)), key=lambda s: -min(s[0], 4 - s[0]) - min(s[1], 4 - s[1])
    )
    dp_steps = sorted(
        ((dy, dz) for dy in range(8) for dz in range(4)), key=lambda s: -min(s[0], 8 - s[0]) - 2 * min(s[1], 4 - s[1])
    )[:-1]

    owns_tail = jnp.logical_and(gathers, high_y == quarter)
    owner = dp // 2 == sp
    from_first = lax.rem(sp - dp // 2 + n_sp, n_sp)
    quarter_owner = from_first % 4 == 0
    (
        COARSE, FINE, BACK, TEXT, TEXT_DP, POOLED, MOD, GRAD_MOD, TILE, TAIL, FINAL,
        PAIR_COT, PAIR_HIDDEN, FAR, CUBE,
    ) = range(15)

    def load(source, target, index):
        return pltpu.make_async_copy(source, target, load_sem.at[index])

    own_lanes = pl.ds(pl.multiple_of(core * half, half), half)
    other_lanes = pl.ds(pl.multiple_of((1 - core) * half, half), half)
    own_pixels = pl.multiple_of(core * pixels, pixels)
    other_pixels = pl.multiple_of((1 - core) * pixels, pixels)
    own_rows = pl.ds(pl.multiple_of(width + core * pixels, width), pixels)
    loads = [
        load(ids_hbm, ids_ref, 1),
        load(table_hbm, table, 2),
        load(coarse_hbm, coarse, 0),
        load(cot_hbm, cot, 3),
    ]
    later = [
        load(feat_hbm, feat, 4),
        load(w_skip_hbm, w_skip, 5),
        load(w_mod_hbm, w_mod, 6),
        load(w_conv_hbm, w_conv, 7),
    ]
    for copy in (loads[2], loads[0], loads[1]):
        copy.start()

    barrier = pltpu.get_barrier_semaphore()

    def greet(place):
        pl.semaphore_signal(barrier, inc=1, device_id=place, device_id_type=MESH)

    @pl.when(owner)
    def _():
        for dy, dz in dp_steps:
            greet((lax.rem(y + dy, 8) * 4 + lax.rem(z_high + dz, 4), sp))

    for there in group:
        greet((dp, there))

    for copy in loads[3:] + later:
        copy.start()

    def remote(source, target, send, recv, place):
        return pltpu.make_async_remote_copy(
            src_ref=source, dst_ref=target, send_sem=send, recv_sem=recv, device_id=place, device_id_type=MESH
        )

    def wait_bytes(sem, ref):
        pltpu.make_async_copy(ref, ref, sem).wait()

    def to_spatial(box, index):
        for there in group:
            remote(box.at[sp], box.at[sp], send_sem.at[index], recv_sem.at[index], (dp, there)).start()

    def to_owners(source_of, box, index):
        for j in range(2):
            there = 2 * sp + j

            @pl.when(there != dp)
            def _():
                remote(source_of(j), box.at[dp], send_sem.at[index], recv_sem.at[index], (there, sp)).start()

    def sent_to_owners(box, index):
        @pl.when(owner)
        def _():
            wait_bytes(send_sem.at[index], box.at[pl.ds(0, 1)])

        @pl.when(jnp.logical_not(owner))
        def _():
            wait_bytes(send_sem.at[index], box.at[pl.ds(0, 2)])

    def from_owner(ref, index):
        for there in group:
            remote(ref, ref, send_sem.at[index], recv_sem.at[index], (dp, there)).start()

    def others(box):
        return box.at[pl.ds(0, box.shape[0] - 1)]

    def receive(box, index):
        wait_bytes(recv_sem.at[index], others(box))

    def total(box):
        return jnp.sum(box[...], axis=0)

    loads[2].wait()
    coarse_f = coarse[...].astype(F32)
    coarse_box[sp] = jnp.concatenate(
        as_rows(jnp.sum(coarse_f, axis=0, keepdims=True))
        + as_rows(jnp.sum(coarse_f * coarse_f, axis=0, keepdims=True)),
        axis=0,
    )

    pl.semaphore_wait(barrier, jnp.where(owner, n_sp, n_sp + 1))

    to_spatial(coarse_box, COARSE)

    vocab = table.shape[0]
    batch, tokens = ids_ref.shape
    loads[0].wait()
    local_ids = jnp.concatenate(
        [ids_ref[pl.ds(j, n_sp, stride=2), :] for j in range(2)], axis=0
    ) - (dp * n_sp + sp) * vocab
    turned_ids = local_ids.astype(F32).T
    quarters = jnp.concatenate([turned_ids] * 4, axis=1) - 16.0 * lax.shift_right_logical(
        iota((tokens, LANES), 1), 5
    ).astype(F32)
    found = [
        jnp.sum(jnp.where(quarters == float(k), 1.0, 0.0), axis=0, keepdims=True) for k in range(16)
    ]
    found = jnp.concatenate(found, axis=0)
    counts = jnp.concatenate([found[:, q * batch : (q + 1) * batch] for q in range(4)], axis=0)[:vocab].astype(BF16)
    loads[1].wait()
    partial = dot(counts, table[...], ((0,), (0,)))
    for i in range(8):
        for j in range(2):
            text_rows[:, 8 * j + i, :] = partial[j * n_sp : (j + 1) * n_sp, i * LANES : (i + 1) * LANES]
    text_out[...] = text_rows[...].astype(BF16)

    for there in group:
        remote(text_out.at[there], text_box.at[sp], send_sem.at[TEXT], recv_sem.at[TEXT], (dp, there)).start()

    text_box[sp] = text_out[sp]

    last = pixels - width

    def edges(rows, first):
        down = remote(
            rows.at[pl.ds(pixels, width)],
            rows.at[pl.ds(0, width)],
            edge_send.at[first],
            edge_recv.at[first],
            (dp, sp + 1),
        )
        upward = remote(
            rows.at[pl.ds(width, width)],
            rows.at[pl.ds(width + pixels, width)],
            edge_send.at[first + 1],
            edge_recv.at[first + 1],
            (dp, sp - 1),
        )
        return down, upward

    def start_edges(rows, first):
        down, upward = edges(rows, first)

        @pl.when(sp < n_sp - 1)
        def _():
            down.start()

        @pl.when(sp > 0)
        def _():
            upward.start()

    def receive_edges(rows, first):
        down, upward = edges(rows, first)

        @pl.when(sp > 0)
        def _():
            down.wait_recv()

        @pl.when(sp < n_sp - 1)
        def _():
            upward.wait_recv()

        @pl.when(sp == 0)
        def _():
            rows[0:width, :] = jnp.zeros((width, channels), BF16)

        @pl.when(sp == n_sp - 1)
        def _():
            rows[width + pixels :, :] = jnp.zeros((width, channels), BF16)

    def finish_edges(rows, first):
        down, upward = edges(rows, first)

        @pl.when(sp < n_sp - 1)
        def _():
            down.wait_send()

        @pl.when(sp > 0)
        def _():
            upward.wait_send()

    loads[3].wait()
    start_edges(cot_rows, 0)
    cot_half[...] = cot[:, other_lanes]
    cot_chip[own_rows, :] = cot[:, own_lanes]
    pair_cot = remote(
        cot_half, cot_chip.at[own_rows], send_sem.at[PAIR_COT], recv_sem.at[PAIR_COT], (dp, other_sp)
    )
    pair_cot.start()
    far = remote(
        cot_chip.at[pl.ds(pl.multiple_of(width + core * (pixels + last), width), width)],
        far_edge,
        send_sem.at[FAR],
        recv_sem.at[FAR],
        (dp, sp - 2 + 4 * core),
    )
    chips = n_sp // 2
    sends_far = jnp.logical_or(jnp.logical_and(core == 0, chip > 0), jnp.logical_and(core == 1, chip < chips - 1))
    takes_far = jnp.logical_or(jnp.logical_and(core == 0, chip < chips - 1), jnp.logical_and(core == 1, chip > 0))

    @pl.when(sends_far)
    def _():
        far.start()

    row, lane = iota((8, LANES), 0), iota((8, LANES), 1)
    half_width = 4 * LANES
    index = ((row & 3) * LANES + lane).astype(F32)
    angle = time_ref[0].astype(F32) * jnp.exp(-math.log(10000.0) * index / half_width)
    time_part[...] = jnp.where(row < 4, jnp.sin(angle), jnp.cos(angle))

    shape = chosen.shape
    coarse_cols = width // 4
    place = iota(shape, 0)
    wanted = lax.shift_right_logical(place, width.bit_length() - 1) * coarse_cols + (
        lax.shift_right_logical(place & (width - 1), 2)
    )
    chosen[...] = (wanted == iota(shape, 1)).astype(F32).astype(BF16)

    def turn_rows(first_row):
        @pl.loop(0, tile_rows, unroll=True)
        def _(r):
            start = pl.multiple_of(first_row + r * width, width)
            turned_shifts(cot_chip[pl.ds(start, width), :].astype(F32), cot_turned, start)

    receive(text_box, TEXT)
    text_sum[...] = jnp.sum(text_box[...].astype(F32), axis=0)
    to_owners(lambda j: text_sum.at[pl.ds(8 * j, 8)], text_dp_box, TEXT_DP)

    later[1].wait()
    receive(coarse_box, COARSE)
    coarse_total = group_total(total(coarse_box), coarse.shape[1] // GROUPS)
    coarse_count = coarse.shape[0] * n_sp * (coarse.shape[1] // GROUPS)
    tiles = coarse.shape[1] // LANES
    c_mean = coarse_total[0:tiles, :] / coarse_count
    c_scale = lax.rsqrt(coarse_total[tiles : 2 * tiles, :] / coarse_count - c_mean * c_mean + EPS)
    c_normed = (coarse[...].astype(F32) - as_row(c_mean, 0, tiles)) * as_row(c_scale, 0, tiles)
    coarse_act = (c_normed * sigmoid(c_normed)).astype(BF16)
    skip = dot(coarse_act, w_skip[...]).astype(BF16)
    up[...] = dot(chosen[...], skip)

    later[0].wait()

    def merge(r, sums):
        start = pl.multiple_of(r * width, width)
        up_start = pl.multiple_of((r // 4) * width, width)
        rows = (feat[pl.ds(start, width), :].astype(F32) + up[pl.ds(up_start, width), :]).astype(BF16)
        merged[pl.ds(start, width), :] = rows
        rows = rows.astype(F32)
        first, second = sums
        first = first + jnp.sum(rows.reshape(width // 8, 8, channels), axis=0)
        second = second + jnp.sum((rows * rows).reshape(width // 8, 8, channels), axis=0)
        return first, second

    zero = jnp.zeros((8, channels), F32)
    first, second = lax.fori_loop(0, tile_rows, merge, (zero, zero), unroll=True)

    def sums_tile(one, two):
        one = jnp.sum(one, axis=0, keepdims=True)
        two = jnp.sum(two, axis=0, keepdims=True)
        return jnp.concatenate(as_rows(one) + as_rows(two) + [jnp.zeros((4, LANES), F32)], axis=0)

    fine_box[sp] = sums_tile(first, second)
    to_spatial(fine_box, FINE)

    @pl.when(owner)
    def _():
        text_dp_box[dp] = text_sum[pl.ds(pl.multiple_of(8 * (dp % 2), 8), 8), :]
        receive(text_dp_box, TEXT_DP)
        pooled[...] = total(text_dp_box)
        from_owner(pooled, POOLED)

    turn_rows(width + own_pixels)
    wait_bytes(recv_sem.at[PAIR_COT], cot_chip.at[own_rows])
    turn_rows(width + other_pixels)
    receive_edges(cot_rows, 0)

    @pl.when(takes_far)
    def _():
        far.wait_recv()

    @pl.when(jnp.logical_not(takes_far))
    def _():
        far_edge[...] = jnp.zeros((width, half), BF16)

    near = cot_rows[pl.ds(pl.multiple_of(core * (width + pixels), width), width), own_lanes].astype(F32)
    farther = far_edge[...].astype(F32)
    turned_shifts(jnp.where(core == 0, near, farther), cot_turned, 0)
    turned_shifts(jnp.where(core == 0, farther, near), cot_turned, width + 2 * pixels)

    receive(fine_box, FINE)
    fine_total = group_total(total(fine_box), channels // GROUPS)
    fine_count = pixels * n_sp * (channels // GROUPS)
    f_mean = fine_total[0:2, :] / fine_count
    f_scale = lax.rsqrt(fine_total[2:4, :] / fine_count - f_mean * f_mean + EPS)
    center, scale = as_row(f_mean, 0, 2), as_row(f_scale, 0, 2)

    @pl.when(jnp.logical_not(owner))
    def _():
        wait_bytes(recv_sem.at[POOLED], pooled)

    embed = time_part[...] + pooled[...] / tokens
    embed = (embed * sigmoid(embed)).astype(BF16).astype(F32)
    later[2].wait()
    embed_row = jnp.broadcast_to(as_row(embed, 0, 8), (8, 8 * LANES)).astype(BF16)
    modulation = dot(embed_row, w_mod[...])[0:1, :]
    gain = 1.0 + modulation[:, :channels]
    shift = modulation[:, channels:]

    factor = scale * gain
    term_of_hidden = shift - center * factor

    @pl.loop(0, tile_rows, unroll=True)
    def _(r):
        start = pl.multiple_of(r * width, width)
        pre = merged[pl.ds(start, width), :].astype(F32) * factor + term_of_hidden
        act = pre * sigmoid(pre)
        hidden[pl.ds(start, width), :] = act.astype(BF16)
        low, high = act[:, :half], act[:, half:]
        block = lax.shift_right_logical(iota(low.shape, 1), 5)
        even = jnp.where((block & 1) == 0, low, pltpu.roll(high, 32, 1))
        odd = jnp.where((block & 1) == 0, pltpu.roll(low, LANES - 32, 1), high)
        rows = pl.ds(pl.multiple_of(own_pixels + start, width), width)
        hidden_pair[rows, :] = jnp.concatenate([even, odd], axis=1).astype(BF16)

        @pl.when(r % 2 == 1)
        def _():
            two = pl.ds(pl.multiple_of(own_pixels + start - width, width), 2 * width)
            remote(
                hidden_pair.at[two], hidden_pair.at[two], send_sem.at[PAIR_HIDDEN], recv_sem.at[PAIR_HIDDEN], (dp, other_sp)
            ).start()

    def weight_term(dr, first_pixel):
        lanes = pl.ds(pl.multiple_of((2 - dr) * width + first_pixel, width), pixels)
        return dot(cot_turned[:, lanes], hidden_pair[pl.ds(first_pixel, pixels), :])

    for dr in range(3):
        weight_own[dr] = weight_term(dr, own_pixels)
    wait_bytes(recv_sem.at[PAIR_HIDDEN], hidden_pair.at[pl.ds(0, pixels)])
    def send_shares(their_quarter):
        dx = odd_x + their_quarter % 2 - 2 * odd_x * (their_quarter % 2)
        dz = odd_z + their_quarter // 2 - 2 * odd_z * (their_quarter // 2)
        for dy in range(2):
            their_y = odd_y + dy - 2 * odd_y * dy
            d = dx + 2 * dy + 4 * dz

            @pl.when(d > 0)
            def _():
                for side in range(2):
                    remote(
                        cube_out.at[side, their_quarter, their_y],
                        cube_box.at[side, d],
                        send_sem.at[CUBE + side],
                        recv_sem.at[CUBE + side],
                        neighbour(side, d),
                    ).start()

    for dr in (2, 1, 0):
        grads = weight_own[dr] + weight_term(dr, other_pixels)
        for dc in (2, 1, 0):
            tap = 3 * dr + dc
            grad = grads[dc * half : (dc + 1) * half, :]
            if tap < 8:
                cube_out[tap % 2, tap // 2, 0, 0:half] = grad[:, :half].astype(BF16)
                cube_out[tap % 2, tap // 2, 1, 0:half] = grad[:, half:].astype(BF16)
            else:
                turned = grad.T.astype(BF16)
                for side in range(2):
                    for number in range(8):
                        first = (number % 2) * half + block_of(number // 2) * 32 + side * 16
                        cube_out[side, number // 2, number % 2, half : half + 16] = turned[first : first + 16, :]
        for their_quarter in ((0, 1), (2,), (3,))[dr]:
            send_shares(their_quarter)

    for side in range(2):
        cube_box[side, 0] = cube_out[side, quarter, odd_y]

    start_edges(hid_rows, 2)

    later[3].wait()
    chunk = pixels // 2

    @pl.loop(0, 2)
    def _(c):
        start = pl.multiple_of(c * chunk, chunk)
        terms = []
        for dc in range(3):
            term = None
            for dr in range(3):
                tap = 3 * dr + dc
                more = dot(
                    cot_rows[pl.ds(pl.multiple_of(start + (2 - dr) * width, width), chunk), :],
                    w_conv[:, tap * channels : (tap + 1) * channels],
                    ((1,), (1,)),
                )
                term = more if term is None else term + more
            terms.append(term)
        grad_hid[pl.ds(start, chunk), :] = from_neighbours(terms[2], terms[1], terms[0], width)

    def backward(r, sums):
        start = pl.multiple_of(r * width, width)
        normed = (merged[pl.ds(start, width), :].astype(F32) - center) * scale
        pre = normed * gain + shift
        sigma = sigmoid(pre)
        grad = grad_hid[pl.ds(start, width), :] * sigma * (1.0 + pre * (1.0 - sigma))
        grad_hid[pl.ds(start, width), :] = grad
        first, second = sums
        first = first + jnp.sum((grad * normed).reshape(width // 8, 8, channels), axis=0)
        second = second + jnp.sum(grad.reshape(width // 8, 8, channels), axis=0)
        return first, second

    first, second = lax.fori_loop(0, tile_rows, backward, (zero, zero), unroll=True)
    back_box[sp] = sums_tile(first, second)
    to_spatial(back_box, BACK)

    sides = []
    for side in range(2):
        wait_bytes(recv_sem.at[CUBE + side], cube_box.at[side, pl.ds(1, 7)])
        summed = cube_box[side, 0].astype(F32)
        for d in range(1, 8):
            summed = summed + cube_box[side, d].astype(F32)
        sides.append(summed[0:half, :].T.reshape(16, part, half))
        tail_sum[side * 16 : (side + 1) * 16, :] = summed[half : half + 16, :]
    weight_out[...] = jnp.concatenate(sides, axis=1).astype(BF16)

    def part_of(number):
        return weight_out.at[block_of(number // 4) * 4 + number % 4]

    for dy, dz in high_steps:
        number = lax.rem(high_y + dy, 4) * 4 + lax.rem(z_high + dz, 4)
        copy = remote(
            part_of(number), tile_box.at[rank], send_sem.at[TILE], recv_sem.at[TILE], gatherer(number)
        )
        if dy + dz > 0:
            copy.start()
        else:
            pl.when(jnp.logical_not(gathers))(copy.start)

    for m in range(4):
        itself = jnp.logical_and(owns_tail, z_high == m)

        @pl.when(jnp.logical_not(itself))
        def _():
            remote(
                tail_sum.at[pl.ds(m * part, part)],
                tail_box.at[rank],
                send_sem.at[TAIL],
                recv_sem.at[TAIL],
                gatherer(quarter * 4 + m),
            ).start()

        @pl.when(itself)
        def _():
            tail_box[rank] = tail_sum[m * part : (m + 1) * part, :]

    @pl.when(gathers)
    def _():
        tile_box[rank] = part_of(high_y * 4 + z_high)[...]

    receive(back_box, BACK)
    back = total(back_box)
    for i in range(4):
        pair_there = lax.rem(sp - 4 * i + n_sp, n_sp)
        wanted_row = jnp.sum(jnp.where(row == pair_there // 2, embed, 0.0), axis=0, keepdims=True)
        mod_out[i] = jnp.concatenate([back[i : i + 1, :], wanted_row, jnp.zeros((6, LANES), F32)], axis=0)
        for j in range(2):
            there = 2 * pair_there + j

            @pl.when(there != dp)
            def _():
                remote(mod_out.at[i], mod_box.at[dp], send_sem.at[MOD], recv_sem.at[MOD], (there, sp)).start()

            @pl.when(there == dp)
            def _():
                mod_box[dp] = mod_out[i]

    receive_edges(hid_rows, 2)

    @pl.loop(0, 2)
    def _(c):
        start = pl.multiple_of(c * chunk, chunk)
        terms = []
        for dc in range(3):
            term = merged[pl.ds(start, chunk), :].astype(F32) if dc == 1 else None
            for dr in range(3):
                tap = 3 * dr + dc
                more = dot(
                    hid_rows[pl.ds(pl.multiple_of(start + dr * width, width), chunk), :],
                    w_conv[:, tap * channels : (tap + 1) * channels],
                )
                term = more if term is None else term + more
            terms.append(term)
        out_ref[pl.ds(start, chunk), :] = from_neighbours(terms[0], terms[1], terms[2], width).astype(BF16)

    stores = [
        pltpu.make_async_copy(source, target, store_sem.at[i])
        for i, (source, target) in enumerate(
            (
                (out_ref, out_hbm), (grad_feat_ref, grad_feat_hbm),
            )
        )
    ]
    stores[0].start()

    gain_tile = jnp.concatenate(as_rows(gain) + as_rows(gain), axis=0)
    means = group_total(back[0:4, :] * gain_tile, channels // GROUPS) / fine_count
    mean_two, mean_one = as_row(means, 0, 2), as_row(means, 2, 2)

    final_slot = 2 * quarter + core

    def to_group(rows):
        for there in group:
            remote(
                final_own.at[rows],
                final_hbm.at[final_slot, rows],
                send_sem.at[FINAL],
                recv_sem.at[FINAL],
                (dp, there),
            ).start()

    def own_final(rows):
        return pltpu.make_async_copy(final_own.at[rows], final_hbm.at[final_slot, rows], store_sem.at[2])

    main, both = pl.ds(0, 16), pl.ds(0, 32)
    no_tail = jnp.logical_and(gathers, jnp.logical_not(owns_tail))

    @pl.when(gathers)
    def _():
        receive(tile_box, TILE)
        final_own[0:16, :] = jnp.sum(tile_box[...].astype(F32), axis=0).astype(BF16)

    @pl.when(no_tail)
    def _():
        to_group(main)
        own_final(main).start()

    @pl.when(owns_tail)
    def _():
        receive(tail_box, TAIL)
        final_own[16:32, :] = jnp.concatenate([total(tail_box), jnp.zeros((part, half), F32)], axis=0).astype(BF16)
        to_group(both)
        own_final(both).start()

    @pl.loop(0, tile_rows, unroll=True)
    def _(r):
        start = pl.multiple_of(r * width, width)
        normed = (merged[pl.ds(start, width), :].astype(F32) - center) * scale
        inner = grad_hid[pl.ds(start, width), :] * gain - mean_one - normed * mean_two
        grad_feat_ref[pl.ds(start, width), :] = (cot[pl.ds(start, width), :].astype(F32) + scale * inner).astype(BF16)

    stores[1].start()

    @pl.when(quarter_owner)
    def _():
        receive(mod_box, MOD)
        share = 8 * LANES // n_dp
        in_lanes = LANES // share
        embeds = mod_box[:, 1, :].astype(BF16)
        rest = mod_box[:, 0, :]
        grads = None
        for _ in range(3):
            piece = rest.astype(BF16)
            rest = rest - piece.astype(F32)
            term = dot(embeds, piece, ((0,), (0,)))
            grads = term if grads is None else grads + term
        mod_rows[...] = grads
        mod_start = pl.multiple_of((dp % in_lanes) * share, share)
        number = from_first // 4
        mod_own[...] = mod_rows[pl.ds(mod_start, share), :].astype(BF16)

        for there in group:
            remote(mod_own, mod_hbm.at[number], send_sem.at[GRAD_MOD], recv_sem.at[GRAD_MOD], (dp, there)).start()

        pltpu.make_async_copy(mod_own, mod_hbm.at[number], store_sem.at[3]).start()

    def units(count):
        return tile_box.at[pl.ds(0, count)]

    @pl.when(jnp.logical_not(gathers))
    def _():
        wait_bytes(recv_sem.at[FINAL], units(10))

    @pl.when(no_tail)
    def _():
        wait_bytes(recv_sem.at[FINAL], units(9))
        wait_bytes(send_sem.at[FINAL], units(n_sp - 1))
        wait_bytes(send_sem.at[TILE], units(15))
        own_final(main).wait()

    @pl.when(owns_tail)
    def _():
        wait_bytes(recv_sem.at[FINAL], units(8))
        wait_bytes(send_sem.at[FINAL], units(2 * (n_sp - 1)))
        wait_bytes(send_sem.at[TILE], units(15))
        own_final(both).wait()

    @pl.when(jnp.logical_not(gathers))
    def _():
        wait_bytes(send_sem.at[TILE], units(16))

    @pl.when(quarter_owner)
    def _():
        wait_bytes(recv_sem.at[GRAD_MOD], mod_hbm.at[pl.ds(0, 3)])
        pltpu.make_async_copy(mod_own, mod_hbm.at[from_first // 4], store_sem.at[3]).wait()

    @pl.when(jnp.logical_not(quarter_owner))
    def _():
        wait_bytes(recv_sem.at[GRAD_MOD], mod_hbm)

    for box, index in (
        (fine_box, FINE), (back_box, BACK), (text_box, TEXT), (coarse_box, COARSE),
    ):
        wait_bytes(send_sem.at[index], others(box))

    for side in range(2):
        wait_bytes(send_sem.at[CUBE + side], cube_box.at[side, pl.ds(1, 7)])
    sent_to_owners(text_dp_box, TEXT_DP)

    @pl.when(quarter_owner)
    def _():
        wait_bytes(send_sem.at[MOD], mod_box.at[pl.ds(0, 7)])
        wait_bytes(send_sem.at[GRAD_MOD], units(2 * (n_sp - 1)))

    @pl.when(jnp.logical_not(quarter_owner))
    def _():
        wait_bytes(send_sem.at[MOD], mod_box.at[pl.ds(0, 8)])

    @pl.when(owner)
    def _():
        wait_bytes(send_sem.at[POOLED], fine_box.at[pl.ds(0, n_sp - 1)])

    pair_cot.wait_send()
    wait_bytes(send_sem.at[PAIR_HIDDEN], hidden_pair.at[pl.ds(0, pixels)])

    @pl.when(sends_far)
    def _():
        far.wait_send()

    finish_edges(cot_rows, 0)
    finish_edges(hid_rows, 2)

    @pl.when(owns_tail)
    def _():
        wait_bytes(send_sem.at[TAIL], tail_box.at[pl.ds(0, 3)])

    @pl.when(jnp.logical_not(owns_tail))
    def _():
        wait_bytes(send_sem.at[TAIL], tail_box.at[pl.ds(0, 4)])

    for store in stores:
        store.wait()


def write(
    out, grad_feat, final, mod, out_hbm, grad_feat_hbm, grad_conv_hbm, grad_mod_hbm,
    out_room, grad_feat_room, final_room, mod_room, grad_conv, grad_mod, load_sem, store_sem,
):
    fetch_final = pltpu.make_async_copy(final, final_room, load_sem.at[4])
    fetch_mod = pltpu.make_async_copy(mod, mod_room, load_sem.at[5])
    fetch_final.start()
    fetch_mod.start()
    moves = []
    for source, room, target in ((out, out_room, out_hbm), (grad_feat, grad_feat_room, grad_feat_hbm)):
        rows = source.shape[0] // 2
        for i in range(2):
            piece = pl.ds(i * rows, rows)
            number = len(moves)
            moves.append(
                (
                    pltpu.make_async_copy(source.at[piece], room.at[piece], load_sem.at[number]),
                    pltpu.make_async_copy(room.at[piece], target.at[piece], store_sem.at[number]),
                )
            )
    for fetch, _ in moves:
        fetch.start()
    fetch_final.wait()
    parts = final_room[...].astype(F32)
    tail_quarter = lax.axis_index("dp") // 8
    columns = [
        parts[2 * (tap // 2) + side, 8 * (tap % 2) : 8 * (tap % 2) + 8, :] for tap in range(8) for side in range(2)
    ] + [final_room[2 * tail_quarter + side].astype(F32)[16:24, :] for side in range(2)]
    grad_conv[...] = jnp.concatenate(columns, axis=1).astype(BF16)
    fetch_mod.wait()
    grad_mod[...] = jnp.concatenate([mod_room[i] for i in range(4)], axis=1)
    last = [
        pltpu.make_async_copy(grad_conv, grad_conv_hbm, store_sem.at[4]),
        pltpu.make_async_copy(grad_mod, grad_mod_hbm, store_sem.at[5]),
    ]
    for store in last:
        store.start()
    for fetch, store in moves:
        fetch.wait()
        store.start()
    for _, store in moves:
        store.wait()
    for store in last:
        store.wait()


def body(n_dp, n_sp, features, coarse, timestep, text_ids, text_table, w_mod, w_skip, w_conv, cotangent):
    _, tile_rows, width, channels = features.shape
    pixels = tile_rows * width
    cells = coarse.shape[1] * coarse.shape[2]
    coarse_width = coarse.shape[3]
    part, half = channels // n_dp, channels // 2
    taps = w_conv.shape[1] // channels
    vm = pltpu.VMEM
    tile = (8, LANES)
    anywhere = pl.BlockSpec(memory_space=pl.ANY)
    mod_rows = w_mod.shape[0] // n_dp
    scratch = [
        vm((pixels, channels), BF16),
        vm((pixels, channels), BF16),
        vm(text_ids.shape, jnp.int32),
        vm((pixels, channels), BF16),
        vm((cells, coarse_width), BF16),
        vm(text_table.shape, BF16),
        vm(w_mod.shape, BF16),
        vm(w_skip.shape, BF16),
        vm(w_conv.shape, BF16),
        vm((pixels + 2 * width, channels), BF16),
        vm((width, half), BF16),
        vm((pixels, half), BF16),
        vm((2 * pixels + 2 * width, half), BF16),
        vm((3 * half, 2 * pixels + 2 * width), BF16),
        vm((4 * cells, cells), BF16),
        vm((4 * cells, channels), F32),
        vm((pixels, channels), BF16),
        vm((pixels + 2 * width, channels), BF16),
        vm((2 * pixels, channels), BF16),
        vm((pixels, channels), F32),
        vm((n_sp,) + tile, F32),
        vm((n_sp,) + tile, F32),
        vm((n_sp,) + tile, F32),
        vm((n_sp, 16, LANES), F32),
        vm((n_sp, 16, LANES), BF16),
        vm((n_sp, 16, LANES), BF16),
        vm((16, LANES), F32),
        vm((n_dp,) + tile, F32),
        vm(tile, F32),
        vm(tile, F32),
        vm((4,) + tile, F32),
        vm((n_dp,) + tile, F32),
        vm((LANES, LANES), F32),
        vm((mod_rows, LANES), BF16),
        vm((3, 3 * half, channels), F32),
        vm((2, 4, 2, half + 16, half), BF16),
        vm((2, 8, half + 16, half), BF16),
        vm((16, 2 * part, half), BF16),
        vm((32, half), F32),
        vm((n_dp, 2 * part, half), BF16),
        vm((n_dp, part, half), F32),
        vm((32, half), BF16),
        pltpu.SemaphoreType.DMA((8,)),
        pltpu.SemaphoreType.DMA((4,)),
        pltpu.SemaphoreType.DMA((4,)),
        pltpu.SemaphoreType.DMA((4,)),
        pltpu.SemaphoreType.DMA((16,)),
        pltpu.SemaphoreType.DMA((16,)),
    ]
    shapes = (
        jax.ShapeDtypeStruct((pixels, channels), BF16),
        jax.ShapeDtypeStruct((pixels, channels), BF16),
        jax.ShapeDtypeStruct((8, 32, half), BF16),
        jax.ShapeDtypeStruct((4, mod_rows, LANES), BF16),
    )
    written = shapes[:2] + (
        jax.ShapeDtypeStruct((part, taps * channels), BF16),
        jax.ShapeDtypeStruct((mod_rows, 2 * channels), BF16),
    )
    results = pl.pallas_call(
        functools.partial(kernel, n_dp, n_sp, tile_rows, width),
        out_shape=shapes,
        in_specs=[pl.BlockSpec(memory_space=pltpu.SMEM)] + [anywhere] * 8,
        out_specs=(anywhere,) * 4,
        scratch_shapes=scratch,
        compiler_params=pltpu.CompilerParams(
            collective_id=0, has_side_effects=True, vmem_limit_bytes=VMEM_LIMIT
        ),
    )(
        timestep,
        text_ids,
        features.reshape(pixels, channels),
        coarse.reshape(cells, coarse_width),
        text_table,
        w_mod,
        w_skip,
        w_conv,
        cotangent.reshape(pixels, channels),
    )
    output, grad_features, grad_conv, grad_mod = pl.pallas_call(
        write,
        out_shape=written,
        in_specs=[anywhere] * 4,
        out_specs=(anywhere,) * 4,
        scratch_shapes=[vm(shape.shape, shape.dtype) for shape in shapes + written[2:]]
        + [pltpu.SemaphoreType.DMA((6,)), pltpu.SemaphoreType.DMA((6,))],
        compiler_params=pltpu.CompilerParams(vmem_limit_bytes=VMEM_LIMIT),
    )(*results)
    return output.reshape(features.shape), grad_features.reshape(features.shape), grad_conv, grad_mod


def solution(mesh):
    in_specs = (
        P("dp", "spatial", None, None),
        P("dp", "spatial", None, None),
        P("dp"),
        P(),
        P(("dp", "spatial"), None),
        P(),
        P(),
        P(),
        P("dp", "spatial", None, None),
    )
    out_specs = (
        P("dp", "spatial", None, None),
        P("dp", "spatial", None, None),
        P("dp", None),
        P("dp", None),
    )
    step = functools.partial(body, mesh.shape["dp"], mesh.shape["spatial"])
    return jax.shard_map(step, mesh=mesh, in_specs=in_specs, out_specs=out_specs, check_vma=False)
```
